128 devices in a mesh: gx: 8 (over y, x_lo), gy: 16 (over x_hi, z, core).
Axes of the slice: x: 4 (x_hi: 2, x_lo: 2; x = x_hi * 2 + x_lo), y: 4, z: 4, core: 2. Of those that a mesh axis runs over, the one named last changes fastest.
Arguments:
- inputs: bfloat16 [24, 197, 1024], P('gx', None, 'gy'), may hold values from -28 to 28
- cotangent: bfloat16 [24, 197, 1024], P('gx', None, 'gy'), may hold values from -6 to 6
- group_images: int32 [8], replicated, may hold values from 1 to 3, 16 in all
- ln1_gain: float32 [2, 1024], P(None, 'gy'), may hold values from 0.25 to 1.75
- ln1_bias: float32 [2, 1024], P(None, 'gy'), may hold values from -4 to 4
- w_qkv: bfloat16 [2, 1024, 16, 192], P(None, 'gx', 'gy'), may hold values from -0.1875 to 0.1875
- b_qv: float32 [2, 16, 128], P(None, 'gy'), may hold values from -4 to 4
- w_out: bfloat16 [2, 1024, 1024], P(None, 'gy', 'gx'), may hold values from -1.5 to 1.5
- b_out: float32 [2, 1024], P(None, 'gy'), may hold values from -4 to 4
- ln2_gain: float32 [2, 1024], P(None, 'gy'), may hold values from 0.25 to 1.75
- ln2_bias: float32 [2, 1024], P(None, 'gy'), may hold values from -4 to 4
- w_up: bfloat16 [2, 1024, 4096], P(None, 'gx', 'gy'), may hold values from -0.1875 to 0.1875
- b_up: float32 [2, 4096], P(None, 'gy'), may hold values from -4 to 4
- w_down: bfloat16 [2, 4096, 1024], P(None, 'gy', 'gx'), may hold values from -0.09375 to 0.09375
- b_down: float32 [2, 1024], P(None, 'gy'), may hold values from -4 to 4
Outputs:
- out: float32 [24, 197, 1024], P('gx', None, 'gy')
- grad_inputs: float32 [24, 197, 1024], P('gx', None, 'gy')
- grad_ln1_gain: float32 [2, 1024], P(None, 'gy')
- grad_ln1_bias: float32 [2, 1024], P(None, 'gy')
- grad_w_qkv: float32 [2, 1024, 16, 192], P(None, 'gx', 'gy')
- grad_b_qv: float32 [2, 16, 128], P(None, 'gy')
- grad_w_out: float32 [2, 1024, 1024], P(None, 'gy', 'gx')
- grad_b_out: float32 [2, 1024], P(None, 'gy')
- grad_ln2_gain: float32 [2, 1024], P(None, 'gy')
- grad_ln2_bias: float32 [2, 1024], P(None, 'gy')
- grad_w_up: float32 [2, 1024, 4096], P(None, 'gx', 'gy')
- grad_b_up: float32 [2, 4096], P(None, 'gy')
- grad_w_down: float32 [2, 4096, 1024], P(None, 'gy', 'gx')
- grad_b_down: float32 [2, 1024], P(None, 'gy')
The draws below stay inside these ranges and needn't reach their ends.
Inputs may be any that keep to these rules, and one draw needn't show every extreme that they name: x-group g holds live images in its first group_images[g] of its 3 slots; the rest are padding; some group is full.
All inputs are finite; a program needn't handle non-finite values.
Results may differ from the reference program's by a relative error of at most 0.023.
Values may be sent and summed in bfloat16 or wider, within the bound.
No kernel may reach another device: no remote copies, remote signals or barrier semaphores. Data moves between devices by JAX's collectives and lax.ppermute only.
A program may use at most 64 MiB of HBM per device.

```python
import math
import jax
import jax.numpy as jnp
import numpy as np
from jax import lax

D = 1024
FF = 4096
H = 16
HD = 64
SEQ = 197
LAYERS = 2
IMG_GRP = 2
CAP = 3
SLOTS = 24
N_GX = 8


def draw_inputs(key, part):
    key = jax.random.fold_in(key, 11)
    key_base, key_jitter, key_shift = jax.random.split(key, 3)
    feature_ramp = 3.0 ** (jnp.arange(D, dtype=jnp.float32) / (D - 1))
    jitter = jax.random.uniform(key_jitter, (D,), jnp.float32, 0.7, 1.3)
    base_draw = jnp.clip(jax.random.normal(key_base, (SLOTS, SEQ, D), jnp.float32), -6.0, 6.0)
    offset_term = 0.5 * jnp.clip(jax.random.normal(key_shift, (SLOTS, SEQ, 1), jnp.float32), -3.0, 3.0)
    return (base_draw * feature_ramp * jitter + offset_term).astype(jnp.bfloat16)


def block_levels(key, extent, cuts, low, top_value):
    def one(position, blocks):
        heights = jax.random.uniform(jax.random.fold_in(jax.random.fold_in(key, 6), position), (blocks,), jnp.float32, low / len(cuts), top_value / len(cuts))
        return jnp.repeat(jnp.exp(heights), extent[position] // blocks).reshape((-1,) + (1,) * (len(extent) - position - 1))

    level = one(*cuts[0])
    for cut in cuts[1:]:
        level = level * one(*cut)
    return level


def length_profile(number_of, total, reach, lean):
    portions = [(1 << 20) // math.isqrt(standing ** lean) + 1 for standing in range(2, number_of + 1)]
    rest, holding = total - reach - (number_of - 1), [1] * (number_of - 1)
    while rest > 0:
        movable = [i for i in range(number_of - 1) if holding[i] < reach]
        whole, remaining = sum([portions[i] for i in movable]), rest
        for i in movable:
            extra = min(reach - holding[i], max(1, remaining * portions[i] // whole), rest)
            holding[i] = holding[i] + extra
            rest = rest - extra
    return np.array([reach] + holding)


def uneven_parts(key, count, total, reach, slope):
    if count == 2:
        one = jax.random.randint(key, (), max(1, total - reach), min(reach, total - 1) + 1)
        return jnp.stack([one, total - one])
    sizes = jnp.asarray(length_profile(count, total, reach, slope), jnp.int32)
    twos = (count - 1) // 2
    giver, receiver = sizes[1:1 + 2 * twos:2], sizes[2:2 + 2 * twos:2]
    slack = jnp.minimum(giver - 1, reach - receiver)
    passed = jax.random.randint(jax.random.fold_in(key, 1), (twos,), 0, 1 << 20) % (slack + 1)
    sizes = sizes.at[1:1 + 2 * twos:2].set(giver - passed).at[2:2 + 2 * twos:2].set(receiver + passed)
    return sizes[jax.random.permutation(jax.random.fold_in(key, 2), count)]


def noise(rng, extent, width, limit, cuts=(), held_as=jnp.bfloat16):
    factor_of = block_levels(rng, extent, cuts, -0.22, 0.18) if cuts else 1.0
    entries = jax.random.normal(rng, extent, jnp.float32) * width * factor_of
    return jnp.minimum(jnp.maximum(entries, -limit), limit).astype(held_as)


def setup_inputs(seed: int = 0) -> dict:
    arg_keys = jax.random.split(jax.random.key(seed), 16)
    inputs = draw_inputs(jax.random.fold_in(arg_keys[15], 71), 0)
    cotangent = noise(arg_keys[1], (SLOTS, SEQ, D), 1.0, 6.0, ((0, 8), (2, 16)))
    group_images = uneven_parts(arg_keys[2], N_GX, IMG_GRP * N_GX, CAP, 2).astype(jnp.int32)
    ln1_gain = jnp.clip(1.0 + 0.15 * jax.random.normal(arg_keys[3], (LAYERS, D), jnp.float32), 0.25, 1.75)
    ln1_bias = noise(arg_keys[4], (LAYERS, D), 0.3, 4.0, ((1, 16),), jnp.float32)
    w_qkv = noise(arg_keys[5], (LAYERS, D, H, 3 * HD), D ** -0.5, 0.1875, ((1, 8), (2, 16)))
    b_qv = noise(arg_keys[6], (LAYERS, H, 2 * HD), 0.5, 4.0, ((1, 16),), jnp.float32)
    w_out = noise(arg_keys[7], (LAYERS, D, D), (D // 64) ** -0.5, 1.5, ((1, 16), (2, 8)))
    b_out = noise(arg_keys[8], (LAYERS, D), 0.3, 4.0, ((1, 16),), jnp.float32)
    ln2_gain = jnp.clip(1.0 + 0.15 * jax.random.normal(arg_keys[9], (LAYERS, D), jnp.float32), 0.25, 1.75)
    ln2_bias = noise(arg_keys[10], (LAYERS, D), 0.3, 4.0, ((1, 16),), jnp.float32)
    w_up = noise(arg_keys[11], (LAYERS, D, FF), D ** -0.5, 0.1875, ((1, 8), (2, 16)))
    b_up = noise(arg_keys[12], (LAYERS, FF), 0.5, 4.0, ((1, 16),), jnp.float32)
    w_down = noise(arg_keys[13], (LAYERS, FF, D), FF ** -0.5, 0.09375, ((1, 16), (2, 8)))
    b_down = noise(arg_keys[14], (LAYERS, D), 0.3, 4.0, ((1, 16),), jnp.float32)
    return {"inputs": inputs, "cotangent": cotangent, "group_images": group_images, "ln1_gain": ln1_gain, "ln1_bias": ln1_bias, "w_qkv": w_qkv, "b_qv": b_qv, "w_out": w_out, "b_out": b_out, "ln2_gain": ln2_gain, "ln2_bias": ln2_bias, "w_up": w_up, "b_up": b_up, "w_down": w_down, "b_down": b_down}


@jax.custom_vjp
def low(v):
    return lax.optimization_barrier(v.astype(jnp.bfloat16)).astype(jnp.float32)

@jax.custom_vjp
def low_back(v):
    return v

def low_keep(v):
    return (low(v), None)

def low_pass(kept, grad):
    return (grad,)

def back_keep(v):
    return (v, None)

def back_low(kept, grad):
    return (low(grad),)
low.defvjp(low_keep, low_pass)
low_back.defvjp(back_keep, back_low)
epsilon = 1e-06
highest = lax.Precision.HIGHEST

def norm_rows(source, gain_vec, bias_vec):
    center = source - lax.optimization_barrier(jnp.mean(source, axis=-1, keepdims=True))
    spread = lax.optimization_barrier(jnp.mean(center * center, axis=-1, keepdims=True))
    return center * lax.rsqrt(spread + epsilon) * gain_vec + bias_vec

def attend(group_block):
    query_part, key_part, value_part = group_block
    scores = jnp.einsum('cshd,cthd->chst', query_part, key_part, precision=highest) * HD ** (-0.5)
    scores = low_back(scores)
    attention = low(jax.nn.softmax(scores, axis=-1))
    return jnp.einsum('chst,cthd->cshd', attention, value_part, precision=highest)

def encoder_layer(stream, params):
    gain_one, bias_one, w_qkv, bias_qv, w_out, bias_out, gain_two, bias_two, w_up, bias_up, w_down, bias_down = params
    normed = low(norm_rows(stream, gain_one, bias_one))
    packed = jnp.einsum('csd,dhk->cshk', normed, w_qkv, precision=highest)
    query_part = low_back(low(packed[..., :HD] + bias_qv[:, :HD]))
    key_part = low_back(low(packed[..., HD:2 * HD]))
    value_part = low_back(low(packed[..., 2 * HD:] + bias_qv[:, HD:]))
    grouped = tuple((tensor.reshape(N_GX, CAP, SEQ, H, HD) for tensor in (query_part, key_part, value_part)))
    attended = lax.map(jax.checkpoint(attend), grouped).reshape(SLOTS, SEQ, D)
    head_rows = low_back(low(attended))
    mixed_out = low_back(jnp.einsum('csk,kd->csd', head_rows, w_out, precision=highest) + bias_out)
    middle = stream + mixed_out
    normed_two = low(norm_rows(middle, gain_two, bias_two))
    upper_pre = low_back(jnp.einsum('csd,df->csf', normed_two, w_up, precision=highest) + bias_up)
    active = low(jax.nn.gelu(upper_pre, approximate=False))
    down_out = low_back(jnp.einsum('csf,fd->csd', active, w_down, precision=highest) + bias_down)
    return middle + down_out

def reference(inputs, cotangent, group_images, ln1_gain, ln1_bias, w_qkv, b_qv, w_out, b_out, ln2_gain, ln2_bias, w_up, b_up, w_down, b_down):
    live_rows = (jnp.arange(SLOTS) % CAP < jnp.repeat(group_images, CAP)).astype(jnp.float32)[:, None, None]
    params = tuple((member.astype(jnp.float32) for member in (ln1_gain, ln1_bias, w_qkv, b_qv, w_out, b_out, ln2_gain, ln2_bias, w_up, b_up, w_down, b_down)))

    def forward(stream, params):
        for depth_index in range(LAYERS):
            stream = encoder_layer(stream, tuple((param[depth_index] for param in params)))
        return stream * live_rows
    result, pullback = jax.vjp(forward, inputs.astype(jnp.float32), params)
    grad_stream, grads = pullback(cotangent.astype(jnp.float32))
    return (result, grad_stream, grads[0], grads[1], grads[2], grads[3], grads[4], grads[5], grads[6], grads[7], grads[8], grads[9], grads[10], grads[11])
```

```python
import jax
import jax.numpy as jnp
from jax import lax
from jax.sharding import Mesh, PartitionSpec as P

EPS = 1e-06
BF = jnp.bfloat16
F32 = jnp.float32
DP = ("y", "xl", "xh")
SWAP = [(0, 1), (1, 0)]
PAIR_A = [(0, 1), (1, 0), (2, 3), (3, 2)]
PAIR_B = [(0, 3), (3, 0), (1, 2), (2, 1)]


def dot(a, b, ca, cb):
    return lax.dot_general(a, b, (((ca,), (cb,)), ((), ())), preferred_element_type=F32)


def bdot(a, b, ca, cb):
    return lax.dot_general(
        a, b, (((ca,), (cb,)), ((0,), (0,))), preferred_element_type=F32
    )


def split_two(vec):
    high = lax.reduce_precision(vec, 8, 7)
    return high.astype(BF), (vec - high).astype(BF)


def core_swap(block):
    return lax.ppermute(block, "c", SWAP)


def core_join(half):
    other = core_swap(half)
    first = lax.axis_index("c") == 0
    return jnp.concatenate(
        [jnp.where(first, half, other), jnp.where(first, other, half)], axis=0
    )


def ring_gather(block):
    here = lax.axis_index("z")
    held = jnp.zeros((4,) + block.shape, block.dtype)
    held = lax.dynamic_update_index_in_dim(held, block, here, 0)
    for step in (1, 3, 2):
        got = lax.ppermute(block, "z", [(i, (i + step) % 4) for i in range(4)])
        held = lax.dynamic_update_index_in_dim(held, got, (here - step) % 4, 0)
    return held


def total(partial):
    half = partial.shape[0] // 2
    core = lax.axis_index("c")
    mine = lax.dynamic_slice_in_dim(partial, core * half, half, 0)
    theirs = lax.dynamic_slice_in_dim(partial, (1 - core) * half, half, 0).astype(BF)
    mine = mine + core_swap(theirs).astype(F32)
    cut = mine.shape[1] // 2
    left, right = mine[:, :cut].astype(BF), mine[:, cut:].astype(BF)
    got_left = lax.ppermute(left, "z", PAIR_A)
    got_right = lax.ppermute(right, "z", PAIR_B)
    left = (left.astype(F32) + got_left.astype(F32)).astype(BF)
    right = (right.astype(F32) + got_right.astype(F32)).astype(BF)
    got_left = lax.ppermute(left, "z", PAIR_B)
    got_right = lax.ppermute(right, "z", PAIR_A)
    return jnp.concatenate(
        [
            left.astype(F32) + got_left.astype(F32),
            right.astype(F32) + got_right.astype(F32),
        ],
        axis=1,
    )


def normalize(stream):
    center = stream - jnp.mean(stream, axis=-1, keepdims=True)
    factor = lax.rsqrt(jnp.mean(center * center, axis=-1, keepdims=True) + EPS)
    return center * factor, factor


def norm_backward(upstream, normed, factor, gain):
    scaled = upstream * gain
    first = jnp.mean(scaled, axis=-1, keepdims=True)
    second = jnp.mean(scaled * normed, axis=-1, keepdims=True)
    return factor * (scaled - first - normed * second)


def gelu_pair(u):
    phi = 0.5 * lax.erfc(u * (-(0.5**0.5)))
    density = jnp.exp(-0.5 * u * u) * 0.3989422804014327
    return u * phi, phi + u * density


def exchange(chunks):
    return lax.all_to_all(chunks, DP, 0, 0)


def share(rows):
    return exchange(jnp.broadcast_to(rows[None], (16,) + rows.shape))


def halves_on_lanes(v):
    cut = v.shape[-2] // 2
    return jnp.concatenate([v[..., :cut, :], v[..., cut:, :]], axis=-1)


def halves_on_rows(v):
    cut = v.shape[-1] // 2
    return jnp.concatenate([v[..., :cut], v[..., cut:]], axis=-2)


def shards(
    inputs,
    cotangent,
    group_images,
    ln1_gain,
    ln1_bias,
    w_qkv,
    b_qv,
    w_out,
    b_out,
    ln2_gain,
    ln2_bias,
    w_up,
    b_up,
    w_down,
    b_down,
):
    seq = inputs.shape[1]
    half = 104
    rows = 2 * half
    core = lax.axis_index("c")
    ring = lax.axis_index("z")
    group = lax.axis_index(("y", "xl"))
    worker = lax.axis_index(DP)
    first_core = core == 0

    offsets = jnp.cumsum(group_images) - group_images
    my_offset = offsets[group]
    my_live = group_images[group]
    source = jnp.sum((offsets <= worker).astype(jnp.int32)) - 1

    both = jnp.concatenate([inputs, cotangent], axis=-1)
    both = jnp.pad(both, ((0, 0), (0, rows - seq), (0, 0)))
    slot = (jnp.arange(16) - my_offset)[:, None, None]
    images = jnp.where(slot <= 0, both[0], jnp.where(slot == 1, both[1], both[2]))
    wide = jnp.stack([ln1_gain, ln1_bias, b_out, ln2_gain, ln2_bias, b_down])
    wide = jnp.concatenate([wide[:, 0], wide[:, 1]], axis=-1)
    narrow = jnp.concatenate([b_qv[:, 0], b_up.reshape(4, 128)], axis=0)
    vector_rows = jnp.concatenate(split_two(wide) + split_two(narrow), axis=0)
    chunks = jnp.concatenate(
        [images, jnp.broadcast_to(vector_rows[None], (16,) + vector_rows.shape)], axis=1
    )
    arrived = exchange(chunks)

    def columns_up(w):
        return jnp.concatenate([w[:, :128], w[:, 128:]], axis=0)

    qk = [w_qkv[d, :, 0, :128] for d in range(2)]
    vv = jnp.concatenate([w_qkv[0, :, 0, 128:], w_qkv[1, :, 0, 128:]], axis=-1)
    got_first = share(jnp.concatenate([qk[0], vv, w_out[0]], axis=0))
    got_second = share(jnp.concatenate([columns_up(w_up[0]), w_down[0]], axis=0))
    got_third = share(
        jnp.concatenate([qk[1], w_out[1], columns_up(w_up[1]), w_down[1]], axis=0)
    )

    def as_qk(block):
        block = block.reshape(8, 2, 128, 128).transpose(0, 2, 1, 3)
        return block.reshape(1024, 256)

    def as_v(block):
        block = block.reshape(8, 2, 128, 64).transpose(0, 2, 1, 3)
        return block.reshape(1024, 128)

    def as_up(block):
        block = block.reshape(8, 2, 2, 128, 128).transpose(0, 3, 1, 2, 4)
        return block.reshape(1024, 512)

    def as_side(block):
        depth = block.shape[1]
        block = block.reshape(8, 2, depth, 128).transpose(1, 2, 0, 3)
        return block.reshape(2 * depth, 1024)

    full_qkv = [
        jnp.concatenate(
            [as_qk(got_first[:, :128]), as_v(got_first[:, 128:256, :64])], axis=1
        ),
        jnp.concatenate(
            [as_qk(got_third[:, :128]), as_v(got_first[:, 128:256, 64:])], axis=1
        ),
    ]
    full_out = [as_side(got_first[:, 256:320]), as_side(got_third[:, 128:192])]
    full_up = [as_up(got_second[:, :256]), as_up(got_third[:, 192:448])]
    full_down = [as_side(got_second[:, 256:]), as_side(got_third[:, 448:])]

    picked = lax.dynamic_slice_in_dim(arrived, 2 * source, 2, 0)
    vectors_here = arrived[:2, rows:]
    low_part, high_part = picked[:, :half], picked[:, half:rows]
    tail = vectors_here[:, :12]
    keep = jnp.concatenate([jnp.where(first_core, low_part, high_part), tail], axis=1)
    give = jnp.concatenate([jnp.where(first_core, high_part, low_part), tail], axis=1)
    got = core_swap(give)
    part_0 = jnp.where(first_core, keep, got)
    part_1 = jnp.where(first_core, got, keep)
    left = jnp.concatenate([part_0[..., :64], part_1[..., :64]], axis=-1)
    right = jnp.concatenate([part_0[..., 64:], part_1[..., 64:]], axis=-1)
    gathered = ring_gather(jnp.concatenate([left, right[:, half:]], axis=1))
    gathered = gathered.transpose(2, 1, 0, 3).reshape(half + 24, 1024)
    stream = gathered[:half].astype(F32)
    cotangent_all = ring_gather(right[:, :half])
    cotangent_all = cotangent_all.transpose(2, 1, 0, 3).reshape(half, 1024)
    wide_all = gathered[half:].astype(F32).reshape(2, 2, 6, 1024).sum(axis=1)
    narrow_all = vectors_here[:, 12:].astype(F32)
    narrow_all = narrow_all[:, :6] + narrow_all[:, 6:]
    bias_qv = [narrow_all[:, d] for d in range(2)]
    bias_up = [narrow_all[:, 2 + 2 * d : 4 + 2 * d].reshape(512) for d in range(2)]

    live_key = (jnp.arange(rows) < seq)[None, None, :]
    scale = 64**-0.5

    kept = []
    for d in range(2):
        gain_1, bias_1, bias_o, gain_2, bias_2, bias_d = [wide_all[d, i] for i in range(6)]
        n1, r1 = normalize(stream)
        h1 = core_join((n1 * gain_1 + bias_1).astype(BF))
        packed = dot(h1, full_qkv[d], 1, 0)
        query = jnp.stack(
            [packed[:, 128 * i : 128 * i + 64] + bias_qv[d][i, :64] for i in range(2)]
        ).astype(BF)
        key = jnp.stack(
            [packed[:, 128 * i + 64 : 128 * i + 128] for i in range(2)]
        ).astype(BF)
        value = jnp.stack(
            [packed[:, 256 + 64 * i : 320 + 64 * i] + bias_qv[d][i, 64:] for i in range(2)]
        ).astype(BF)
        scores = jnp.where(live_key, bdot(query, key, 2, 2) * scale, -1e30)
        exponent = jnp.exp(scores - jnp.max(scores, axis=-1, keepdims=True))
        p = exponent / jnp.sum(exponent, axis=-1, keepdims=True)
        probs = p.astype(BF)
        attended = bdot(probs, value, 2, 1).astype(BF)
        heads = jnp.concatenate([attended[0], attended[1]], axis=-1)
        middle = stream + (total(dot(heads, full_out[d], 1, 0)) + bias_o)
        n2, r2 = normalize(middle)
        h2 = core_join((n2 * gain_2 + bias_2).astype(BF))
        upper = dot(h2, full_up[d], 1, 0) + bias_up[d]
        active, slope = gelu_pair(upper)
        active = active.astype(BF)
        stream = middle + (total(dot(active, full_down[d], 1, 0)) + bias_d)
        kept.append((n1, r1, h1, query, key, value, p, probs, heads, n2, r2, h2, slope, active))

    def to_owner(block, extra):
        mine = lax.dynamic_slice_in_dim(
            block.astype(BF).reshape(half, 2, 4, 128), ring, 1, 2
        )[:, :, 0]
        lanes_0 = jnp.concatenate([mine[:, 0, :64], mine[:, 1, :64]], axis=-1)
        lanes_1 = jnp.concatenate([mine[:, 0, 64:], mine[:, 1, 64:]], axis=-1)
        keep = jnp.where(first_core, lanes_0, lanes_1)
        got = core_swap(jnp.where(first_core, lanes_1, lanes_0))
        early = jnp.where(first_core, keep, got)
        late = jnp.where(first_core, got, keep)
        chunk = jnp.stack(
            [
                jnp.concatenate([early[:, 64 * i : 64 * i + 64], late[:, 64 * i : 64 * i + 64]], axis=-1)
                for i in range(2)
            ]
        )
        if extra is not None:
            chunk = jnp.concatenate([chunk, extra], axis=1)
        chunk = jnp.broadcast_to(chunk[None], (8,) + chunk.shape)
        return exchange(chunk.reshape((16,) + chunk.shape[2:]))

    def own_slots(received):
        slots = []
        for s in range(3):
            block = lax.dynamic_index_in_dim(
                received, jnp.minimum(my_offset + s, 15), 0, keepdims=False
            )[:half]
            tokens = jnp.concatenate([block[:, :64], block[: seq - half, 64:]], axis=0)
            slots.append(jnp.where(s < my_live, tokens.astype(F32), 0.0))
        return jnp.stack(slots)

    result = own_slots(to_owner(stream, None))

    def column(v):
        return jnp.sum(v.astype(F32), axis=0)

    def up_rows(grad):
        grad = grad.astype(BF).reshape(8, 128, 2, 2, 128).transpose(0, 2, 3, 1, 4)
        return grad.reshape(16, 256, 128)

    def side_rows(grad):
        depth = grad.shape[0] // 2
        grad = grad.astype(BF).reshape(2, depth, 8, 128).transpose(2, 0, 1, 3)
        return grad.reshape(16, depth, 128)

    def qkv_rows(grad):
        grad = grad.astype(BF)
        front = grad[:, :256].reshape(8, 128, 2, 128).transpose(0, 2, 1, 3)
        back = grad[:, 256:].reshape(8, 128, 2, 64).transpose(0, 2, 1, 3)
        return jnp.concatenate(
            [front.reshape(16, 128, 128), halves_on_lanes(back.reshape(16, 128, 64))], axis=1
        )

    grad_stream = cotangent_all.astype(F32)
    mlp_rows, attn_rows, wide_grads, narrow_grads = [None] * 2, [None] * 2, [None] * 2, [None] * 2
    mlp_got = None
    for d in (1, 0):
        gain_1, bias_1, bias_o, gain_2, bias_2, bias_d = [wide_all[d, i] for i in range(6)]
        n1, r1, h1, query, key, value, p, probs, heads, n2, r2, h2, slope, active = kept[d]
        down_half = grad_stream.astype(BF)
        down_grad = core_join(down_half)
        upper_grad = (dot(down_grad, full_down[d], 1, 1) * slope).astype(BF)
        norm_grad = total(dot(upper_grad, full_up[d], 1, 1))
        mlp_rows[d] = jnp.concatenate(
            [up_rows(dot(h2, upper_grad, 0, 0)), side_rows(dot(active, down_grad, 0, 0))], axis=1
        )
        if d == 1:
            mlp_got = exchange(mlp_rows[1])
        else:
            mixed_got = exchange(jnp.concatenate([attn_rows[1], mlp_rows[0]], axis=1))
        ln2 = [column(norm_grad * n2), column(norm_grad)]
        middle_grad = grad_stream + norm_backward(norm_grad, n2, r2, gain_2)
        mixed_half = middle_grad.astype(BF)
        mixed_grad = core_join(mixed_half)
        heads_grad = dot(mixed_grad, full_out[d], 1, 1).astype(BF)
        heads_grad = jnp.stack([heads_grad[:, :64], heads_grad[:, 64:]])
        prob_grad = bdot(heads_grad, value, 2, 2)
        value_grad = bdot(probs, heads_grad, 1, 1).astype(BF)
        score_grad = (
            p * (prob_grad - jnp.sum(prob_grad * p, axis=-1, keepdims=True))
        ).astype(BF)
        query_grad = (bdot(score_grad, key, 2, 1) * scale).astype(BF)
        key_grad = (bdot(score_grad, query, 1, 1) * scale).astype(BF)
        packed_grad = jnp.concatenate(
            [query_grad[0], key_grad[0], query_grad[1], key_grad[1], value_grad[0], value_grad[1]],
            axis=-1,
        )
        norm_grad = total(dot(packed_grad, full_qkv[d], 1, 1))
        attn_rows[d] = jnp.concatenate(
            [qkv_rows(dot(h1, packed_grad, 0, 0)), side_rows(dot(heads, mixed_grad, 0, 0))], axis=1
        )
        if d == 0:
            attn_got = exchange(attn_rows[0])
        wide_grads[d] = jnp.stack(
            [column(norm_grad * n1), column(norm_grad), column(mixed_half)]
            + ln2
            + [column(down_half)]
        )
        narrow_grads[d] = (
            jnp.concatenate([column(query_grad.transpose(1, 0, 2)), column(value_grad.transpose(1, 0, 2))], axis=-1),
            column(upper_grad).reshape(2, 256),
        )
        grad_stream = middle_grad + norm_backward(norm_grad, n1, r1, gain_1)

    wide = jnp.stack(wide_grads).reshape(12, 2, 4, 128)
    wide = lax.dynamic_slice_in_dim(wide, ring, 1, 2)[:, :, 0]
    keep = jnp.where(first_core, wide[..., :64], wide[..., 64:])
    give = jnp.where(first_core, wide[..., 64:], wide[..., :64])
    wide = (keep + core_swap(give)).transpose(1, 0, 2)
    wide = jnp.concatenate([wide[:, :6], wide[:, 6:]], axis=-1)
    narrow = jnp.concatenate(
        [
            narrow_grads[0][0][:, None],
            narrow_grads[1][0][:, None],
            narrow_grads[0][1].reshape(2, 2, 128),
            narrow_grads[1][1].reshape(2, 2, 128),
        ],
        axis=1,
    )
    extra = jnp.concatenate(split_two(jnp.concatenate([wide, narrow], axis=1)), axis=1)
    received = to_owner(grad_stream, extra)
    grad_inputs = own_slots(received)
    vector_sums = jnp.sum(received[:, half:].astype(F32), axis=0)
    vector_sums = vector_sums[:12] + vector_sums[12:]
    wide_sums = jnp.stack([vector_sums[:6, :64], vector_sums[:6, 64:]], axis=1)
    grad_b_qv = vector_sums[6:8].reshape(2, 1, 128)
    grad_b_up = vector_sums[8:12].reshape(2, 256)

    def summed(block):
        return jnp.sum(block.astype(F32), axis=0)

    mlp_1 = summed(mlp_got)
    mixed = summed(mixed_got)
    attn_0 = summed(attn_got)
    attn = [attn_0, mixed[:256]]
    mlp = [mixed[256:], mlp_1]

    def own_qkv(block):
        return jnp.concatenate([block[:128], halves_on_rows(block[128:192])], axis=-1)

    grad_qkv = jnp.stack([own_qkv(a) for a in attn])[:, :, None, :]
    grad_out = jnp.stack([a[192:256] for a in attn])
    grad_up = jnp.stack([jnp.concatenate([m[:128], m[128:256]], axis=-1) for m in mlp])
    grad_down = jnp.stack([m[256:] for m in mlp])
    return (
        result,
        grad_inputs,
        wide_sums[0],
        wide_sums[1],
        grad_qkv,
        grad_b_qv,
        grad_out,
        wide_sums[2],
        wide_sums[3],
        wide_sums[4],
        grad_up,
        grad_b_up,
        grad_down,
        wide_sums[5],
    )


def solution(mesh):
    split = Mesh(mesh.devices.reshape(4, 2, 2, 4, 2), ("y", "xl", "xh", "z", "c"))
    gx = ("y", "xl")
    gy = ("xh", "z", "c")
    token = P(gx, None, gy)
    vector = P(None, gy)
    return jax.shard_map(
        shards,
        mesh=split,
        in_specs=(
            token,
            token,
            P(),
            vector,
            vector,
            P(None, gx, gy, None),
            P(None, gy, None),
            P(None, gy, gx),
            vector,
            vector,
            vector,
            P(None, gx, gy),
            vector,
            P(None, gy, gx),
            vector,
        ),
        out_specs=(
            token,
            token,
            vector,
            vector,
            P(None, gx, gy, None),
            P(None, gy, None),
            P(None, gy, gx),
            vector,
            vector,
            vector,
            P(None, gx, gy),
            vector,
            P(None, gy, gx),
            vector,
        ),
        check_vma=False,
    )
```

```python
import functools

import jax
import jax.numpy as jnp
from jax import lax
from jax.experimental import pallas as pl
from jax.experimental.pallas import tpu as pltpu
from jax.sharding import Mesh, PartitionSpec as P

EPS = 1e-06
BF = jnp.bfloat16
F32 = jnp.float32
DP = ("y", "xl", "xh")
SWAP = [(0, 1), (1, 0)]
PAIR_A = [(0, 1), (1, 0), (2, 3), (3, 2)]
PAIR_B = [(0, 3), (3, 0), (1, 2), (2, 1)]


def dot(a, b, ca, cb):
    return lax.dot_general(a, b, (((ca,), (cb,)), ((), ())), preferred_element_type=F32)


def core_swap(block):
    return lax.ppermute(block, "c", SWAP)


def ring_blocks(block):
    return [block] + [
        lax.ppermute(block, "z", [(i, (i + step) % 4) for i in range(4)]) for step in (1, 3, 2)
    ]


def total(mine, theirs, work=None, late=None):
    mine = (mine + core_swap(theirs).astype(F32)).astype(BF)
    if work is not None:
        mine, given = lax.optimization_barrier((mine, work[1]))
    cut = mine.shape[1] // 2
    left, right = mine[:, :cut], mine[:, cut:]
    got_left = lax.ppermute(left, "z", PAIR_A)
    got_right = lax.ppermute(right, "z", PAIR_B)
    done = work[0](given) if work is not None else None
    left = (left.astype(F32) + got_left.astype(F32)).astype(BF)
    right = (right.astype(F32) + got_right.astype(F32)).astype(BF)
    left, right, late, done = lax.optimization_barrier((left, right, late, done))
    got_left = lax.ppermute(left, "z", PAIR_B)
    got_right = lax.ppermute(right, "z", PAIR_A)
    return (left, got_left, right, got_right), done, late


HALF = 112
ROWS = 2 * HALF
WIDTH = 1024


def run(kernel, outs, args, flops, scratch=(), smem=0, far=(), grant=16):
    far = [f if isinstance(f, tuple) else (f, None, None) for f in far]
    size = sum(a.size * a.dtype.itemsize for a in args)
    size += sum(o.size * o.dtype.itemsize for o in outs)
    fetched = [f[0] for f in far]
    specs = [
        pl.BlockSpec(
            memory_space=pltpu.SMEM if i < smem else pltpu.HBM if i in fetched else pltpu.VMEM
        )
        for i in range(len(args))
    ]
    held = []
    for i, _, count in far:
        sizes = args[i].shape
        sizes = sizes if count is None else (sizes[0], count) + sizes[2:]
        held.append(pltpu.VMEM(sizes, args[i].dtype))

    def body(*refs):
        refs = list(refs)
        rest = refs[len(args) :]
        if far:
            spaces, sems = rest[-1 - len(far) : -1], rest[-1]
            rest = rest[: -1 - len(far)]
            copies = []
            for k, (i, start, count) in enumerate(far):
                source = refs[i] if count is None else refs[i].at[:, start : start + count]
                copies.append(pltpu.make_async_copy(source, spaces[k], sems.at[k]))
                copies[-1].start()
            for k, copy in enumerate(copies):
                copy.wait()
                refs[fetched[k]] = spaces[k]
        kernel(*refs[: len(args)], *rest)

    return pl.pallas_call(
        body,
        out_shape=list(outs),
        in_specs=specs,
        out_specs=[pl.BlockSpec(memory_space=pltpu.VMEM)] * len(outs),
        scratch_shapes=list(scratch) + held + ([pltpu.SemaphoreType.DMA((len(far),))] if far else []),
        compiler_params=pltpu.CompilerParams(vmem_limit_bytes=grant * 2**20),
        cost_estimate=pl.CostEstimate(
            flops=int(flops), bytes_accessed=int(size), transcendentals=0
        ),
    )(*args)


def shape(dtype, *sizes):
    return jax.ShapeDtypeStruct(sizes, dtype)


def norm_parts(stream):
    center = stream - jnp.mean(stream, axis=-1, keepdims=True)
    factor = lax.rsqrt(jnp.mean(center * center, axis=-1, keepdims=True) + EPS)
    return center * factor, factor


def place_attention(w, w_qkv, w_out):
    for g in range(8):
        rows = slice(128 * g, 128 * g + 128)
        for i in range(2):
            w_qkv[rows, 128 * i : 128 * i + 128] = w[2 * g + i, :128]
            w_out[64 * i : 64 * i + 64, rows] = w[2 * g + i, 192:256]
        first, second = w[2 * g, 128:192], w[2 * g + 1, 128:192]
        w_qkv[128 * g : 128 * g + 64, 256:] = jnp.concatenate(
            [first[:, :64], second[:, :64]], axis=1
        )
        w_qkv[128 * g + 64 : 128 * g + 128, 256:] = jnp.concatenate(
            [first[:, 64:], second[:, 64:]], axis=1
        )


def place_mlp(w, w_up, w_down):
    for g in range(8):
        rows = slice(128 * g, 128 * g + 128)
        for i in range(2):
            for j in range(2):
                at = 256 * i + 128 * j
                w_up[rows, at : at + 128] = w[2 * g + i, 128 * j : 128 * j + 128]
            w_down[256 * i : 256 * i + 256, rows] = w[2 * g + i, 256:512]


def both_rows(mine, other):
    return jnp.concatenate([mine[...], other[...]], axis=0)


def softmax(valid, query, key):
    scores = dot(query, key, 1, 1) * 64**-0.5
    at = lax.broadcasted_iota(jnp.int32, (1, ROWS), 1)
    limit = jnp.where(at < HALF, valid[0], valid[1] + HALF)
    scores = jnp.where(at < limit, scores, -1e30)
    exponent = jnp.exp(scores - jnp.max(scores, axis=-1, keepdims=True))
    return exponent / jnp.sum(exponent, axis=-1, keepdims=True)


def part_of(packed, name, i):
    start = {"q": 128 * i, "k": 128 * i + 64, "v": 256 + 64 * i}[name]
    return packed[:, start : start + 64]


def attention_forward(valid, mine, other, w, bias, packed_out, heads_out, out, away, w_qkv, w_out):
    place_attention(w, w_qkv, w_out)
    packed = dot(both_rows(mine, other), w_qkv[...], 1, 0) + bias[...]
    packed_out[...] = packed.astype(BF)
    heads = []
    for i in range(2):
        query, key, value = [part_of(packed, n, i).astype(BF) for n in "qkv"]
        probs = softmax(valid, query, key).astype(BF)
        heads.append(dot(probs, value, 1, 0))
    heads = jnp.concatenate(heads, axis=1).astype(BF)
    heads_out[...] = heads
    result = dot(heads, w_out[...], 1, 0)
    out[...] = result[:HALF]
    away[...] = result[HALF:].astype(BF)


def attention_backward(valid, mine, other, packed_in, w, grad_out, sums, out, away, w_qkv, w_out):
    place_attention(w, w_qkv, w_out)
    heads_grad = dot(both_rows(mine, other), w_out[...], 1, 1)
    packed = packed_in[...].astype(F32)
    parts = []
    values = []
    for i in range(2):
        query, key, value = [part_of(packed, n, i).astype(BF) for n in "qkv"]
        p = softmax(valid, query, key)
        upstream = heads_grad[:, 64 * i : 64 * i + 64].astype(BF)
        prob_grad = dot(upstream, value, 1, 1)
        values.append(dot(p.astype(BF), upstream, 0, 0))
        score_grad = (
            p * (prob_grad - jnp.sum(prob_grad * p, axis=-1, keepdims=True))
        ).astype(BF)
        parts.append(dot(score_grad, key, 1, 0) * 64**-0.5)
        parts.append(dot(score_grad, query, 0, 0) * 64**-0.5)
    grad = jnp.concatenate(parts + values, axis=1).astype(BF)
    grad_out[...] = grad
    sums[...] = jnp.sum(grad.astype(F32), axis=0, keepdims=True)
    result = dot(grad, w_qkv[...], 1, 1)
    out[...] = result[:HALF]
    away[...] = result[HALF:].astype(BF)


def attention_weights(h_mine, h_other, grad, heads, mine, other, rows_out):
    qkv = dot(both_rows(h_mine, h_other), grad[...], 0, 0)
    back = dot(heads[...], both_rows(mine, other), 0, 0).astype(BF)
    for g in range(8):
        for i in range(2):
            at = 2 * g + i
            rows_out[at, :128] = qkv[128 * g : 128 * g + 128, 128 * i : 128 * i + 128].astype(BF)
            side = qkv[128 * g : 128 * g + 128, 256 + 64 * i : 320 + 64 * i]
            rows_out[at, 128:192] = jnp.concatenate([side[:64], side[64:]], axis=1).astype(BF)
            rows_out[at, 192:256] = back[64 * i : 64 * i + 64, 128 * g : 128 * g + 128]


def mlp_forward(mine, other, w, bias, act_out, slope_out, out, away, w_up, w_down):
    place_mlp(w, w_up, w_down)
    upper = dot(both_rows(mine, other), w_up[...], 1, 0) + bias[...]
    phi = 0.5 * (1.0 + lax.erf(upper * 0.5**0.5))
    act = (upper * phi).astype(BF)
    act_out[...] = act
    slope_out[...] = phi + upper * (jnp.exp(-0.5 * upper * upper) * 0.3989422804014327)
    result = dot(act, w_down[...], 1, 0)
    out[...] = result[:HALF]
    away[...] = result[HALF:].astype(BF)


def mlp_backward(mine, other, w, slope, grad_out, sums, out, away, w_up, w_down):
    place_mlp(w, w_up, w_down)
    grad = (dot(both_rows(mine, other), w_down[...], 1, 1) * slope[...]).astype(BF)
    grad_out[...] = grad
    sums[...] = jnp.sum(grad.astype(F32), axis=0, keepdims=True)
    result = dot(grad, w_up[...], 1, 1)
    out[...] = result[:HALF]
    away[...] = result[HALF:].astype(BF)


def mixed_rows(place, h_mine, h_other, grad, act, mine, other, attention, keep, got, rows_out):
    mlp_weights(h_mine, h_other, grad, act, mine, other, rows_out)
    tokens = owner_rows(place[1] == 0, keep, got)
    for g in range(8):
        for i in range(2):
            rows_out[2 * g + i, 512:768] = attention[2 * g + i]
            rows_out[2 * g + i, 768:] = tokens[i]


def mlp_weights(h_mine, h_other, grad, act, mine, other, rows_out):
    up = dot(both_rows(h_mine, h_other), grad[...], 0, 0).astype(BF)
    down = dot(act[...], both_rows(mine, other), 0, 0).astype(BF)
    for g in range(8):
        cols = slice(128 * g, 128 * g + 128)
        for i in range(2):
            for j in range(2):
                at = 256 * i + 128 * j
                rows_out[2 * g + i, 128 * j : 128 * j + 128] = up[cols, at : at + 128]
            rows_out[2 * g + i, 256:512] = down[256 * i : 256 * i + 256, cols]


def pair_sum(left, got_left, right, got_right):
    return jnp.concatenate(
        [
            left[...].astype(F32) + got_left[...].astype(F32),
            right[...].astype(F32) + got_right[...].astype(F32),
        ],
        axis=1,
    )


def ring_place(ring, blocks, store):
    for step, block in zip((0, 1, 3, 2), blocks):
        place = lax.rem(ring + 4 - step, 4) * 128
        for i in range(2):
            store(pl.ds(pl.multiple_of(512 * i + place, 128), 128), block, i)


def norm_first(ring, a, b, c, d, stream_out, out, wide_out, cotangent, sums):
    def store(columns, block, i):
        stream_out[:, columns] = block[i, :HALF].astype(F32)
        for depth in range(2):
            rows = block[i, HALF + 16 * depth : HALF + 16 * depth + 16].astype(F32)
            wide_out[depth, :, columns] = rows[:8] + rows[8:]
        upstream = block[i, HALF + 32 :]
        cotangent[:, columns] = upstream
        sums[:, columns] = jnp.sum(upstream.astype(F32), axis=0, keepdims=True)

    ring_place(ring[0], (a, b, c, d), store)
    normed, _ = norm_parts(stream_out[...])
    out[...] = (normed * wide_out[0, 0:1] + wide_out[0, 1:2]).astype(BF)


def owner_lanes(source, ring, first_core, keep, give):
    parts = []
    for i in range(2):
        at = pl.multiple_of(512 * i + 128 * ring, 128)
        parts.append(source[:, pl.ds(at, 128)].astype(F32))
    lanes = [
        jnp.concatenate([parts[0][:, s], parts[1][:, s]], axis=1)
        for s in (slice(0, 64), slice(64, 128))
    ]
    keep[...] = jnp.where(first_core, lanes[0], lanes[1]).astype(keep.dtype)
    give[...] = jnp.where(first_core, lanes[1], lanes[0]).astype(give.dtype)


def owner_rows(first_core, keep, got):
    keep, got = keep[...].astype(F32), got[...].astype(F32)
    early, late = jnp.where(first_core, keep, got), jnp.where(first_core, got, keep)
    return [
        jnp.concatenate([early[:, s], late[:, s]], axis=1).astype(BF)
        for s in (slice(0, 64), slice(64, 128))
    ]


def owner_tokens(block, live):
    block = block.astype(F32)
    tokens = jnp.concatenate([block[:, :64], block[:, 64:]], axis=0)
    return jnp.where(live, tokens.T[:, :197], 0.0)


def norm_last(place, left, got_left, right, got_right, stream, wide, keep, give, new):
    new[...] = stream[...] + (pair_sum(left, got_left, right, got_right) + wide[1, 5:6])
    owner_lanes(new, place[0], place[1] == 0, keep, give)


def prepare(offset, images, g1, b1, bo, g2, b2, bd, qv, up, w_qkv, w_out, out):
    wide = [jnp.concatenate([v[0:1], v[1:2]], axis=1) for v in (g1, b1, bo, g2, b2, bd)]
    wide = jnp.concatenate(wide + [jnp.zeros((2, 128), F32)], axis=0)
    narrow = [qv[0], qv[1], up[0:1, :128], up[0:1, 128:], up[1:2, :128], up[1:2, 128:]]
    narrow = jnp.concatenate(narrow + [jnp.zeros((2, 128), F32)], axis=0)
    rows = []
    for v in (wide, narrow):
        high = v.astype(BF).astype(F32)
        rows += [high, v - high]
    rows = jnp.concatenate(rows, axis=0).astype(BF)
    side = w_qkv[0, :, 128:].astype(F32)
    side = jnp.concatenate([side[:64], side[64:]], axis=1).astype(BF)
    for w in range(16):
        out[w, :ROWS] = images[jnp.clip(w - offset[0], 0, 2)]
        out[w, ROWS:256] = rows
        out[w, 256:384] = w_qkv[0, :, :128]
        out[w, 384:448] = side
        out[w, 448:512] = w_out[0]


def prepare_next(w_qkv, w_out, w_up, w_down, out):
    side = w_qkv[1, :, 128:].astype(F32)
    side = jnp.concatenate([side[:64], side[64:]], axis=1).astype(BF)
    for w in range(16):
        out[w, :128] = w_up[0, :, :128]
        out[w, 128:256] = w_up[0, :, 128:]
        out[w, 256:512] = w_down[0]
        out[w, 512:640] = w_qkv[1, :, :128]
        out[w, 640:704] = side
        out[w, 704:768] = w_out[1]


def prepare_mlp(w_up, w_down, out):
    for w in range(out.shape[0]):
        out[w, :128] = w_up[1, :, :128]
        out[w, 128:256] = w_up[1, :, 128:]
        out[w, 256:] = w_down[1]


def norm_forward(at, left, got_left, right, got_right, stream, wide, stream_out, out):
    shift, gain, bias = [wide[d, i : i + 1] for d, i in at]
    new = stream[...] + (pair_sum(left, got_left, right, got_right) + shift)
    stream_out[...] = new
    normed, _ = norm_parts(new)
    out[...] = (normed * gain + bias).astype(BF)


def norm_backward(at, left, got_left, right, got_right, stream, upstream, wide, grad_out, low_out, sums):
    grad = pair_sum(left, got_left, right, got_right)
    normed, factor = norm_parts(stream[...])
    scaled = grad * wide[at[0], at[1] : at[1] + 1]
    first = jnp.mean(scaled, axis=-1, keepdims=True)
    second = jnp.mean(scaled * normed, axis=-1, keepdims=True)
    new = upstream[...].astype(F32) + factor * (scaled - first - normed * second)
    grad_out[...] = new
    low = new.astype(BF)
    low_out[...] = low.astype(low_out.dtype)
    sums[0:1] = jnp.sum(grad * normed, axis=0, keepdims=True)
    sums[1:2] = jnp.sum(grad, axis=0, keepdims=True)
    sums[2:3] = jnp.sum(low.astype(F32), axis=0, keepdims=True)
    sums[3:8] = jnp.zeros((5, WIDTH), F32)


def norm_backward_last(
    place, left, got_left, right, got_right, stream, upstream, wide, s20, s11, s21, low_sum,
    keep, give, keep_v, give_v, new, sums, table,
):
    norm_backward((0, 0), left, got_left, right, got_right, stream, upstream, wide, new, new, sums)
    owner_lanes(new, place[0], place[1] == 0, keep, give)
    pieces = [sums[0:2], s20[2:3], s20[0:2], s11[2:3], s11[0:2], s21[2:3], s21[0:2], low_sum[...]]
    table[...] = jnp.concatenate(pieces + [jnp.zeros((4, WIDTH), F32)], axis=0)
    owner_lanes(table, place[0], place[1] == 0, keep_v, give_v)


def final_rows(place, rows_in, keep, got, keep_v, got_v, p0, p1, u0, u1, out, held, sem):
    wide = keep_v[...] + got_v[...]
    high = wide.astype(BF).astype(F32)
    low = wide - high
    tokens = owner_rows(place[1] == 0, keep, got)
    for i in range(2):
        part = slice(64 * i, 64 * i + 64)
        narrow = [
            jnp.concatenate(
                [p[:, 128 * i : 128 * i + 64], p[:, 256 + 64 * i : 320 + 64 * i]], axis=1
            )
            for p in (p0, p1)
        ]
        for u in (u0, u1):
            narrow += [u[:, 256 * i : 256 * i + 128], u[:, 256 * i + 128 : 256 * i + 256]]
        narrow = jnp.concatenate(narrow + [jnp.zeros((2, 128), F32)], axis=0)
        narrow_high = narrow.astype(BF).astype(F32)
        rows = jnp.concatenate(
            [jnp.concatenate([high[:, part], low[:, part]], axis=1), narrow_high, narrow - narrow_high],
            axis=0,
        ).astype(BF)
        for g in range(8):
            held[2 * g + i, :HALF] = tokens[i]
            held[2 * g + i, HALF:] = rows
    copy = pltpu.make_async_copy(held, out.at[:, 256:400], sem)
    copy.start()
    copy.wait()


def collect(meta, received, out, held, sems):
    copies = []
    for s in range(3):
        at = jnp.minimum(meta[0] + s, 15)
        copies.append(
            pltpu.make_async_copy(received.at[at, 768:880], held.at[s], sems.at[s])
        )
        copies[-1].start()
    for s in range(3):
        copies[s].wait()
        out[s] = owner_tokens(held[s], s < meta[1])


def finish(meta, received, sum_1, out, qkv, w_out, g1, b1, bo, g2, b2, bd, qv, up, weights, vectors, held, sems):
    copies = [
        pltpu.make_async_copy(received.at[:, 0:256], weights, sems.at[3]),
        pltpu.make_async_copy(received.at[:, 368:400], vectors, sems.at[4]),
    ]
    for s in range(3):
        at = jnp.minimum(meta[0] + s, 15)
        copies.append(
            pltpu.make_async_copy(received.at[at, 256:368], held.at[s], sems.at[s])
        )
    for copy in copies:
        copy.start()
    for copy in copies:
        copy.wait()
    for s in range(3):
        out[s] = owner_tokens(held[s], s < meta[1])
    total_v = jnp.sum(vectors[...].astype(F32), axis=0)
    wide = total_v[:16, :64] + total_v[:16, 64:]
    for v, ref in enumerate((g1, b1, bo, g2, b2, bd)):
        ref[...] = jnp.concatenate([wide[v : v + 1], wide[v + 6 : v + 7]], axis=0)
    narrow = total_v[16:24] + total_v[24:32]
    qv[...] = narrow[0:2]
    for d in range(2):
        up[d : d + 1] = jnp.concatenate([narrow[2 + 2 * d : 3 + 2 * d], narrow[3 + 2 * d : 4 + 2 * d]], axis=1)
    for d in range(2):
        block = jnp.sum(weights[...].astype(F32), axis=0) if d == 0 else sum_1[...]
        side = block[128:192]
        qkv[d, :, :128] = block[:128]
        qkv[d, :64, 128:] = side[:, :64]
        qkv[d, 64:, 128:] = side[:, 64:]
        w_out[d] = block[192:256]


ATTENTION_SCRATCH = (pltpu.VMEM((WIDTH, 384), BF), pltpu.VMEM((128, WIDTH), BF))
MLP_SCRATCH = (pltpu.VMEM((WIDTH, 512), BF), pltpu.VMEM((512, WIDTH), BF))
SUM_SHAPES = (shape(F32, HALF, WIDTH), shape(BF, HALF, WIDTH))
NORM_SHAPES = (shape(F32, HALF, WIDTH), shape(BF, HALF, WIDTH))
ATTENTION_FLOPS = 2 * ROWS * WIDTH * 512
MLP_FLOPS = 2 * ROWS * WIDTH * 1024


def exchange(chunks):
    return lax.all_to_all(chunks, DP, 0, 0)


def shards(
    inputs,
    cotangent,
    group_images,
    ln1_gain,
    ln1_bias,
    w_qkv,
    b_qv,
    w_out,
    b_out,
    ln2_gain,
    ln2_bias,
    w_up,
    b_up,
    w_down,
    b_down,
):
    seq = inputs.shape[1]
    half, rows = HALF, ROWS
    core = lax.axis_index("c")
    ring = lax.axis_index("z")
    group = lax.axis_index(("y", "xl"))
    worker = lax.axis_index(DP)
    first_core = core == 0

    earlier = jnp.arange(8)[:, None] > jnp.arange(8)[None, :]
    offsets = jnp.sum(jnp.where(earlier, group_images[None, :], 0), axis=1)
    my_offset = jnp.sum(jnp.where(jnp.arange(8) < group, group_images, 0))
    my_live = jnp.sum(jnp.where(jnp.arange(8) == group, group_images, 0))
    source = jnp.sum((offsets <= worker).astype(jnp.int32)) - 1
    valid = jnp.where(first_core, jnp.array([half, seq - half]), jnp.array([seq - half, half]))
    valid = valid.astype(jnp.int32)

    images = jnp.concatenate([inputs, cotangent], axis=-1)
    images = jnp.pad(images, ((0, 0), (0, rows - seq), (0, 0)))
    w_qkv = w_qkv.reshape(2, 128, 192)
    (chunks,) = run(
        prepare,
        (shape(BF, 16, 512, 128),),
        (my_offset.reshape(1), images, ln1_gain, ln1_bias, b_out, ln2_gain, ln2_bias)
        + (b_down, b_qv, b_up, w_qkv, w_out),
        0,
        (),
        1,
        range(2, 12),
        56,
    )
    arrived = exchange(chunks)
    (next_rows,) = run(
        prepare_next, (shape(BF, 16, 768, 128),), (w_qkv, w_out, w_up, w_down), 0
    )
    (mlp_rows_1,) = run(prepare_mlp, (shape(BF, 16, 512, 128),), (w_up, w_down), 0)
    next_rows, mlp_rows_1, arrived = lax.optimization_barrier((next_rows, mlp_rows_1, arrived))
    following = exchange(next_rows)
    mlp_w = [following, None]
    attention_w = [arrived, following]
    attention_at = [256, 512]

    picked = lax.dynamic_slice(arrived, (2 * source, 0, 0), (2, rows, 128))
    vectors_here = arrived[:2, rows:256]
    low_part, high_part = picked[:, :half], picked[:, half:rows]
    tail = vectors_here[:, :16]
    keep = jnp.concatenate([jnp.where(first_core, low_part, high_part), tail], axis=1)
    give = jnp.concatenate([jnp.where(first_core, high_part, low_part), tail], axis=1)
    got = core_swap(give)
    part_0 = jnp.where(first_core, keep, got)
    part_1 = jnp.where(first_core, got, keep)
    left = jnp.concatenate([part_0[..., :64], part_1[..., :64]], axis=-1)
    right = jnp.concatenate([part_0[..., 64:], part_1[..., 64:]], axis=-1)
    place = jnp.stack([ring, core]).astype(jnp.int32)
    stream, h1, wide, cotangent_low, low_sum = run(
        norm_first,
        NORM_SHAPES
        + (shape(F32, 2, 8, WIDTH), shape(BF, half, WIDTH), shape(F32, 1, WIDTH)),
        [place] + ring_blocks(jnp.concatenate([left, right[:, half:], right[:, :half]], axis=1)),
        0,
        (),
        1,
    )
    narrow_all = vectors_here[:, 16:].astype(F32)
    narrow_all = narrow_all[:, :8] + narrow_all[:, 8:]
    bias_qv = [narrow_all[:, d] for d in range(2)]
    bias_up = [narrow_all[:, 2 + 2 * d : 4 + 2 * d].reshape(512) for d in range(2)]

    row = lambda v: v.reshape(1, -1)
    bias_packed = [
        jnp.concatenate(
            [bias_qv[d][0, :64], jnp.zeros(64), bias_qv[d][1, :64], jnp.zeros(64)]
            + [bias_qv[d][0, 64:], bias_qv[d][1, 64:]]
        )[None]
        for d in range(2)
    ]

    kept = []
    for d in range(2):
        h1_other = core_swap(h1)
        packed, heads, mine, theirs = run(
            attention_forward,
            (shape(BF, ROWS, 384), shape(BF, ROWS, 128)) + SUM_SHAPES,
            (valid, h1, h1_other, attention_w[d], bias_packed[d]),
            ATTENTION_FLOPS,
            ATTENTION_SCRATCH,
            1,
            ((3, attention_at[d], 256),),
        )
        pairs, _, _ = total(mine, theirs)
        if d == 1:
            pairs, mlp_w[1] = lax.optimization_barrier((pairs, mlp_w[1]))
        middle, h2 = run(
            functools.partial(norm_forward, ((d, 2), (d, 3), (d, 4))),
            NORM_SHAPES,
            pairs + (stream, wide),
            0,
        )
        h2_other = core_swap(h2)
        act, slope, mine, theirs = run(
            mlp_forward,
            (shape(BF, ROWS, 512), shape(F32, ROWS, 512)) + SUM_SHAPES,
            (h2, h2_other, mlp_w[d], row(bias_up[d])),
            MLP_FLOPS,
            MLP_SCRATCH,
            0,
            ((2, 0, 512),),
        )
        kept.append((stream, h1, h1_other, packed, heads, middle, h2, h2_other, act, slope))
        if d == 0:
            pairs, _, _ = total(mine, theirs)
            mlp_rows_1, _ = lax.optimization_barrier((mlp_rows_1, following))
            mlp_w[1] = exchange(mlp_rows_1)
            stream, h1 = run(
                functools.partial(norm_forward, ((0, 5), (1, 0), (1, 1))),
                NORM_SHAPES,
                pairs + (middle, wide),
                0,
            )
    grad_low = cotangent_low
    low_other = core_swap(grad_low)
    pairs, _, _ = total(mine, theirs)
    keep, give = run(
        norm_last,
        (shape(BF, half, 128), shape(BF, half, 128)),
        (place,) + pairs + (middle, wide),
        0,
        (pltpu.VMEM((half, WIDTH), F32),),
        1,
    )
    out_keep, out_got = keep, core_swap(give)

    grad_stream = cotangent_low
    previous = mlp_got = None
    sums, narrow_sums = {}, {}
    for d in (1, 0):
        start, h1, h1_other, packed, heads, middle, h2, h2_other, act, slope = kept[d]
        if d == 0:
            low_other = core_swap(grad_low)
            low_other, mlp_got = lax.optimization_barrier((low_other, previous))
        upper_grad, up_sum, mine, theirs = run(
            mlp_backward,
            (shape(BF, ROWS, 512), shape(F32, 1, 512)) + SUM_SHAPES,
            (grad_low, low_other, mlp_w[d], slope),
            MLP_FLOPS,
            MLP_SCRATCH,
            0,
            ((2, 0, 512), 3),
        )

        def mlp_work(upper_grad):
            args = (h2, h2_other, upper_grad, act, grad_low, low_other)
            if d == 0:
                return run(
                    mixed_rows,
                    (shape(BF, 16, 880, 128),),
                    (place,) + args + (attention_grad, out_keep, out_got),
                    MLP_FLOPS,
                    (),
                    1,
                    (1, 2, 4),
                )[0]
            return run(mlp_weights, (shape(BF, 16, 512, 128),), args, MLP_FLOPS, (), 0, (0, 1, 3))[0]

        pairs, mlp_grad, _ = total(mine, theirs, (mlp_work, upper_grad))
        if d == 0:
            mlp_grad, mlp_got = lax.optimization_barrier((mlp_grad, mlp_got))
        previous = exchange(mlp_grad)
        grad_stream, grad_low, sums[2, d] = run(
            functools.partial(norm_backward, (d, 3)),
            NORM_SHAPES + (shape(F32, 8, WIDTH),),
            pairs + (middle, grad_stream, wide),
            0,
        )
        low_other = core_swap(grad_low)
        packed_grad, packed_sum, mine, theirs = run(
            attention_backward,
            (shape(BF, ROWS, 384), shape(F32, 1, 384)) + SUM_SHAPES,
            (valid, grad_low, low_other, packed, attention_w[d]),
            ATTENTION_FLOPS,
            ATTENTION_SCRATCH,
            1,
            (3, (4, attention_at[d], 256)),
        )
        narrow_sums[d] = (packed_sum, up_sum)

        def attention_work(packed_grad):
            return run(
                attention_weights,
                (shape(BF, 16, 256 if d == 1 else 400, 128),),
                (h1, h1_other, packed_grad, heads, grad_low, low_other),
                ATTENTION_FLOPS,
                (),
                0,
                (0, 1, 3),
            )[0]

        pairs, attention_grad, _ = total(mine, theirs, (attention_work, packed_grad))
        if d == 1:
            grad_stream, grad_low, sums[1, d] = run(
                functools.partial(norm_backward, (d, 0)),
                NORM_SHAPES + (shape(F32, 8, WIDTH),),
                pairs + (start, grad_stream, wide),
                0,
            )
    keep, give, keep_v, give_v = run(
        norm_backward_last,
        (shape(BF, half, 128), shape(BF, half, 128), shape(F32, 16, 128), shape(F32, 16, 128)),
        (place,) + pairs + (start, grad_stream, wide, sums[2, 0], sums[1, 1], sums[2, 1], low_sum),
        0,
        (pltpu.VMEM((half, WIDTH), F32), pltpu.VMEM((8, WIDTH), F32), pltpu.VMEM((16, WIDTH), F32)),
        1,
    )
    (last_rows,) = pl.pallas_call(
        final_rows,
        out_shape=[shape(BF, 16, 400, 128)],
        in_specs=[pl.BlockSpec(memory_space=pltpu.SMEM), pl.BlockSpec(memory_space=pltpu.HBM)]
        + [pl.BlockSpec(memory_space=pltpu.VMEM)] * 8,
        out_specs=[pl.BlockSpec(memory_space=pltpu.HBM)],
        scratch_shapes=[pltpu.VMEM((16, 144, 128), BF), pltpu.SemaphoreType.DMA(())],
        input_output_aliases={1: 0},
        compiler_params=pltpu.CompilerParams(vmem_limit_bytes=16 * 2**20),
    )(
        place,
        attention_grad,
        keep,
        core_swap(give),
        keep_v,
        core_swap(give_v),
        narrow_sums[0][0],
        narrow_sums[1][0],
        narrow_sums[0][1],
        narrow_sums[1][1],
    )
    last_rows, previous = lax.optimization_barrier((last_rows, previous))
    last = exchange(last_rows)
    mixed, _ = lax.optimization_barrier((previous, last_rows))

    def summed(block):
        return jnp.sum(block.astype(F32), axis=0)

    mlp = [summed(mixed[:, :512]), summed(mlp_got)]
    grad_up = jnp.stack([jnp.concatenate([m[:128], m[128:256]], axis=-1) for m in mlp])
    grad_down = jnp.stack([m[256:] for m in mlp])
    meta = jnp.stack([my_offset, my_live]).astype(jnp.int32)
    hbm, vmem = pl.BlockSpec(memory_space=pltpu.HBM), pl.BlockSpec(memory_space=pltpu.VMEM)
    smem = pl.BlockSpec(memory_space=pltpu.SMEM)
    (result,) = pl.pallas_call(
        collect,
        out_shape=[shape(F32, 3, 64, seq)],
        in_specs=[smem, hbm],
        out_specs=[vmem],
        scratch_shapes=[pltpu.VMEM((3, half, 128), BF), pltpu.SemaphoreType.DMA((3,))],
    )(meta, mixed)
    grad_inputs, grad_qkv, grad_out, g1, b1, bo, g2, b2, bd, grad_qv, grad_b_up = pl.pallas_call(
        finish,
        out_shape=[shape(F32, 3, 64, seq), shape(F32, 2, 128, 192), shape(F32, 2, 64, 128)]
        + [shape(F32, 2, 64)] * 6
        + [shape(F32, 2, 128), shape(F32, 2, 256)],
        in_specs=[smem, hbm, vmem],
        out_specs=[vmem] * 11,
        scratch_shapes=[
            pltpu.VMEM((16, 256, 128), BF),
            pltpu.VMEM((16, 32, 128), BF),
            pltpu.VMEM((3, half, 128), BF),
            pltpu.SemaphoreType.DMA((5,)),
        ],
        compiler_params=pltpu.CompilerParams(vmem_limit_bytes=16 * 2**20),
    )(meta, last, summed(mixed[:, 512:768]))
    return (
        result.transpose(0, 2, 1),
        grad_inputs.transpose(0, 2, 1),
        g1,
        b1,
        grad_qkv[:, :, None, :],
        grad_qv[:, None, :],
        grad_out,
        bo,
        g2,
        b2,
        grad_up,
        grad_b_up,
        grad_down,
        bd,
    )


def solution(mesh):
    split = Mesh(mesh.devices.reshape(4, 2, 2, 4, 2), ("y", "xl", "xh", "z", "c"))
    gx = ("y", "xl")
    gy = ("xh", "z", "c")
    token = P(gx, None, gy)
    vector = P(None, gy)
    return jax.shard_map(
        shards,
        mesh=split,
        in_specs=(
            token,
            token,
            P(),
            vector,
            vector,
            P(None, gx, gy, None),
            P(None, gy, None),
            P(None, gy, gx),
            vector,
            vector,
            vector,
            P(None, gx, gy),
            vector,
            P(None, gy, gx),
            vector,
        ),
        out_specs=(
            token,
            token,
            vector,
            vector,
            P(None, gx, gy, None),
            P(None, gy, None),
            P(None, gy, gx),
            vector,
            vector,
            vector,
            P(None, gx, gy),
            vector,
            P(None, gy, gx),
            vector,
        ),
        check_vma=False,
    )
```

```python
import functools

import jax
import jax.numpy as jnp
from jax import lax
from jax.experimental import pallas as pl
from jax.experimental.pallas import tpu as pltpu
from jax.sharding import Mesh, PartitionSpec as P

EPS = 1e-06
BF = jnp.bfloat16
F32 = jnp.float32
DP = ("y", "xl", "xh")
SWAP = [(0, 1), (1, 0)]
PAIR_A = [(0, 1), (1, 0), (2, 3), (3, 2)]
PAIR_B = [(0, 3), (3, 0), (1, 2), (2, 1)]


def dot(a, b, ca, cb):
    return lax.dot_general(a, b, (((ca,), (cb,)), ((), ())), preferred_element_type=F32)


def core_swap(block):
    return lax.ppermute(block, "c", SWAP)


def ring_blocks(block):
    return [block] + [
        lax.ppermute(block, "z", [(i, (i + step) % 4) for i in range(4)]) for step in (1, 3, 2)
    ]


def total(mine, theirs, work=None, late=None):
    parts = (shape(BF, HALF, WIDTH // 2),) * 2
    left, right = run(add_cores, parts, (mine, core_swap(theirs)), 0)
    if work is not None:
        left, right, given = lax.optimization_barrier((left, right, work[1]))
    got_left = lax.ppermute(left, "z", PAIR_A)
    got_right = lax.ppermute(right, "z", PAIR_B)
    done = work[0](given) if work is not None else None
    left, right = run(add_pairs, parts, (left, got_left, right, got_right), 0)
    left, right, late, done = lax.optimization_barrier((left, right, late, done))
    got_left = lax.ppermute(left, "z", PAIR_B)
    got_right = lax.ppermute(right, "z", PAIR_A)
    return (left, got_left, right, got_right), done, late


def add_cores(mine, got, left, right):
    both = (mine[...] + got[...].astype(F32)).astype(BF)
    left[...] = both[:, : WIDTH // 2]
    right[...] = both[:, WIDTH // 2 :]


def add_pairs(left, got_left, right, got_right, left_out, right_out):
    left_out[...] = (left[...].astype(F32) + got_left[...].astype(F32)).astype(BF)
    right_out[...] = (right[...].astype(F32) + got_right[...].astype(F32)).astype(BF)


HALF = 112
ROWS = 2 * HALF
WIDTH = 1024


def run(
    kernel, outs, args, flops, scratch=(), smem=0, far=(), grant=16, mirrors=(), direct=False
):
    far = [f if isinstance(f, tuple) else (f, None, None) for f in far]
    size = sum(a.size * a.dtype.itemsize for a in args)
    size += sum(o.size * o.dtype.itemsize for o in outs)
    fetched = [f[0] for f in far]
    specs = [
        pl.BlockSpec(
            memory_space=pltpu.SMEM if i < smem else pltpu.HBM if i in fetched else pltpu.VMEM
        )
        for i in range(len(args))
    ]
    held = []
    for i, _, count in far:
        sizes = args[i].shape
        sizes = sizes if count is None else (sizes[0], count) + sizes[2:]
        held.append(pltpu.VMEM(sizes, args[i].dtype))
    more = [
        shape(args[m[0]].dtype, ROWS, WIDTH) if isinstance(m, tuple) else outs[m] for m in mirrors
    ]
    semaphores = [pltpu.SemaphoreType.DMA((max(len(far), 1),))]
    semaphores += [pltpu.SemaphoreType.DMA((max(2 * len(mirrors), 1),))]

    def body(*refs):
        refs = list(refs)
        n, m = len(args), len(outs)
        results, copied = refs[n : n + m], refs[n + m : n + m + len(mirrors)]
        rest = refs[n + m + len(mirrors) : -2]
        sems, out_sems = refs[-2:]
        spaces, rest = rest[len(rest) - len(far) :], rest[: len(rest) - len(far)]
        copies = []
        for k, (i, start, count) in enumerate(far):
            source = refs[i] if count is None else refs[i].at[:, start : start + count]
            copies.append(pltpu.make_async_copy(source, spaces[k], sems.at[k]))
            copies[-1].start()
        sent = {}

        def send(k):
            if isinstance(mirrors[k], tuple):
                sent[k] = [
                    pltpu.make_async_copy(
                        refs[i], copied[k].at[HALF * j : HALF * j + HALF], out_sems.at[2 * k + j]
                    )
                    for j, i in enumerate(mirrors[k])
                ]
            else:
                sent[k] = [
                    pltpu.make_async_copy(results[mirrors[k]], copied[k], out_sems.at[2 * k])
                ]
            for copy in sent[k]:
                copy.start()

        for k, mirror in enumerate(mirrors):
            if isinstance(mirror, tuple):
                send(k)
        for k, copy in enumerate(copies):
            copy.wait()
            refs[fetched[k]] = spaces[k]
        if mirrors:
            kernel(*refs[:n], *results, *rest, send=send)
        else:
            kernel(*refs[:n], *results, *rest)
        for k in range(len(mirrors)):
            if k not in sent:
                send(k)
        for group in sent.values():
            for copy in group:
                copy.wait()

    space = pltpu.HBM if direct else pltpu.VMEM
    return pl.pallas_call(
        body,
        out_shape=list(outs) + more,
        in_specs=specs,
        out_specs=[pl.BlockSpec(memory_space=space)] * len(outs)
        + [pl.BlockSpec(memory_space=pltpu.HBM)] * len(more),
        scratch_shapes=list(scratch) + held + semaphores,
        compiler_params=pltpu.CompilerParams(vmem_limit_bytes=grant * 2**20),
        cost_estimate=pl.CostEstimate(
            flops=int(flops), bytes_accessed=int(size), transcendentals=0
        ),
    )(*args)


def shape(dtype, *sizes):
    return jax.ShapeDtypeStruct(sizes, dtype)


def norm_parts(stream):
    center = stream - jnp.mean(stream, axis=-1, keepdims=True)
    factor = lax.rsqrt(jnp.mean(center * center, axis=-1, keepdims=True) + EPS)
    return center * factor, factor


def place_attention(w, w_qkv, w_out):
    for g in range(8):
        cols = slice(128 * g, 128 * g + 128)
        for i in range(2):
            w_qkv[128 * i : 128 * i + 128, cols] = w[2 * g + i, :128]
            w_qkv[256 + 64 * i : 320 + 64 * i, cols] = w[2 * g + i, 128:192]
            w_out[64 * i : 64 * i + 64, cols] = w[2 * g + i, 192:256]


def place_mlp(w, w_up, w_down):
    for g in range(8):
        rows = slice(128 * g, 128 * g + 128)
        for i in range(2):
            for j in range(2):
                at = 256 * i + 128 * j
                w_up[rows, at : at + 128] = w[2 * g + i, 128 * j : 128 * j + 128]
            w_down[256 * i : 256 * i + 256, rows] = w[2 * g + i, 256:512]


def both_rows(mine, other):
    return jnp.concatenate([mine[...], other[...]], axis=0)


def softmax(valid, query, key):
    scores = dot(query, key, 1, 1) * 64**-0.5
    at = lax.broadcasted_iota(jnp.int32, (1, ROWS), 1)
    limit = jnp.where(at < HALF, valid[4], valid[5] + HALF)
    scores = jnp.where(at < limit, scores, -1e30)
    exponent = jnp.exp(scores - jnp.max(scores, axis=-1, keepdims=True))
    return exponent / jnp.sum(exponent, axis=-1, keepdims=True)


def part_of(packed, name, i):
    start = {"q": 128 * i, "k": 128 * i + 64, "v": 256 + 64 * i}[name]
    return packed[:, start : start + 64]


def attention_forward(at, valid, mine, other, w, bias, packed_out, heads_out, out, away, w_qkv, w_out):
    place_attention(w, w_qkv, w_out)
    packed = dot(both_rows(mine, other), w_qkv[...], 1, 1) + bias[at, 0:1, :384]
    packed_out[...] = packed.astype(BF)
    heads = []
    for i in range(2):
        query, key, value = [part_of(packed, n, i).astype(BF) for n in "qkv"]
        probs = softmax(valid, query, key).astype(BF)
        heads.append(dot(probs, value, 1, 0))
    heads = jnp.concatenate(heads, axis=1).astype(BF)
    heads_out[...] = heads
    result = dot(heads, w_out[...], 1, 0)
    out[...] = result[:HALF]
    away[...] = result[HALF:].astype(BF)


def attention_backward(valid, mine, other, packed_in, w, grad_out, sums, out, away, w_qkv, w_out):
    place_attention(w, w_qkv, w_out)
    heads_grad = dot(both_rows(mine, other), w_out[...], 1, 1)
    packed = packed_in[...].astype(F32)
    parts = []
    values = []
    for i in range(2):
        query, key, value = [part_of(packed, n, i).astype(BF) for n in "qkv"]
        p = softmax(valid, query, key)
        upstream = heads_grad[:, 64 * i : 64 * i + 64].astype(BF)
        prob_grad = dot(upstream, value, 1, 1)
        values.append(dot(p.astype(BF), upstream, 0, 0))
        score_grad = (
            p * (prob_grad - jnp.sum(prob_grad * p, axis=-1, keepdims=True))
        ).astype(BF)
        parts.append(dot(score_grad, key, 1, 0) * 64**-0.5)
        parts.append(dot(score_grad, query, 0, 0) * 64**-0.5)
    grad = jnp.concatenate(parts + values, axis=1).astype(BF)
    grad_out[...] = grad
    sums[...] = jnp.sum(grad.astype(F32), axis=0, keepdims=True)
    result = dot(grad, w_qkv[...], 1, 0)
    out[...] = result[:HALF]
    away[...] = result[HALF:].astype(BF)


def attention_weights(h_mine, h_other, grad, heads, mine, other, rows_out, send):
    qkv = dot(grad[...], both_rows(h_mine, h_other), 0, 0).astype(BF)
    back = dot(heads[...], both_rows(mine, other), 0, 0).astype(BF)
    for g in range(8):
        cols = slice(128 * g, 128 * g + 128)
        for i in range(2):
            at = 2 * g + i
            rows_out[at, :128] = qkv[128 * i : 128 * i + 128, cols]
            rows_out[at, 128:192] = qkv[256 + 64 * i : 320 + 64 * i, cols]
            rows_out[at, 192:256] = back[64 * i : 64 * i + 64, cols]


def mlp_forward(at, mine, other, w, bias, act_out, slope_out, out, away, w_up, w_down):
    place_mlp(w, w_up, w_down)
    upper = dot(both_rows(mine, other), w_up[...], 1, 0) + bias[at, 1:2]
    phi = 0.5 * (1.0 + lax.erf(upper * 0.5**0.5))
    act = (upper * phi).astype(BF)
    act_out[...] = act
    slope_out[...] = phi + upper * (jnp.exp(-0.5 * upper * upper) * 0.3989422804014327)
    result = dot(act, w_down[...], 1, 0)
    out[...] = result[:HALF]
    away[...] = result[HALF:].astype(BF)


def mlp_backward(mine, other, w, slope, grad_out, sums, out, away, w_up, w_down):
    place_mlp(w, w_up, w_down)
    grad = (dot(both_rows(mine, other), w_down[...], 1, 1) * slope[...]).astype(BF)
    grad_out[...] = grad
    sums[...] = jnp.sum(grad.astype(F32), axis=0, keepdims=True)
    result = dot(grad, w_up[...], 1, 1)
    out[...] = result[:HALF]
    away[...] = result[HALF:].astype(BF)


def attention_weights_and_out(place, h_mine, h_other, grad, heads, mine, other, keep, got, rows_out, send):
    attention_weights(h_mine, h_other, grad, heads, mine, other, rows_out, send)
    tokens = owner_rows(place[1] == 0, keep, got)
    for g in range(8):
        for i in range(2):
            rows_out[2 * g + i, 256:] = tokens[i]


def mlp_weights(h_mine, h_other, grad, act, mine, other, rows_out, send):
    up = dot(both_rows(h_mine, h_other), grad[...], 0, 0).astype(BF)
    down = dot(act[...], both_rows(mine, other), 0, 0).astype(BF)
    for g in range(8):
        cols = slice(128 * g, 128 * g + 128)
        for i in range(2):
            for j in range(2):
                at = 256 * i + 128 * j
                rows_out[2 * g + i, 128 * j : 128 * j + 128] = up[cols, at : at + 128]
            rows_out[2 * g + i, 256:512] = down[256 * i : 256 * i + 256, cols]


def pair_sum(left, got_left, right, got_right):
    return jnp.concatenate(
        [
            left[...].astype(F32) + got_left[...].astype(F32),
            right[...].astype(F32) + got_right[...].astype(F32),
        ],
        axis=1,
    )


def ring_place(ring, blocks, store):
    for step, block in zip((0, 1, 3, 2), blocks):
        place = lax.rem(ring + 4 - step, 4) * 128
        for i in range(2):
            store(pl.ds(pl.multiple_of(512 * i + place, 128), 128), block, i)


def norm_first(ring, a, b, c, d, narrow, stream_out, out, wide_out, cotangent, sums, bias_out):
    def store(columns, block, i):
        stream_out[:, columns] = block[i, :HALF].astype(F32)
        for depth in range(2):
            rows = block[i, HALF + 16 * depth : HALF + 16 * depth + 16].astype(F32)
            wide_out[depth, :, columns] = rows[:8] + rows[8:]
        upstream = block[i, HALF + 32 :]
        cotangent[:, columns] = upstream
        sums[:, columns] = jnp.sum(upstream.astype(F32), axis=0, keepdims=True)

    ring_place(ring[0], (a, b, c, d), store)
    normed, _ = norm_parts(stream_out[...])
    out[...] = (normed * wide_out[0, 0:1] + wide_out[0, 1:2]).astype(BF)
    pieces = []
    for i in range(2):
        piece = narrow[i].astype(F32)
        pieces.append(piece[:8] + piece[8:])
    blank = jnp.zeros((1, 64), F32)
    for depth in range(2):
        qv = [piece[depth : depth + 1] for piece in pieces]
        bias_out[depth, 0:1] = jnp.concatenate(
            [qv[0][:, :64], blank, qv[1][:, :64], blank, qv[0][:, 64:], qv[1][:, 64:]]
            + [jnp.zeros((1, 128), F32)],
            axis=1,
        )
        bias_out[depth, 1:2] = jnp.concatenate(
            [piece[at : at + 1] for piece in pieces for at in (2 + 2 * depth, 3 + 2 * depth)],
            axis=1,
        )


def owner_lanes(source, ring, first_core, keep, give):
    parts = []
    for i in range(2):
        at = pl.multiple_of(512 * i + 128 * ring, 128)
        parts.append(source[:, pl.ds(at, 128)].astype(F32))
    lanes = [
        jnp.concatenate([parts[0][:, s], parts[1][:, s]], axis=1)
        for s in (slice(0, 64), slice(64, 128))
    ]
    keep[...] = jnp.where(first_core, lanes[0], lanes[1]).astype(keep.dtype)
    give[...] = jnp.where(first_core, lanes[1], lanes[0]).astype(give.dtype)


def owner_rows(first_core, keep, got):
    keep, got = keep[...].astype(F32), got[...].astype(F32)
    early, late = jnp.where(first_core, keep, got), jnp.where(first_core, got, keep)
    return [
        jnp.concatenate([early[:, s], late[:, s]], axis=1).astype(BF)
        for s in (slice(0, 64), slice(64, 128))
    ]


def owner_tokens(block, live):
    block = block.astype(F32)
    tokens = jnp.concatenate([block[:, :64], block[:, 64:]], axis=0)
    return jnp.where(live, tokens.T[:, :197], 0.0)


def norm_last(place, left, got_left, right, got_right, stream, wide, keep, give, new):
    new[...] = stream[...] + (pair_sum(left, got_left, right, got_right) + wide[1, 5:6])
    owner_lanes(new, place[0], place[1] == 0, keep, give)


def prepare(
    counts, inputs, cotangent, g1, b1, bo, g2, b2, bd, qv, up, w_qkv, w_out, out, turned, held, block, sems
):
    group = lax.axis_index(("y", "xl"))
    first = jnp.int32(0)
    for g in range(8):
        first = first + jnp.where(g < group, counts[g], 0)
    wide = [jnp.concatenate([v[0:1], v[1:2]], axis=1) for v in (g1, b1, bo, g2, b2, bd)]
    wide = jnp.concatenate(wide + [jnp.zeros((2, 128), F32)], axis=0)
    narrow = [qv[0], qv[1], up[0:1, :128], up[0:1, 128:], up[1:2, :128], up[1:2, 128:]]
    narrow = jnp.concatenate(narrow + [jnp.zeros((2, 128), F32)], axis=0)
    rows = []
    for v in (wide, narrow):
        high = v.astype(BF).astype(F32)
        rows += [high, v - high]
    block[:32] = jnp.concatenate(rows, axis=0).astype(BF)
    block[32:224] = w_qkv[0]
    block[224:288] = w_out[0]
    copies = [pltpu.make_async_copy(block, out.at[w, ROWS:512], sems.at[16 + w]) for w in range(16)]
    for copy in copies:
        copy.start()
    seq = inputs.shape[2]
    turned[...] = jnp.zeros(turned.shape, F32)
    for s in range(3):
        turned[:64, :seq] = inputs[s].astype(F32)
        turned[64:, :seq] = cotangent[s].astype(F32)
        held[s] = turned[...].T[:ROWS].astype(BF)
    for w in range(16):
        slot = jnp.clip(w - first, 0, 2)
        copies.append(pltpu.make_async_copy(held.at[slot], out.at[w, 0:ROWS], sems.at[w]))
        copies[-1].start()
    for copy in copies:
        copy.wait()


def prepare_next(w_qkv, w_out, w_up, w_down, out):
    for w in range(16):
        out[w, :128] = w_up[0, :, :128]
        out[w, 128:256] = w_up[0, :, 128:]
        out[w, 256:512] = w_down[0]
        out[w, 512:704] = w_qkv[1]
        out[w, 704:768] = w_out[1]


def prepare_mlp(w_up, w_down, out):
    for w in range(out.shape[0]):
        out[w, :128] = w_up[1, :, :128]
        out[w, 128:256] = w_up[1, :, 128:]
        out[w, 256:] = w_down[1]


def norm_forward(at, left, got_left, right, got_right, stream, wide, stream_out, out):
    shift, gain, bias = [wide[d, i : i + 1] for d, i in at]
    new = stream[...] + (pair_sum(left, got_left, right, got_right) + shift)
    stream_out[...] = new
    normed, _ = norm_parts(new)
    out[...] = (normed * gain + bias).astype(BF)


def norm_backward(at, left, got_left, right, got_right, stream, upstream, wide, grad_out, low_out, sums):
    grad = pair_sum(left, got_left, right, got_right)
    normed, factor = norm_parts(stream[...])
    scaled = grad * wide[at[0], at[1] : at[1] + 1]
    first = jnp.mean(scaled, axis=-1, keepdims=True)
    second = jnp.mean(scaled * normed, axis=-1, keepdims=True)
    new = upstream[...].astype(F32) + factor * (scaled - first - normed * second)
    grad_out[...] = new
    low = new.astype(BF)
    low_out[...] = low.astype(low_out.dtype)
    sums[0:1] = jnp.sum(grad * normed, axis=0, keepdims=True)
    sums[1:2] = jnp.sum(grad, axis=0, keepdims=True)
    sums[2:3] = jnp.sum(low.astype(F32), axis=0, keepdims=True)
    sums[3:8] = jnp.zeros((5, WIDTH), F32)


def norm_backward_last(
    place, left, got_left, right, got_right, stream, upstream, wide, s20, s11, s21, low_sum,
    keep, give, keep_v, give_v, new, sums, table,
):
    norm_backward((0, 0), left, got_left, right, got_right, stream, upstream, wide, new, new, sums)
    owner_lanes(new, place[0], place[1] == 0, keep, give)
    pieces = [sums[0:2], s20[2:3], s20[0:2], s11[2:3], s11[0:2], s21[2:3], s21[0:2], low_sum[...]]
    table[...] = jnp.concatenate(pieces + [jnp.zeros((4, WIDTH), F32)], axis=0)
    owner_lanes(table, place[0], place[1] == 0, keep_v, give_v)


def final_rows(place, rows_in, keep, got, keep_v, got_v, p0, p1, u0, u1, out, held, sem):
    wide = keep_v[...] + got_v[...]
    high = wide.astype(BF).astype(F32)
    low = wide - high
    tokens = owner_rows(place[1] == 0, keep, got)
    for i in range(2):
        part = slice(64 * i, 64 * i + 64)
        narrow = [
            jnp.concatenate(
                [p[:, 128 * i : 128 * i + 64], p[:, 256 + 64 * i : 320 + 64 * i]], axis=1
            )
            for p in (p0, p1)
        ]
        for u in (u0, u1):
            narrow += [u[:, 256 * i : 256 * i + 128], u[:, 256 * i + 128 : 256 * i + 256]]
        narrow = jnp.concatenate(narrow + [jnp.zeros((2, 128), F32)], axis=0)
        narrow_high = narrow.astype(BF).astype(F32)
        rows = jnp.concatenate(
            [jnp.concatenate([high[:, part], low[:, part]], axis=1), narrow_high, narrow - narrow_high],
            axis=0,
        ).astype(BF)
        for g in range(8):
            held[2 * g + i, :HALF] = tokens[i]
            held[2 * g + i, HALF:] = rows
    copy = pltpu.make_async_copy(held, out.at[:, 256:400], sem)
    copy.start()
    copy.wait()


def collect(meta, received, out, held, sems):
    copies = []
    for s in range(3):
        at = jnp.minimum(meta[2] + s, 15)
        copies.append(
            pltpu.make_async_copy(received.at[at, 256:368], held.at[s], sems.at[s])
        )
        copies[-1].start()
    for s in range(3):
        copies[s].wait()
        out[s] = owner_tokens(held[s], s < meta[3])


def finish(meta, received, sum_1, out, qkv, w_out, g1, b1, bo, g2, b2, bd, qv, up, weights, vectors, held, sems):
    copies = [
        pltpu.make_async_copy(received.at[:, 0:256], weights, sems.at[3]),
        pltpu.make_async_copy(received.at[:, 368:400], vectors, sems.at[4]),
    ]
    for s in range(3):
        at = jnp.minimum(meta[2] + s, 15)
        copies.append(
            pltpu.make_async_copy(received.at[at, 256:368], held.at[s], sems.at[s])
        )
    for copy in copies:
        copy.start()
    for copy in copies:
        copy.wait()
    for s in range(3):
        out[s] = owner_tokens(held[s], s < meta[3])
    total_v = jnp.sum(vectors[...].astype(F32), axis=0)
    wide = total_v[:16, :64] + total_v[:16, 64:]
    for v, ref in enumerate((g1, b1, bo, g2, b2, bd)):
        ref[...] = jnp.concatenate([wide[v : v + 1], wide[v + 6 : v + 7]], axis=0)
    narrow = total_v[16:24] + total_v[24:32]
    qv[...] = narrow[0:2]
    for d in range(2):
        up[d : d + 1] = jnp.concatenate([narrow[2 + 2 * d : 3 + 2 * d], narrow[3 + 2 * d : 4 + 2 * d]], axis=1)
    for d in range(2):
        block = jnp.sum(weights[...].astype(F32), axis=0) if d == 0 else sum_1[...]
        qkv[d] = block[:192]
        w_out[d] = block[192:256]


ATTENTION_SCRATCH = (pltpu.VMEM((384, WIDTH), BF), pltpu.VMEM((128, WIDTH), BF))
MLP_SCRATCH = (pltpu.VMEM((WIDTH, 512), BF), pltpu.VMEM((512, WIDTH), BF))
SUM_SHAPES = (shape(F32, HALF, WIDTH), shape(BF, HALF, WIDTH))
NORM_SHAPES = (shape(F32, HALF, WIDTH), shape(BF, HALF, WIDTH))
ATTENTION_FLOPS = 2 * ROWS * WIDTH * 512
MLP_FLOPS = 2 * ROWS * WIDTH * 1024


def exchange(chunks):
    return lax.all_to_all(chunks, DP, 0, 0)


def shards(
    inputs,
    cotangent,
    group_images,
    ln1_gain,
    ln1_bias,
    w_qkv,
    b_qv,
    w_out,
    b_out,
    ln2_gain,
    ln2_bias,
    w_up,
    b_up,
    w_down,
    b_down,
):
    seq = inputs.shape[1]
    half, rows = HALF, ROWS
    core = lax.axis_index("c")
    ring = lax.axis_index("z")
    group = lax.axis_index(("y", "xl"))
    worker = lax.axis_index(DP)
    first_core = core == 0

    earlier = jnp.arange(8)[:, None] > jnp.arange(8)[None, :]
    offsets = jnp.sum(jnp.where(earlier, group_images[None, :], 0), axis=1)
    my_offset = jnp.sum(jnp.where(jnp.arange(8) < group, group_images, 0))
    my_live = jnp.sum(jnp.where(jnp.arange(8) == group, group_images, 0))
    source = jnp.sum((offsets <= worker).astype(jnp.int32)) - 1
    mine_valid = jnp.where(first_core, half, seq - half)
    place = jnp.stack([ring, core, my_offset, my_live, mine_valid, seq - mine_valid])
    place = place.astype(jnp.int32)

    w_qkv = w_qkv.transpose(0, 2, 3, 1).reshape(2, 192, 128)
    (chunks,) = run(
        prepare,
        (shape(BF, 16, 512, 128),),
        (group_images, inputs.transpose(0, 2, 1), cotangent.transpose(0, 2, 1))
        + (ln1_gain, ln1_bias, b_out, ln2_gain, ln2_bias, b_down, b_qv, b_up, w_qkv, w_out),
        0,
        (
            pltpu.VMEM((128, 256), F32),
            pltpu.VMEM((3, rows, 128), BF),
            pltpu.VMEM((288, 128), BF),
            pltpu.SemaphoreType.DMA((32,)),
        ),
        1,
        range(1, 13),
        56,
        (),
        True,
    )
    arrived = exchange(chunks)
    (next_rows,) = run(
        prepare_next, (shape(BF, 16, 768, 128),), (w_qkv, w_out, w_up, w_down), 0
    )
    (mlp_rows_1,) = run(prepare_mlp, (shape(BF, 16, 512, 128),), (w_up, w_down), 0)
    next_rows, mlp_rows_1, arrived, place = lax.optimization_barrier(
        (next_rows, mlp_rows_1, arrived, place)
    )

    picked = lax.dynamic_slice(arrived, (2 * source, 0, 0), (2, rows, 128))
    vectors_here = arrived[:2, rows:256]
    low_part, high_part = picked[:, :half], picked[:, half:rows]
    tail = vectors_here[:, :16]
    keep = jnp.concatenate([jnp.where(first_core, low_part, high_part), tail], axis=1)
    give = jnp.concatenate([jnp.where(first_core, high_part, low_part), tail], axis=1)
    got = core_swap(give)
    part_0 = jnp.where(first_core, keep, got)
    part_1 = jnp.where(first_core, got, keep)
    left = jnp.concatenate([part_0[..., :64], part_1[..., :64]], axis=-1)
    right = jnp.concatenate([part_0[..., 64:], part_1[..., 64:]], axis=-1)
    blocks = ring_blocks(jnp.concatenate([left, right[:, half:], right[:, :half]], axis=1))
    following = exchange(next_rows)
    mlp_w = [following, None]
    attention_w = [arrived, following]
    attention_at = [256, 512]
    stream, h1, wide, cotangent_low, low_sum, bias = run(
        norm_first,
        NORM_SHAPES
        + (shape(F32, 2, 8, WIDTH), shape(BF, half, WIDTH), shape(F32, 1, WIDTH))
        + (shape(F32, 2, 2, 512),),
        [place] + blocks + [vectors_here[:, 16:]],
        0,
        (),
        1,
    )
    kept = []
    for d in range(2):
        h1_other = core_swap(h1)
        packed, heads, mine, theirs = run(
            functools.partial(attention_forward, d),
            (shape(BF, ROWS, 384), shape(BF, ROWS, 128)) + SUM_SHAPES,
            (place, h1, h1_other, attention_w[d], bias),
            ATTENTION_FLOPS,
            ATTENTION_SCRATCH,
            1,
            ((3, attention_at[d], 256),),
        )
        pairs, _, done = total(mine, theirs, None, mlp_w[1])
        mlp_w[1] = done
        middle, h2 = run(
            functools.partial(norm_forward, ((d, 2), (d, 3), (d, 4))),
            NORM_SHAPES,
            pairs + (stream, wide),
            0,
        )
        h2_other = core_swap(h2)
        act, slope, mine, theirs = run(
            functools.partial(mlp_forward, d),
            (shape(BF, ROWS, 512), shape(F32, ROWS, 512)) + SUM_SHAPES,
            (h2, h2_other, mlp_w[d], bias),
            MLP_FLOPS,
            MLP_SCRATCH,
            0,
            ((2, 0, 512),),
        )
        kept.append((stream, h1, h1_other, packed, heads, middle, h2, h2_other, act, slope))
        if d == 0:
            pairs, _, _ = total(mine, theirs)
            mlp_rows_1, _ = lax.optimization_barrier((mlp_rows_1, act))
            mlp_w[1] = exchange(mlp_rows_1)
            stream, h1 = run(
                functools.partial(norm_forward, ((0, 5), (1, 0), (1, 1))),
                NORM_SHAPES,
                pairs + (middle, wide),
                0,
            )
    grad_low = cotangent_low
    low_other = core_swap(grad_low)
    pairs, _, _ = total(mine, theirs)
    keep, give = run(
        norm_last,
        (shape(BF, half, 128), shape(BF, half, 128)),
        (place,) + pairs + (middle, wide),
        0,
        (pltpu.VMEM((half, WIDTH), F32),),
        1,
    )
    out_keep, out_got = keep, core_swap(give)

    grad_stream = cotangent_low
    previous = mlp_got = None
    sums, narrow_sums = {}, {}
    for d in (1, 0):
        start, h1, h1_other, packed, heads, middle, h2, h2_other, act, slope = kept[d]
        if d == 0:
            low_other = core_swap(grad_low)
            attention_grad, _ = lax.optimization_barrier((attention_grad, mlp_got))
            mixed = exchange(attention_grad)
        upper_grad, up_sum, mine, theirs = run(
            mlp_backward,
            (shape(BF, ROWS, 512), shape(F32, 1, 512)) + SUM_SHAPES,
            (grad_low, low_other, mlp_w[d], slope),
            MLP_FLOPS,
            MLP_SCRATCH,
            0,
            ((2, 0, 512),),
        )

        def mlp_work(upper_grad):
            args = (h2, h2_other, upper_grad, act, grad_low, low_other)
            return run(
                mlp_weights,
                (shape(BF, 16, 512, 128),),
                args,
                MLP_FLOPS,
                mirrors=(0,),
            )[1]

        pairs, mlp_grad, _ = total(mine, theirs, (mlp_work, upper_grad))
        if d == 0:
            mlp_grad, mixed = lax.optimization_barrier((mlp_grad, mixed))
        previous = exchange(mlp_grad)
        grad_stream, grad_low, sums[2, d] = run(
            functools.partial(norm_backward, (d, 3)),
            NORM_SHAPES + (shape(F32, 8, WIDTH),),
            pairs + (middle, grad_stream, wide),
            0,
        )
        low_other = core_swap(grad_low)
        packed_grad, packed_sum, mine, theirs = run(
            attention_backward,
            (shape(BF, ROWS, 384), shape(F32, 1, 384)) + SUM_SHAPES,
            (place, grad_low, low_other, packed, attention_w[d]),
            ATTENTION_FLOPS,
            ATTENTION_SCRATCH,
            1,
            ((4, attention_at[d], 256),),
        )
        narrow_sums[d] = (packed_sum, up_sum)

        def attention_work(packed_grad):
            args = (h1, h1_other, packed_grad, heads, grad_low, low_other)
            if d == 1:
                return run(
                    attention_weights_and_out,
                    (shape(BF, 16, 368, 128),),
                    (place,) + args + (out_keep, out_got),
                    ATTENTION_FLOPS,
                    smem=1,
                    mirrors=(0,),
                )[1]
            return run(
                attention_weights,
                (shape(BF, 16, 400, 128),),
                args,
                ATTENTION_FLOPS,
                mirrors=(0,),
            )[1]

        pairs, attention_grad, mlp_done = total(
            mine, theirs, (attention_work, packed_grad), previous if d == 1 else None
        )
        if d == 1:
            mlp_got = mlp_done
        if d == 1:
            grad_stream, grad_low, sums[1, d] = run(
                functools.partial(norm_backward, (d, 0)),
                NORM_SHAPES + (shape(F32, 8, WIDTH),),
                pairs + (start, grad_stream, wide),
                0,
            )
    keep, give, keep_v, give_v = run(
        norm_backward_last,
        (shape(BF, half, 128), shape(BF, half, 128), shape(F32, 16, 128), shape(F32, 16, 128)),
        (place,) + pairs + (start, grad_stream, wide, sums[2, 0], sums[1, 1], sums[2, 1], low_sum),
        0,
        (pltpu.VMEM((half, WIDTH), F32), pltpu.VMEM((8, WIDTH), F32), pltpu.VMEM((16, WIDTH), F32)),
        1,
    )
    (last_rows,) = pl.pallas_call(
        final_rows,
        out_shape=[shape(BF, 16, 400, 128)],
        in_specs=[pl.BlockSpec(memory_space=pltpu.SMEM), pl.BlockSpec(memory_space=pltpu.HBM)]
        + [pl.BlockSpec(memory_space=pltpu.VMEM)] * 8,
        out_specs=[pl.BlockSpec(memory_space=pltpu.HBM)],
        scratch_shapes=[pltpu.VMEM((16, 144, 128), BF), pltpu.SemaphoreType.DMA(())],
        input_output_aliases={1: 0},
        compiler_params=pltpu.CompilerParams(vmem_limit_bytes=56 * 2**20),
    )(
        place,
        attention_grad,
        keep,
        core_swap(give),
        keep_v,
        core_swap(give_v),
        narrow_sums[0][0],
        narrow_sums[1][0],
        narrow_sums[0][1],
        narrow_sums[1][1],
    )
    last_rows, previous = lax.optimization_barrier((last_rows, previous))
    last = exchange(last_rows)
    mixed, previous, mlp_got, _ = lax.optimization_barrier((mixed, previous, mlp_got, last_rows))

    def summed(block):
        return jnp.sum(block.astype(F32), axis=0)

    mlp = [summed(previous), summed(mlp_got)]
    grad_up = jnp.stack([jnp.concatenate([m[:128], m[128:256]], axis=-1) for m in mlp])
    grad_down = jnp.stack([m[256:] for m in mlp])
    hbm, vmem = pl.BlockSpec(memory_space=pltpu.HBM), pl.BlockSpec(memory_space=pltpu.VMEM)
    smem = pl.BlockSpec(memory_space=pltpu.SMEM)
    (result,) = pl.pallas_call(
        collect,
        out_shape=[shape(F32, 3, 64, seq)],
        in_specs=[smem, hbm],
        out_specs=[vmem],
        scratch_shapes=[pltpu.VMEM((3, half, 128), BF), pltpu.SemaphoreType.DMA((3,))],
    )(place, mixed)
    grad_inputs, grad_qkv, grad_out, g1, b1, bo, g2, b2, bd, grad_qv, grad_b_up = pl.pallas_call(
        finish,
        out_shape=[shape(F32, 3, 64, seq), shape(F32, 2, 192, 128), shape(F32, 2, 64, 128)]
        + [shape(F32, 2, 64)] * 6
        + [shape(F32, 2, 128), shape(F32, 2, 256)],
        in_specs=[smem, hbm, vmem],
        out_specs=[vmem] * 11,
        scratch_shapes=[
            pltpu.VMEM((16, 256, 128), BF),
            pltpu.VMEM((16, 32, 128), BF),
            pltpu.VMEM((3, half, 128), BF),
            pltpu.SemaphoreType.DMA((5,)),
        ],
        compiler_params=pltpu.CompilerParams(vmem_limit_bytes=16 * 2**20),
    )(place, last, summed(mixed[:, :256]))
    return (
        result.transpose(0, 2, 1),
        grad_inputs.transpose(0, 2, 1),
        g1,
        b1,
        grad_qkv[:, None].transpose(0, 3, 1, 2),
        grad_qv[:, None, :],
        grad_out,
        bo,
        g2,
        b2,
        grad_up,
        grad_b_up,
        grad_down,
        bd,
    )


def solution(mesh):
    split = Mesh(mesh.devices.reshape(4, 2, 2, 4, 2), ("y", "xl", "xh", "z", "c"))
    gx = ("y", "xl")
    gy = ("xh", "z", "c")
    token = P(gx, None, gy)
    vector = P(None, gy)
    return jax.shard_map(
        shards,
        mesh=split,
        in_specs=(
            token,
            token,
            P(),
            vector,
            vector,
            P(None, gx, gy, None),
            P(None, gy, None),
            P(None, gy, gx),
            vector,
            vector,
            vector,
            P(None, gx, gy),
            vector,
            P(None, gy, gx),
            vector,
        ),
        out_specs=(
            token,
            token,
            vector,
            vector,
            P(None, gx, gy, None),
            P(None, gy, None),
            P(None, gy, gx),
            vector,
            vector,
            vector,
            P(None, gx, gy),
            vector,
            P(None, gy, gx),
            vector,
        ),
        check_vma=False,
    )
```

```python
import functools

import jax
import jax.numpy as jnp
from jax import lax
from jax.experimental import pallas as pl
from jax.experimental.pallas import tpu as pltpu
from jax.sharding import Mesh, PartitionSpec as P

EPS = 1e-06
BF = jnp.bfloat16
F32 = jnp.float32
DP = ("y", "xl", "xh")
SWAP = [(0, 1), (1, 0)]
PAIR_A = [(0, 1), (1, 0), (2, 3), (3, 2)]
PAIR_B = [(0, 3), (3, 0), (1, 2), (2, 1)]


def dot(a, b, ca, cb):
    return lax.dot_general(a, b, (((ca,), (cb,)), ((), ())), preferred_element_type=F32)


def core_swap(block):
    return lax.ppermute(block, "c", SWAP)


def ring_blocks(block):
    return [block] + [
        lax.ppermute(block, "z", [(i, (i + step) % 4) for i in range(4)]) for step in (1, 3, 2)
    ]


def total(mine, theirs, work=None, late=None):
    parts = (shape(BF, HALF, mine.shape[1] // 2),) * 2
    left, right = run(add_cores, parts, (mine, core_swap(theirs)), 0)
    if work is not None:
        left, right, given = lax.optimization_barrier((left, right, work[1]))
    got_left = lax.ppermute(left, "z", PAIR_A)
    got_right = lax.ppermute(right, "z", PAIR_B)
    done = work[0](given) if work is not None else None
    left, right = run(add_pairs, parts, (left, got_left, right, got_right), 0)
    left, right, late, done = lax.optimization_barrier((left, right, late, done))
    got_left = lax.ppermute(left, "z", PAIR_B)
    got_right = lax.ppermute(right, "z", PAIR_A)
    return (left, got_left, right, got_right), done, late


def add_cores(mine, got, left, right):
    both = (mine[...] + got[...].astype(F32)).astype(BF)
    cut = mine.shape[1] // 2
    left[...] = both[:, :cut]
    right[...] = both[:, cut:]


def add_pairs(left, got_left, right, got_right, left_out, right_out):
    left_out[...] = (left[...].astype(F32) + got_left[...].astype(F32)).astype(BF)
    right_out[...] = (right[...].astype(F32) + got_right[...].astype(F32)).astype(BF)


HALF = 112
ROWS = 2 * HALF
WIDTH = 1024


def run(
    kernel, outs, args, flops, scratch=(), smem=0, far=(), grant=16, mirrors=(), direct=False
):
    far = [f if isinstance(f, tuple) else (f, None, None) for f in far]
    size = sum(a.size * a.dtype.itemsize for a in args)
    size += sum(o.size * o.dtype.itemsize for o in outs)
    fetched = [f[0] for f in far]
    specs = [
        pl.BlockSpec(
            memory_space=pltpu.SMEM if i < smem else pltpu.HBM if i in fetched else pltpu.VMEM
        )
        for i in range(len(args))
    ]
    held = []
    for i, _, count in far:
        sizes = args[i].shape
        sizes = sizes if count is None else (sizes[0], count) + sizes[2:]
        held.append(pltpu.VMEM(sizes, args[i].dtype))
    more = [
        shape(args[m[0]].dtype, ROWS, WIDTH) if isinstance(m, tuple) else outs[m] for m in mirrors
    ]
    semaphores = [pltpu.SemaphoreType.DMA((max(len(far), 1),))]
    semaphores += [pltpu.SemaphoreType.DMA((max(2 * len(mirrors), 1),))]

    def body(*refs):
        refs = list(refs)
        n, m = len(args), len(outs)
        results, copied = refs[n : n + m], refs[n + m : n + m + len(mirrors)]
        rest = refs[n + m + len(mirrors) : -2]
        sems, out_sems = refs[-2:]
        spaces, rest = rest[len(rest) - len(far) :], rest[: len(rest) - len(far)]
        copies = []
        for k, (i, start, count) in enumerate(far):
            source = refs[i] if count is None else refs[i].at[:, start : start + count]
            copies.append(pltpu.make_async_copy(source, spaces[k], sems.at[k]))
            copies[-1].start()
        sent = {}

        def send(k):
            if isinstance(mirrors[k], tuple):
                sent[k] = [
                    pltpu.make_async_copy(
                        refs[i], copied[k].at[HALF * j : HALF * j + HALF], out_sems.at[2 * k + j]
                    )
                    for j, i in enumerate(mirrors[k])
                ]
            else:
                sent[k] = [
                    pltpu.make_async_copy(results[mirrors[k]], copied[k], out_sems.at[2 * k])
                ]
            for copy in sent[k]:
                copy.start()

        for k, mirror in enumerate(mirrors):
            if isinstance(mirror, tuple):
                send(k)
        for k, copy in enumerate(copies):
            copy.wait()
            refs[fetched[k]] = spaces[k]
        if mirrors:
            kernel(*refs[:n], *results, *rest, send=send)
        else:
            kernel(*refs[:n], *results, *rest)
        for k in range(len(mirrors)):
            if k not in sent:
                send(k)
        for group in sent.values():
            for copy in group:
                copy.wait()

    space = pltpu.HBM if direct else pltpu.VMEM
    return pl.pallas_call(
        body,
        out_shape=list(outs) + more,
        in_specs=specs,
        out_specs=[pl.BlockSpec(memory_space=space)] * len(outs)
        + [pl.BlockSpec(memory_space=pltpu.HBM)] * len(more),
        scratch_shapes=list(scratch) + held + semaphores,
        compiler_params=pltpu.CompilerParams(vmem_limit_bytes=grant * 2**20),
        cost_estimate=pl.CostEstimate(
            flops=int(flops), bytes_accessed=int(size), transcendentals=0
        ),
    )(*args)


def shape(dtype, *sizes):
    return jax.ShapeDtypeStruct(sizes, dtype)


def norm_parts(stream):
    center = stream - jnp.mean(stream, axis=-1, keepdims=True)
    factor = lax.rsqrt(jnp.mean(center * center, axis=-1, keepdims=True) + EPS)
    return center * factor, factor


def place_attention(w, w_qkv, w_out):
    for g in range(8):
        cols = slice(128 * g, 128 * g + 128)
        for i in range(2):
            w_qkv[128 * i : 128 * i + 128, cols] = w[2 * g + i, :128]
            w_qkv[256 + 64 * i : 320 + 64 * i, cols] = w[2 * g + i, 128:192]
            w_out[64 * i : 64 * i + 64, cols] = w[2 * g + i, 192:256]


def place_mlp(w, w_up, w_down):
    for g in range(8):
        rows = slice(128 * g, 128 * g + 128)
        for i in range(2):
            for j in range(2):
                at = 256 * i + 128 * j
                w_up[rows, at : at + 128] = w[2 * g + i, 128 * j : 128 * j + 128]
            w_down[256 * i : 256 * i + 256, rows] = w[2 * g + i, 256:512]


def both_rows(mine, other):
    return jnp.concatenate([mine[...], other[...]], axis=0)


def softmax(valid, query, key):
    scores = dot(query, key, 1, 1) * 64**-0.5
    at = lax.broadcasted_iota(jnp.int32, (1, ROWS), 1)
    limit = jnp.where(at < HALF, valid[4], valid[5] + HALF)
    scores = jnp.where(at < limit, scores, -1e30)
    exponent = jnp.exp(scores - jnp.max(scores, axis=-1, keepdims=True))
    return exponent / jnp.sum(exponent, axis=-1, keepdims=True)


def part_of(packed, name, i):
    start = {"q": 128 * i, "k": 128 * i + 64, "v": 256 + 64 * i}[name]
    return packed[:, start : start + 64]


def attention_forward(at, valid, mine, other, w, bias, packed_out, heads_out, out, away, w_qkv, w_out):
    place_attention(w, w_qkv, w_out)
    packed = dot(both_rows(mine, other), w_qkv[...], 1, 1) + bias[at, 0:1, :384]
    packed_out[...] = packed.astype(BF)
    heads = []
    for i in range(2):
        query, key, value = [part_of(packed, n, i).astype(BF) for n in "qkv"]
        probs = softmax(valid, query, key).astype(BF)
        heads.append(dot(probs, value, 1, 0))
    heads = jnp.concatenate(heads, axis=1).astype(BF)
    heads_out[...] = heads
    result = dot(heads, w_out[...], 1, 0)
    out[...] = result[:HALF]
    away[...] = result[HALF:].astype(BF)


def attention_backward(valid, mine, other, packed_in, w, grad_out, sums, out, away, w_qkv, w_out):
    place_attention(w, w_qkv, w_out)
    heads_grad = dot(both_rows(mine, other), w_out[...], 1, 1)
    packed = packed_in[...].astype(F32)
    parts = []
    values = []
    for i in range(2):
        query, key, value = [part_of(packed, n, i).astype(BF) for n in "qkv"]
        p = softmax(valid, query, key)
        upstream = heads_grad[:, 64 * i : 64 * i + 64].astype(BF)
        prob_grad = dot(upstream, value, 1, 1)
        values.append(dot(p.astype(BF), upstream, 0, 0))
        score_grad = (
            p * (prob_grad - jnp.sum(prob_grad * p, axis=-1, keepdims=True))
        ).astype(BF)
        parts.append(dot(score_grad, key, 1, 0) * 64**-0.5)
        parts.append(dot(score_grad, query, 0, 0) * 64**-0.5)
    grad = jnp.concatenate(parts + values, axis=1).astype(BF)
    grad_out[...] = grad
    sums[...] = jnp.sum(grad.astype(F32), axis=0, keepdims=True)
    result = dot(grad, w_qkv[...], 1, 0)
    out[...] = result[:HALF]
    away[...] = result[HALF:].astype(BF)


def attention_weights(h_mine, h_other, grad, heads, mine, other, rows_out, send):
    qkv = dot(grad[...], both_rows(h_mine, h_other), 0, 0).astype(BF)
    back = dot(heads[...], both_rows(mine, other), 0, 0).astype(BF)
    for g in range(8):
        cols = slice(128 * g, 128 * g + 128)
        for i in range(2):
            at = 2 * g + i
            rows_out[at, :128] = qkv[128 * i : 128 * i + 128, cols]
            rows_out[at, 128:192] = qkv[256 + 64 * i : 320 + 64 * i, cols]
            rows_out[at, 192:256] = back[64 * i : 64 * i + 64, cols]


def mlp_forward(at, mine, other, w, bias, act_out, slope_out, out, away, w_up, w_down):
    place_mlp(w, w_up, w_down)
    upper = dot(both_rows(mine, other), w_up[...], 1, 0) + bias[at, 1:2]
    phi = 0.5 * (1.0 + lax.erf(upper * 0.5**0.5))
    act = (upper * phi).astype(BF)
    act_out[...] = act
    slope_out[...] = phi + upper * (jnp.exp(-0.5 * upper * upper) * 0.3989422804014327)
    result = dot(act, w_down[...], 1, 0)
    out[...] = result[:HALF]
    away[...] = result[HALF:].astype(BF)


def mlp_backward(mine, other, w, slope, grad_out, sums, out, away, w_up, w_down):
    place_mlp(w, w_up, w_down)
    grad = (dot(both_rows(mine, other), w_down[...], 1, 1) * slope[...]).astype(BF)
    grad_out[...] = grad
    sums[...] = jnp.sum(grad.astype(F32), axis=0, keepdims=True)
    result = dot(grad, w_up[...], 1, 1)
    out[...] = result[:HALF]
    away[...] = result[HALF:].astype(BF)


def mlp_backward_and_out(
    mine, other, w, slope, f_mine, f_theirs, grad_out, sums, out, away, w_up, w_down
):
    mlp_backward(
        mine, other, w, slope, grad_out, sums, out.at[:, :WIDTH], away.at[:, :WIDTH], w_up, w_down
    )
    out[:, WIDTH:] = f_mine[...]
    away[:, WIDTH:] = f_theirs[...]


def attention_weights_and_out(place, h_mine, h_other, grad, heads, mine, other, keep, got, rows_out, send):
    attention_weights(h_mine, h_other, grad, heads, mine, other, rows_out, send)
    tokens = owner_rows(place[1] == 0, keep, got)
    for g in range(8):
        for i in range(2):
            rows_out[2 * g + i, 256:] = tokens[i]


def mlp_weights(h_mine, h_other, grad, act, mine, other, rows_out, send):
    up = dot(both_rows(h_mine, h_other), grad[...], 0, 0).astype(BF)
    down = dot(act[...], both_rows(mine, other), 0, 0).astype(BF)
    for g in range(8):
        cols = slice(128 * g, 128 * g + 128)
        for i in range(2):
            for j in range(2):
                at = 256 * i + 128 * j
                rows_out[2 * g + i, 128 * j : 128 * j + 128] = up[cols, at : at + 128]
            rows_out[2 * g + i, 256:512] = down[256 * i : 256 * i + 256, cols]


def pair_sum(left, got_left, right, got_right):
    return jnp.concatenate(
        [
            left[...].astype(F32) + got_left[...].astype(F32),
            right[...].astype(F32) + got_right[...].astype(F32),
        ],
        axis=1,
    )


def ring_place(ring, blocks, store):
    for step, block in zip((0, 1, 3, 2), blocks):
        place = lax.rem(ring + 4 - step, 4) * 128
        for i in range(2):
            store(pl.ds(pl.multiple_of(512 * i + place, 128), 128), block, i)


def norm_first(ring, a, b, c, d, narrow, stream_out, out, wide_out, cotangent, sums, bias_out):
    def store(columns, block, i):
        stream_out[:, columns] = block[i, :HALF].astype(F32)
        for depth in range(2):
            rows = block[i, HALF + 16 * depth : HALF + 16 * depth + 16].astype(F32)
            wide_out[depth, :, columns] = rows[:8] + rows[8:]
        upstream = block[i, HALF + 32 :]
        cotangent[:, columns] = upstream
        sums[:, columns] = jnp.sum(upstream.astype(F32), axis=0, keepdims=True)

    ring_place(ring[0], (a, b, c, d), store)
    normed, _ = norm_parts(stream_out[...])
    out[...] = (normed * wide_out[0, 0:1] + wide_out[0, 1:2]).astype(BF)
    pieces = []
    for i in range(2):
        piece = narrow[i].astype(F32)
        pieces.append(piece[:8] + piece[8:])
    blank = jnp.zeros((1, 64), F32)
    for depth in range(2):
        qv = [piece[depth : depth + 1] for piece in pieces]
        bias_out[depth, 0:1] = jnp.concatenate(
            [qv[0][:, :64], blank, qv[1][:, :64], blank, qv[0][:, 64:], qv[1][:, 64:]]
            + [jnp.zeros((1, 128), F32)],
            axis=1,
        )
        bias_out[depth, 1:2] = jnp.concatenate(
            [piece[at : at + 1] for piece in pieces for at in (2 + 2 * depth, 3 + 2 * depth)],
            axis=1,
        )


def owner_lanes(source, ring, first_core, keep, give):
    parts = []
    for i in range(2):
        at = pl.multiple_of(512 * i + 128 * ring, 128)
        parts.append(source[:, pl.ds(at, 128)].astype(F32))
    lanes = [
        jnp.concatenate([parts[0][:, s], parts[1][:, s]], axis=1)
        for s in (slice(0, 64), slice(64, 128))
    ]
    keep[...] = jnp.where(first_core, lanes[0], lanes[1]).astype(keep.dtype)
    give[...] = jnp.where(first_core, lanes[1], lanes[0]).astype(give.dtype)


def owner_rows(first_core, keep, got):
    keep, got = keep[...].astype(F32), got[...].astype(F32)
    early, late = jnp.where(first_core, keep, got), jnp.where(first_core, got, keep)
    return [
        jnp.concatenate([early[:, s], late[:, s]], axis=1).astype(BF)
        for s in (slice(0, 64), slice(64, 128))
    ]


def owner_tokens(block, live):
    block = block.astype(F32)
    tokens = jnp.concatenate([block[:, :64], block[:, 64:]], axis=0)
    return jnp.where(live, tokens.T[:, :197], 0.0)


def norm_last(place, part, got, stream, wide, keep, give, new):
    new[...] = stream[...] + (part[...].astype(F32) + got[...].astype(F32) + wide[1, 5:6])
    owner_lanes(new, place[0], place[1] == 0, keep, give)


def prepare(
    counts, inputs, cotangent, g1, b1, bo, g2, b2, bd, qv, up, w_qkv, w_out, out, turned, held, block, sems
):
    group = lax.axis_index(("y", "xl"))
    first = jnp.int32(0)
    for g in range(8):
        first = first + jnp.where(g < group, counts[g], 0)
    wide = [jnp.concatenate([v[0:1], v[1:2]], axis=1) for v in (g1, b1, bo, g2, b2, bd)]
    wide = jnp.concatenate(wide + [jnp.zeros((2, 128), F32)], axis=0)
    narrow = [qv[0], qv[1], up[0:1, :128], up[0:1, 128:], up[1:2, :128], up[1:2, 128:]]
    narrow = jnp.concatenate(narrow + [jnp.zeros((2, 128), F32)], axis=0)
    rows = []
    for v in (wide, narrow):
        high = v.astype(BF).astype(F32)
        rows += [high, v - high]
    block[:32] = jnp.concatenate(rows, axis=0).astype(BF)
    block[32:224] = w_qkv[0]
    block[224:288] = w_out[0]
    copies = [pltpu.make_async_copy(block, out.at[w, ROWS:512], sems.at[16 + w]) for w in range(16)]
    for copy in copies:
        copy.start()
    seq = inputs.shape[2]
    turned[...] = jnp.zeros(turned.shape, F32)
    for s in range(3):
        turned[:64, :seq] = inputs[s].astype(F32)
        turned[64:, :seq] = cotangent[s].astype(F32)
        held[s] = turned[...].T[:ROWS].astype(BF)
    for w in range(16):
        slot = jnp.clip(w - first, 0, 2)
        copies.append(pltpu.make_async_copy(held.at[slot], out.at[w, 0:ROWS], sems.at[w]))
        copies[-1].start()
    for copy in copies:
        copy.wait()


def prepare_next(w_qkv, w_out, w_up, w_down, out):
    for w in range(16):
        out[w, :128] = w_up[0, :, :128]
        out[w, 128:256] = w_up[0, :, 128:]
        out[w, 256:512] = w_down[0]
        out[w, 512:704] = w_qkv[1]
        out[w, 704:768] = w_out[1]


def prepare_mlp(w_up, w_down, out):
    for w in range(out.shape[0]):
        out[w, :128] = w_up[1, :, :128]
        out[w, 128:256] = w_up[1, :, 128:]
        out[w, 256:] = w_down[1]


def norm_forward(at, left, got_left, right, got_right, stream, wide, stream_out, out):
    shift, gain, bias = [wide[d, i : i + 1] for d, i in at]
    new = stream[...] + (pair_sum(left, got_left, right, got_right) + shift)
    stream_out[...] = new
    normed, _ = norm_parts(new)
    out[...] = (normed * gain + bias).astype(BF)


def norm_backward(at, left, got_left, right, got_right, stream, upstream, wide, grad_out, low_out, sums):
    grad = pair_sum(left, got_left, right, got_right)
    norm_backward_of(grad, at, stream, upstream, wide, grad_out, low_out, sums)


def norm_backward_single(at, part, got, stream, upstream, wide, grad_out, low_out, sums):
    grad = part[...].astype(F32) + got[...].astype(F32)
    norm_backward_of(grad, at, stream, upstream, wide, grad_out, low_out, sums)


def norm_backward_of(grad, at, stream, upstream, wide, grad_out, low_out, sums):
    normed, factor = norm_parts(stream[...])
    scaled = grad * wide[at[0], at[1] : at[1] + 1]
    first = jnp.mean(scaled, axis=-1, keepdims=True)
    second = jnp.mean(scaled * normed, axis=-1, keepdims=True)
    new = upstream[...].astype(F32) + factor * (scaled - first - normed * second)
    grad_out[...] = new
    low = new.astype(BF)
    low_out[...] = low.astype(low_out.dtype)
    sums[0:1] = jnp.sum(grad * normed, axis=0, keepdims=True)
    sums[1:2] = jnp.sum(grad, axis=0, keepdims=True)
    sums[2:3] = jnp.sum(low.astype(F32), axis=0, keepdims=True)
    sums[3:8] = jnp.zeros((5, WIDTH), F32)


def norm_backward_last(
    place, left, got_left, right, got_right, stream, upstream, wide, s20, s11, s21, low_sum,
    keep, give, keep_v, give_v, new, sums, table,
):
    norm_backward((0, 0), left, got_left, right, got_right, stream, upstream, wide, new, new, sums)
    owner_lanes(new, place[0], place[1] == 0, keep, give)
    pieces = [sums[0:2], s20[2:3], s20[0:2], s11[2:3], s11[0:2], s21[2:3], s21[0:2], low_sum[...]]
    table[...] = jnp.concatenate(pieces + [jnp.zeros((4, WIDTH), F32)], axis=0)
    owner_lanes(table, place[0], place[1] == 0, keep_v, give_v)


def final_rows(place, rows_in, keep, got, keep_v, got_v, p0, p1, u0, u1, out, held, sem):
    wide = keep_v[...] + got_v[...]
    high = wide.astype(BF).astype(F32)
    low = wide - high
    tokens = owner_rows(place[1] == 0, keep, got)
    for i in range(2):
        part = slice(64 * i, 64 * i + 64)
        narrow = [
            jnp.concatenate(
                [p[:, 128 * i : 128 * i + 64], p[:, 256 + 64 * i : 320 + 64 * i]], axis=1
            )
            for p in (p0, p1)
        ]
        for u in (u0, u1):
            narrow += [u[:, 256 * i : 256 * i + 128], u[:, 256 * i + 128 : 256 * i + 256]]
        narrow = jnp.concatenate(narrow + [jnp.zeros((2, 128), F32)], axis=0)
        narrow_high = narrow.astype(BF).astype(F32)
        rows = jnp.concatenate(
            [jnp.concatenate([high[:, part], low[:, part]], axis=1), narrow_high, narrow - narrow_high],
            axis=0,
        ).astype(BF)
        for g in range(8):
            held[2 * g + i, :HALF] = tokens[i]
            held[2 * g + i, HALF:] = rows
    copy = pltpu.make_async_copy(held, out.at[:, 256:400], sem)
    copy.start()
    copy.wait()


def collect(meta, received, out, held, sems):
    copies = []
    for s in range(3):
        at = jnp.minimum(meta[2] + s, 15)
        copies.append(
            pltpu.make_async_copy(received.at[at, 256:368], held.at[s], sems.at[s])
        )
        copies[-1].start()
    for s in range(3):
        copies[s].wait()
        out[s] = owner_tokens(held[s], s < meta[3])


def finish(meta, received, sum_1, out, qkv, w_out, g1, b1, bo, g2, b2, bd, qv, up, weights, vectors, held, sems):
    copies = [
        pltpu.make_async_copy(received.at[:, 0:256], weights, sems.at[3]),
        pltpu.make_async_copy(received.at[:, 368:400], vectors, sems.at[4]),
    ]
    for s in range(3):
        at = jnp.minimum(meta[2] + s, 15)
        copies.append(
            pltpu.make_async_copy(received.at[at, 256:368], held.at[s], sems.at[s])
        )
    for copy in copies:
        copy.start()
    for copy in copies:
        copy.wait()
    for s in range(3):
        out[s] = owner_tokens(held[s], s < meta[3])
    total_v = jnp.sum(vectors[...].astype(F32), axis=0)
    wide = total_v[:16, :64] + total_v[:16, 64:]
    for v, ref in enumerate((g1, b1, bo, g2, b2, bd)):
        ref[...] = jnp.concatenate([wide[v : v + 1], wide[v + 6 : v + 7]], axis=0)
    narrow = total_v[16:24] + total_v[24:32]
    qv[...] = narrow[0:2]
    for d in range(2):
        up[d : d + 1] = jnp.concatenate([narrow[2 + 2 * d : 3 + 2 * d], narrow[3 + 2 * d : 4 + 2 * d]], axis=1)
    for d in range(2):
        block = jnp.sum(weights[...].astype(F32), axis=0) if d == 0 else sum_1[...]
        qkv[d] = block[:192]
        w_out[d] = block[192:256]


ATTENTION_SCRATCH = (pltpu.VMEM((384, WIDTH), BF), pltpu.VMEM((128, WIDTH), BF))
MLP_SCRATCH = (pltpu.VMEM((WIDTH, 512), BF), pltpu.VMEM((512, WIDTH), BF))
SUM_SHAPES = (shape(F32, HALF, WIDTH), shape(BF, HALF, WIDTH))
NORM_SHAPES = (shape(F32, HALF, WIDTH), shape(BF, HALF, WIDTH))
ATTENTION_FLOPS = 2 * ROWS * WIDTH * 512
MLP_FLOPS = 2 * ROWS * WIDTH * 1024


def exchange(chunks):
    return lax.all_to_all(chunks, DP, 0, 0)


def shards(
    inputs,
    cotangent,
    group_images,
    ln1_gain,
    ln1_bias,
    w_qkv,
    b_qv,
    w_out,
    b_out,
    ln2_gain,
    ln2_bias,
    w_up,
    b_up,
    w_down,
    b_down,
):
    seq = inputs.shape[1]
    half, rows = HALF, ROWS
    core = lax.axis_index("c")
    ring = lax.axis_index("z")
    group = lax.axis_index(("y", "xl"))
    worker = lax.axis_index(DP)
    first_core = core == 0

    earlier = jnp.arange(8)[:, None] > jnp.arange(8)[None, :]
    offsets = jnp.sum(jnp.where(earlier, group_images[None, :], 0), axis=1)
    my_offset = jnp.sum(jnp.where(jnp.arange(8) < group, group_images, 0))
    my_live = jnp.sum(jnp.where(jnp.arange(8) == group, group_images, 0))
    source = jnp.sum((offsets <= worker).astype(jnp.int32)) - 1
    mine_valid = jnp.where(first_core, half, seq - half)
    place = jnp.stack([ring, core, my_offset, my_live, mine_valid, seq - mine_valid])
    place = place.astype(jnp.int32)

    w_qkv = w_qkv.transpose(0, 2, 3, 1).reshape(2, 192, 128)
    (chunks,) = run(
        prepare,
        (shape(BF, 16, 512, 128),),
        (group_images, inputs.transpose(0, 2, 1), cotangent.transpose(0, 2, 1))
        + (ln1_gain, ln1_bias, b_out, ln2_gain, ln2_bias, b_down, b_qv, b_up, w_qkv, w_out),
        0,
        (
            pltpu.VMEM((128, 256), F32),
            pltpu.VMEM((3, rows, 128), BF),
            pltpu.VMEM((288, 128), BF),
            pltpu.SemaphoreType.DMA((32,)),
        ),
        1,
        range(1, 13),
        56,
        (),
        True,
    )
    arrived = exchange(chunks)
    (next_rows,) = run(
        prepare_next, (shape(BF, 16, 768, 128),), (w_qkv, w_out, w_up, w_down), 0
    )
    (mlp_rows_1,) = run(prepare_mlp, (shape(BF, 16, 512, 128),), (w_up, w_down), 0)
    next_rows, mlp_rows_1, arrived, place = lax.optimization_barrier(
        (next_rows, mlp_rows_1, arrived, place)
    )

    picked = lax.dynamic_slice(arrived, (2 * source, 0, 0), (2, rows, 128))
    vectors_here = arrived[:2, rows:256]
    low_part, high_part = picked[:, :half], picked[:, half:rows]
    tail = vectors_here[:, :16]
    keep = jnp.concatenate([jnp.where(first_core, low_part, high_part), tail], axis=1)
    give = jnp.concatenate([jnp.where(first_core, high_part, low_part), tail], axis=1)
    got = core_swap(give)
    part_0 = jnp.where(first_core, keep, got)
    part_1 = jnp.where(first_core, got, keep)
    left = jnp.concatenate([part_0[..., :64], part_1[..., :64]], axis=-1)
    right = jnp.concatenate([part_0[..., 64:], part_1[..., 64:]], axis=-1)
    blocks = ring_blocks(jnp.concatenate([left, right[:, half:], right[:, :half]], axis=1))
    following = exchange(next_rows)
    mlp_w = [following, None]
    attention_w = [arrived, following]
    attention_at = [256, 512]
    stream, h1, wide, cotangent_low, low_sum, bias = run(
        norm_first,
        NORM_SHAPES
        + (shape(F32, 2, 8, WIDTH), shape(BF, half, WIDTH), shape(F32, 1, WIDTH))
        + (shape(F32, 2, 2, 512),),
        [place] + blocks + [vectors_here[:, 16:]],
        0,
        (),
        1,
    )
    kept = []
    for d in range(2):
        h1_other = core_swap(h1)
        packed, heads, mine, theirs = run(
            functools.partial(attention_forward, d),
            (shape(BF, ROWS, 384), shape(BF, ROWS, 128)) + SUM_SHAPES,
            (place, h1, h1_other, attention_w[d], bias),
            ATTENTION_FLOPS,
            ATTENTION_SCRATCH,
            1,
            ((3, attention_at[d], 256),),
        )
        pairs, _, done = total(mine, theirs, None, mlp_w[1])
        mlp_w[1] = done
        middle, h2 = run(
            functools.partial(norm_forward, ((d, 2), (d, 3), (d, 4))),
            NORM_SHAPES,
            pairs + (stream, wide),
            0,
        )
        if d == 0:
            mlp_rows_1, _, h2 = lax.optimization_barrier((mlp_rows_1, following, h2))
            mlp_w[1] = exchange(mlp_rows_1)
        h2_other = core_swap(h2)
        act, slope, mine, theirs = run(
            functools.partial(mlp_forward, d),
            (shape(BF, ROWS, 512), shape(F32, ROWS, 512)) + SUM_SHAPES,
            (h2, h2_other, mlp_w[d], bias),
            MLP_FLOPS,
            MLP_SCRATCH,
            0,
            ((2, 0, 512),),
        )
        kept.append((stream, h1, h1_other, packed, heads, middle, h2, h2_other, act, slope))
        if d == 0:
            pairs, _, _ = total(mine, theirs)
            stream, h1 = run(
                functools.partial(norm_forward, ((0, 5), (1, 0), (1, 1))),
                NORM_SHAPES,
                pairs + (middle, wide),
                0,
            )
    grad_low = cotangent_low
    low_other = core_swap(grad_low)
    grad_stream = cotangent_low
    previous = mlp_got = None
    sums, narrow_sums = {}, {}
    for d in (1, 0):
        start, h1, h1_other, packed, heads, middle, h2, h2_other, act, slope = kept[d]
        if d == 0:
            low_other = core_swap(grad_low)
            attention_grad, _ = lax.optimization_barrier((attention_grad, mlp_got))
            mixed = exchange(attention_grad)
        extra = (mine, theirs) if d == 1 else ()
        both = WIDTH * 2 if d == 1 else WIDTH
        upper_grad, up_sum, mine, theirs = run(
            mlp_backward_and_out if d == 1 else mlp_backward,
            (shape(BF, ROWS, 512), shape(F32, 1, 512))
            + (shape(F32, HALF, both), shape(BF, HALF, both)),
            (grad_low, low_other, mlp_w[d], slope) + extra,
            MLP_FLOPS,
            MLP_SCRATCH,
            0,
            ((2, 0, 512),),
        )

        def mlp_work(upper_grad):
            args = (h2, h2_other, upper_grad, act, grad_low, low_other)
            return run(
                mlp_weights,
                (shape(BF, 16, 512, 128),),
                args,
                MLP_FLOPS,
                mirrors=(0,),
            )[1]

        pairs, mlp_grad, _ = total(mine, theirs, (mlp_work, upper_grad))
        if d == 0:
            mlp_grad, mixed = lax.optimization_barrier((mlp_grad, mixed))
        previous = exchange(mlp_grad)
        step = norm_backward
        if d == 1:
            pairs = lax.optimization_barrier(pairs)
            keep, give = run(
                norm_last,
                (shape(BF, half, 128), shape(BF, half, 128)),
                (place,) + pairs[2:] + (middle, wide),
                0,
                (pltpu.VMEM((half, WIDTH), F32),),
                1,
            )
            keep, give, pairs = lax.optimization_barrier((keep, give, pairs))
            out_keep, out_got = keep, core_swap(give)
            step, pairs = norm_backward_single, pairs[:2]
        grad_stream, grad_low, sums[2, d] = run(
            functools.partial(step, (d, 3)),
            NORM_SHAPES + (shape(F32, 8, WIDTH),),
            pairs + (middle, grad_stream, wide),
            0,
        )
        low_other = core_swap(grad_low)
        packed_grad, packed_sum, mine, theirs = run(
            attention_backward,
            (shape(BF, ROWS, 384), shape(F32, 1, 384)) + SUM_SHAPES,
            (place, grad_low, low_other, packed, attention_w[d]),
            ATTENTION_FLOPS,
            ATTENTION_SCRATCH,
            1,
            ((4, attention_at[d], 256),),
        )
        narrow_sums[d] = (packed_sum, up_sum)

        def attention_work(packed_grad):
            args = (h1, h1_other, packed_grad, heads, grad_low, low_other)
            if d == 1:
                return run(
                    attention_weights_and_out,
                    (shape(BF, 16, 368, 128),),
                    (place,) + args + (out_keep, out_got),
                    ATTENTION_FLOPS,
                    smem=1,
                    mirrors=(0,),
                )[1]
            return run(
                attention_weights,
                (shape(BF, 16, 400, 128),),
                args,
                ATTENTION_FLOPS,
                mirrors=(0,),
            )[1]

        pairs, attention_grad, mlp_done = total(
            mine, theirs, (attention_work, packed_grad), previous if d == 1 else None
        )
        if d == 1:
            mlp_got = mlp_done
        if d == 1:
            grad_stream, grad_low, sums[1, d] = run(
                functools.partial(norm_backward, (d, 0)),
                NORM_SHAPES + (shape(F32, 8, WIDTH),),
                pairs + (start, grad_stream, wide),
                0,
            )
    keep, give, keep_v, give_v = run(
        norm_backward_last,
        (shape(BF, half, 128), shape(BF, half, 128), shape(F32, 16, 128), shape(F32, 16, 128)),
        (place,) + pairs + (start, grad_stream, wide, sums[2, 0], sums[1, 1], sums[2, 1], low_sum),
        0,
        (pltpu.VMEM((half, WIDTH), F32), pltpu.VMEM((8, WIDTH), F32), pltpu.VMEM((16, WIDTH), F32)),
        1,
    )
    (last_rows,) = pl.pallas_call(
        final_rows,
        out_shape=[shape(BF, 16, 400, 128)],
        in_specs=[pl.BlockSpec(memory_space=pltpu.SMEM), pl.BlockSpec(memory_space=pltpu.HBM)]
        + [pl.BlockSpec(memory_space=pltpu.VMEM)] * 8,
        out_specs=[pl.BlockSpec(memory_space=pltpu.HBM)],
        scratch_shapes=[pltpu.VMEM((16, 144, 128), BF), pltpu.SemaphoreType.DMA(())],
        input_output_aliases={1: 0},
        compiler_params=pltpu.CompilerParams(vmem_limit_bytes=56 * 2**20),
    )(
        place,
        attention_grad,
        keep,
        core_swap(give),
        keep_v,
        core_swap(give_v),
        narrow_sums[0][0],
        narrow_sums[1][0],
        narrow_sums[0][1],
        narrow_sums[1][1],
    )
    last_rows, previous = lax.optimization_barrier((last_rows, previous))
    last = exchange(last_rows)
    mixed, previous, mlp_got, _ = lax.optimization_barrier((mixed, previous, mlp_got, last_rows))

    def summed(block):
        return jnp.sum(block.astype(F32), axis=0)

    mlp = [summed(previous), summed(mlp_got)]
    grad_up = jnp.stack([jnp.concatenate([m[:128], m[128:256]], axis=-1) for m in mlp])
    grad_down = jnp.stack([m[256:] for m in mlp])
    hbm, vmem = pl.BlockSpec(memory_space=pltpu.HBM), pl.BlockSpec(memory_space=pltpu.VMEM)
    smem = pl.BlockSpec(memory_space=pltpu.SMEM)
    (result,) = pl.pallas_call(
        collect,
        out_shape=[shape(F32, 3, 64, seq)],
        in_specs=[smem, hbm],
        out_specs=[vmem],
        scratch_shapes=[pltpu.VMEM((3, half, 128), BF), pltpu.SemaphoreType.DMA((3,))],
    )(place, mixed)
    grad_inputs, grad_qkv, grad_out, g1, b1, bo, g2, b2, bd, grad_qv, grad_b_up = pl.pallas_call(
        finish,
        out_shape=[shape(F32, 3, 64, seq), shape(F32, 2, 192, 128), shape(F32, 2, 64, 128)]
        + [shape(F32, 2, 64)] * 6
        + [shape(F32, 2, 128), shape(F32, 2, 256)],
        in_specs=[smem, hbm, vmem],
        out_specs=[vmem] * 11,
        scratch_shapes=[
            pltpu.VMEM((16, 256, 128), BF),
            pltpu.VMEM((16, 32, 128), BF),
            pltpu.VMEM((3, half, 128), BF),
            pltpu.SemaphoreType.DMA((5,)),
        ],
        compiler_params=pltpu.CompilerParams(vmem_limit_bytes=16 * 2**20),
    )(place, last, summed(mixed[:, :256]))
    return (
        result.transpose(0, 2, 1),
        grad_inputs.transpose(0, 2, 1),
        g1,
        b1,
        grad_qkv[:, None].transpose(0, 3, 1, 2),
        grad_qv[:, None, :],
        grad_out,
        bo,
        g2,
        b2,
        grad_up,
        grad_b_up,
        grad_down,
        bd,
    )


def solution(mesh):
    split = Mesh(mesh.devices.reshape(4, 2, 2, 4, 2), ("y", "xl", "xh", "z", "c"))
    gx = ("y", "xl")
    gy = ("xh", "z", "c")
    token = P(gx, None, gy)
    vector = P(None, gy)
    return jax.shard_map(
        shards,
        mesh=split,
        in_specs=(
            token,
            token,
            P(),
            vector,
            vector,
            P(None, gx, gy, None),
            P(None, gy, None),
            P(None, gy, gx),
            vector,
            vector,
            vector,
            P(None, gx, gy),
            vector,
            P(None, gy, gx),
            vector,
        ),
        out_specs=(
            token,
            token,
            vector,
            vector,
            P(None, gx, gy, None),
            P(None, gy, None),
            P(None, gy, gx),
            vector,
            vector,
            vector,
            P(None, gx, gy),
            vector,
            P(None, gy, gx),
            vector,
        ),
        check_vma=False,
    )
```

```python
import functools

import jax
import jax.numpy as jnp
from jax import lax
from jax.experimental import pallas as pl
from jax.experimental.pallas import tpu as pltpu
from jax.sharding import Mesh, PartitionSpec as P

EPS = 1e-06
BF = jnp.bfloat16
F32 = jnp.float32
DP = ("y", "xl", "xh")
SWAP = [(0, 1), (1, 0)]
PAIR_A = [(0, 1), (1, 0), (2, 3), (3, 2)]
PAIR_B = [(0, 3), (3, 0), (1, 2), (2, 1)]


def dot(a, b, ca, cb):
    return lax.dot_general(a, b, (((ca,), (cb,)), ((), ())), preferred_element_type=F32)


def core_swap(block):
    return lax.ppermute(block, "c", SWAP)


def ring_blocks(block):
    return [block] + [
        lax.ppermute(block, "z", [(i, (i + step) % 4) for i in range(4)]) for step in (1, 3, 2)
    ]


def total(mine, theirs, work=None, late=None):
    parts = (shape(BF, HALF, mine.shape[1] // 2),) * 2
    left, right = run(add_cores, parts, (mine, core_swap(theirs)), 0)
    if work is not None:
        left, right, given = lax.optimization_barrier((left, right, work[1]))
    got_left = lax.ppermute(left, "z", PAIR_A)
    got_right = lax.ppermute(right, "z", PAIR_B)
    done = work[0](given) if work is not None else None
    left, right = run(add_pairs, parts, (left, got_left, right, got_right), 0)
    left, right, late, done = lax.optimization_barrier((left, right, late, done))
    got_left = lax.ppermute(left, "z", PAIR_B)
    got_right = lax.ppermute(right, "z", PAIR_A)
    return (left, got_left, right, got_right), done, late


def add_cores(mine, got, left, right):
    both = (mine[...] + got[...].astype(F32)).astype(BF)
    cut = mine.shape[1] // 2
    left[...] = both[:, :cut]
    right[...] = both[:, cut:]


def add_pairs(left, got_left, right, got_right, left_out, right_out):
    left_out[...] = (left[...].astype(F32) + got_left[...].astype(F32)).astype(BF)
    right_out[...] = (right[...].astype(F32) + got_right[...].astype(F32)).astype(BF)


HALF = 112
ROWS = 2 * HALF
WIDTH = 1024


def run(
    kernel, outs, args, flops, scratch=(), smem=0, far=(), grant=16, mirrors=(), direct=False
):
    far = [f if isinstance(f, tuple) else (f, None, None) for f in far]
    size = sum(a.size * a.dtype.itemsize for a in args)
    size += sum(o.size * o.dtype.itemsize for o in outs)
    fetched = [f[0] for f in far]
    specs = [
        pl.BlockSpec(
            memory_space=pltpu.SMEM if i < smem else pltpu.HBM if i in fetched else pltpu.VMEM
        )
        for i in range(len(args))
    ]
    held = []
    for i, _, count in far:
        sizes = args[i].shape
        sizes = sizes if count is None else (sizes[0], count) + sizes[2:]
        held.append(pltpu.VMEM(sizes, args[i].dtype))
    more = [
        shape(args[m[0]].dtype, ROWS, WIDTH) if isinstance(m, tuple) else outs[m] for m in mirrors
    ]
    semaphores = [pltpu.SemaphoreType.DMA((max(len(far), 1),))]
    semaphores += [pltpu.SemaphoreType.DMA((max(2 * len(mirrors), 1),))]

    def body(*refs):
        refs = list(refs)
        n, m = len(args), len(outs)
        results, copied = refs[n : n + m], refs[n + m : n + m + len(mirrors)]
        rest = refs[n + m + len(mirrors) : -2]
        sems, out_sems = refs[-2:]
        spaces, rest = rest[len(rest) - len(far) :], rest[: len(rest) - len(far)]
        copies = []
        for k, (i, start, count) in enumerate(far):
            source = refs[i] if count is None else refs[i].at[:, start : start + count]
            copies.append(pltpu.make_async_copy(source, spaces[k], sems.at[k]))
            copies[-1].start()
        sent = {}

        def send(k):
            if isinstance(mirrors[k], tuple):
                sent[k] = [
                    pltpu.make_async_copy(
                        refs[i], copied[k].at[HALF * j : HALF * j + HALF], out_sems.at[2 * k + j]
                    )
                    for j, i in enumerate(mirrors[k])
                ]
            else:
                sent[k] = [
                    pltpu.make_async_copy(results[mirrors[k]], copied[k], out_sems.at[2 * k])
                ]
            for copy in sent[k]:
                copy.start()

        for k, mirror in enumerate(mirrors):
            if isinstance(mirror, tuple):
                send(k)
        for k, copy in enumerate(copies):
            copy.wait()
            refs[fetched[k]] = spaces[k]
        if mirrors:
            kernel(*refs[:n], *results, *rest, send=send)
        else:
            kernel(*refs[:n], *results, *rest)
        for k in range(len(mirrors)):
            if k not in sent:
                send(k)
        for group in sent.values():
            for copy in group:
                copy.wait()

    space = pltpu.HBM if direct else pltpu.VMEM
    return pl.pallas_call(
        body,
        out_shape=list(outs) + more,
        in_specs=specs,
        out_specs=[pl.BlockSpec(memory_space=space)] * len(outs)
        + [pl.BlockSpec(memory_space=pltpu.HBM)] * len(more),
        scratch_shapes=list(scratch) + held + semaphores,
        compiler_params=pltpu.CompilerParams(vmem_limit_bytes=grant * 2**20),
        cost_estimate=pl.CostEstimate(
            flops=int(flops), bytes_accessed=int(size), transcendentals=0
        ),
    )(*args)


def shape(dtype, *sizes):
    return jax.ShapeDtypeStruct(sizes, dtype)


def norm_parts(stream):
    center = stream - jnp.mean(stream, axis=-1, keepdims=True)
    factor = lax.rsqrt(jnp.mean(center * center, axis=-1, keepdims=True) + EPS)
    return center * factor, factor


def place_attention(w, w_qkv, w_out):
    for g in range(8):
        cols = slice(128 * g, 128 * g + 128)
        for i in range(2):
            w_qkv[128 * i : 128 * i + 128, cols] = w[2 * g + i, :128]
            w_qkv[256 + 64 * i : 320 + 64 * i, cols] = w[2 * g + i, 128:192]
            w_out[64 * i : 64 * i + 64, cols] = w[2 * g + i, 192:256]


def place_mlp(w, w_up, w_down):
    for g in range(8):
        rows = slice(128 * g, 128 * g + 128)
        for i in range(2):
            for j in range(2):
                at = 256 * i + 128 * j
                w_up[rows, at : at + 128] = w[2 * g + i, 128 * j : 128 * j + 128]
            w_down[256 * i : 256 * i + 256, rows] = w[2 * g + i, 256:512]


def both_rows(mine, other):
    return jnp.concatenate([mine[...], other[...]], axis=0)


def softmax(valid, query, key):
    scores = dot(query, key, 1, 1) * 64**-0.5
    at = lax.broadcasted_iota(jnp.int32, (1, ROWS), 1)
    limit = jnp.where(at < HALF, valid[4], valid[5] + HALF)
    scores = jnp.where(at < limit, scores, -1e30)
    exponent = jnp.exp(scores - jnp.max(scores, axis=-1, keepdims=True))
    return exponent / jnp.sum(exponent, axis=-1, keepdims=True)


def part_of(packed, name, i):
    start = {"q": 128 * i, "k": 128 * i + 64, "v": 256 + 64 * i}[name]
    return packed[:, start : start + 64]


def attention_forward(at, valid, mine, other, w, bias, packed_out, heads_out, out, away, w_qkv, w_out):
    place_attention(w, w_qkv, w_out)
    packed = dot(both_rows(mine, other), w_qkv[...], 1, 1) + bias[at, 0:1, :384]
    packed_out[...] = packed.astype(BF)
    heads = []
    for i in range(2):
        query, key, value = [part_of(packed, n, i).astype(BF) for n in "qkv"]
        probs = softmax(valid, query, key).astype(BF)
        heads.append(dot(probs, value, 1, 0))
    heads = jnp.concatenate(heads, axis=1).astype(BF)
    heads_out[...] = heads
    result = dot(heads, w_out[...], 1, 0)
    out[...] = result[:HALF]
    away[...] = result[HALF:].astype(BF)


def attention_backward(valid, mine, other, packed_in, w, grad_out, sums, out, away, w_qkv, w_out):
    place_attention(w, w_qkv, w_out)
    heads_grad = dot(both_rows(mine, other), w_out[...], 1, 1)
    packed = packed_in[...].astype(F32)
    parts = []
    values = []
    for i in range(2):
        query, key, value = [part_of(packed, n, i).astype(BF) for n in "qkv"]
        p = softmax(valid, query, key)
        upstream = heads_grad[:, 64 * i : 64 * i + 64].astype(BF)
        prob_grad = dot(upstream, value, 1, 1)
        values.append(dot(p.astype(BF), upstream, 0, 0))
        score_grad = (
            p * (prob_grad - jnp.sum(prob_grad * p, axis=-1, keepdims=True))
        ).astype(BF)
        parts.append(dot(score_grad, key, 1, 0) * 64**-0.5)
        parts.append(dot(score_grad, query, 0, 0) * 64**-0.5)
    grad = jnp.concatenate(parts + values, axis=1).astype(BF)
    grad_out[...] = grad
    sums[...] = jnp.sum(grad.astype(F32), axis=0, keepdims=True)
    result = dot(grad, w_qkv[...], 1, 0)
    out[...] = result[:HALF]
    away[...] = result[HALF:].astype(BF)


def attention_weights(h_mine, h_other, grad, heads, mine, other, rows_out, send):
    qkv = dot(grad[...], both_rows(h_mine, h_other), 0, 0).astype(BF)
    back = dot(heads[...], both_rows(mine, other), 0, 0).astype(BF)
    for g in range(8):
        cols = slice(128 * g, 128 * g + 128)
        for i in range(2):
            at = 2 * g + i
            rows_out[at, :128] = qkv[128 * i : 128 * i + 128, cols]
            rows_out[at, 128:192] = qkv[256 + 64 * i : 320 + 64 * i, cols]
            rows_out[at, 192:256] = back[64 * i : 64 * i + 64, cols]


def mlp_forward(at, mine, other, w, bias, act_out, slope_out, out, away, w_up, w_down):
    place_mlp(w, w_up, w_down)
    upper = dot(both_rows(mine, other), w_up[...], 1, 0) + bias[at, 1:2]
    phi = 0.5 * (1.0 + lax.erf(upper * 0.5**0.5))
    act = (upper * phi).astype(BF)
    act_out[...] = act
    slope_out[...] = phi + upper * (jnp.exp(-0.5 * upper * upper) * 0.3989422804014327)
    result = dot(act, w_down[...], 1, 0)
    out[...] = result[:HALF]
    away[...] = result[HALF:].astype(BF)


def mlp_backward(mine, other, w, slope, grad_out, sums, out, away, w_up, w_down):
    place_mlp(w, w_up, w_down)
    grad = (dot(both_rows(mine, other), w_down[...], 1, 1) * slope[...]).astype(BF)
    grad_out[...] = grad
    sums[...] = jnp.sum(grad.astype(F32), axis=0, keepdims=True)
    result = dot(grad, w_up[...], 1, 1)
    out[...] = result[:HALF]
    away[...] = result[HALF:].astype(BF)


def mlp_backward_and_out(
    mine, other, w, slope, f_mine, f_theirs, grad_out, sums, out, away, w_up, w_down
):
    mlp_backward(
        mine, other, w, slope, grad_out, sums, out.at[:, :WIDTH], away.at[:, :WIDTH], w_up, w_down
    )
    out[:, WIDTH:] = f_mine[...]
    away[:, WIDTH:] = f_theirs[...]


def attention_weights_and_out(place, h_mine, h_other, grad, heads, mine, other, keep, got, rows_out, send):
    attention_weights(h_mine, h_other, grad, heads, mine, other, rows_out, send)
    tokens = owner_rows(place[1] == 0, keep, got)
    for g in range(8):
        for i in range(2):
            rows_out[2 * g + i, 256:] = tokens[i]


def mlp_weights(h_mine, h_other, grad, act, mine, other, rows_out, send):
    up = dot(both_rows(h_mine, h_other), grad[...], 0, 0).astype(BF)
    down = dot(act[...], both_rows(mine, other), 0, 0).astype(BF)
    for g in range(8):
        cols = slice(128 * g, 128 * g + 128)
        for i in range(2):
            for j in range(2):
                at = 256 * i + 128 * j
                rows_out[2 * g + i, 128 * j : 128 * j + 128] = up[cols, at : at + 128]
            rows_out[2 * g + i, 256:512] = down[256 * i : 256 * i + 256, cols]


def pair_sum(left, got_left, right, got_right):
    return jnp.concatenate(
        [
            left[...].astype(F32) + got_left[...].astype(F32),
            right[...].astype(F32) + got_right[...].astype(F32),
        ],
        axis=1,
    )


def ring_place(ring, blocks, store):
    for step, block in zip((0, 1, 3, 2), blocks):
        place = lax.rem(ring + 4 - step, 4) * 128
        for i in range(2):
            store(pl.ds(pl.multiple_of(512 * i + place, 128), 128), block, i)


def norm_first(ring, a, b, c, d, narrow, stream_out, out, wide_out, cotangent, sums, bias_out):
    def store(columns, block, i):
        stream_out[:, columns] = block[i, :HALF].astype(F32)
        for depth in range(2):
            rows = block[i, HALF + 16 * depth : HALF + 16 * depth + 16].astype(F32)
            wide_out[depth, :, columns] = rows[:8] + rows[8:]
        upstream = block[i, HALF + 32 :]
        cotangent[:, columns] = upstream
        sums[:, columns] = jnp.sum(upstream.astype(F32), axis=0, keepdims=True)

    ring_place(ring[0], (a, b, c, d), store)
    normed, _ = norm_parts(stream_out[...])
    out[...] = (normed * wide_out[0, 0:1] + wide_out[0, 1:2]).astype(BF)
    pieces = []
    for i in range(2):
        piece = narrow[i].astype(F32)
        pieces.append(piece[:8] + piece[8:])
    blank = jnp.zeros((1, 64), F32)
    for depth in range(2):
        qv = [piece[depth : depth + 1] for piece in pieces]
        bias_out[depth, 0:1] = jnp.concatenate(
            [qv[0][:, :64], blank, qv[1][:, :64], blank, qv[0][:, 64:], qv[1][:, 64:]]
            + [jnp.zeros((1, 128), F32)],
            axis=1,
        )
        bias_out[depth, 1:2] = jnp.concatenate(
            [piece[at : at + 1] for piece in pieces for at in (2 + 2 * depth, 3 + 2 * depth)],
            axis=1,
        )


def owner_lanes(source, ring, first_core, keep, give):
    parts = []
    for i in range(2):
        at = pl.multiple_of(512 * i + 128 * ring, 128)
        parts.append(source[:, pl.ds(at, 128)].astype(F32))
    lanes = [
        jnp.concatenate([parts[0][:, s], parts[1][:, s]], axis=1)
        for s in (slice(0, 64), slice(64, 128))
    ]
    keep[...] = jnp.where(first_core, lanes[0], lanes[1]).astype(keep.dtype)
    give[...] = jnp.where(first_core, lanes[1], lanes[0]).astype(give.dtype)


def owner_rows(first_core, keep, got):
    keep, got = keep[...].astype(F32), got[...].astype(F32)
    early, late = jnp.where(first_core, keep, got), jnp.where(first_core, got, keep)
    return [
        jnp.concatenate([early[:, s], late[:, s]], axis=1).astype(BF)
        for s in (slice(0, 64), slice(64, 128))
    ]


def owner_tokens(block, live):
    block = block.astype(F32)
    tokens = jnp.concatenate([block[:, :64], block[:, 64:]], axis=0)
    return jnp.where(live, tokens.T[:, :197], 0.0)


def norm_last(place, part, got, stream, wide, keep, give, new):
    new[...] = stream[...] + (part[...].astype(F32) + got[...].astype(F32) + wide[1, 5:6])
    owner_lanes(new, place[0], place[1] == 0, keep, give)


def prepare(
    counts, inputs, cotangent, g1, b1, bo, g2, b2, bd, qv, up, w_qkv, w_out, out, turned, held, block, sems
):
    group = lax.axis_index(("y", "xl"))
    first = jnp.int32(0)
    for g in range(8):
        first = first + jnp.where(g < group, counts[g], 0)
    wide = [jnp.concatenate([v[0:1], v[1:2]], axis=1) for v in (g1, b1, bo, g2, b2, bd)]
    wide = jnp.concatenate(wide + [jnp.zeros((2, 128), F32)], axis=0)
    narrow = [qv[0], qv[1], up[0:1, :128], up[0:1, 128:], up[1:2, :128], up[1:2, 128:]]
    narrow = jnp.concatenate(narrow + [jnp.zeros((2, 128), F32)], axis=0)
    rows = []
    for v in (wide, narrow):
        high = v.astype(BF).astype(F32)
        rows += [high, v - high]
    block[:32] = jnp.concatenate(rows, axis=0).astype(BF)
    block[32:224] = w_qkv[0]
    block[224:288] = w_out[0]
    copies = [pltpu.make_async_copy(block, out.at[w, ROWS:512], sems.at[16 + w]) for w in range(16)]
    for copy in copies:
        copy.start()
    seq = inputs.shape[2]
    turned[...] = jnp.zeros(turned.shape, F32)
    for s in range(3):
        turned[:64, :seq] = inputs[s].astype(F32)
        turned[64:, :seq] = cotangent[s].astype(F32)
        held[s] = turned[...].T[:ROWS].astype(BF)
    for w in range(16):
        slot = jnp.clip(w - first, 0, 2)
        copies.append(pltpu.make_async_copy(held.at[slot], out.at[w, 0:ROWS], sems.at[w]))
        copies[-1].start()
    for copy in copies:
        copy.wait()


def prepare_next(w_qkv, w_out, w_up, w_down, out):
    for w in range(16):
        out[w, :128] = w_up[0, :, :128]
        out[w, 128:256] = w_up[0, :, 128:]
        out[w, 256:512] = w_down[0]
        out[w, 512:704] = w_qkv[1]
        out[w, 704:768] = w_out[1]


def prepare_mlp(w_up, w_down, out):
    for w in range(out.shape[0]):
        out[w, :128] = w_up[1, :, :128]
        out[w, 128:256] = w_up[1, :, 128:]
        out[w, 256:] = w_down[1]


def norm_forward(at, left, got_left, right, got_right, stream, wide, stream_out, out):
    shift, gain, bias = [wide[d, i : i + 1] for d, i in at]
    new = stream[...] + (pair_sum(left, got_left, right, got_right) + shift)
    stream_out[...] = new
    normed, _ = norm_parts(new)
    out[...] = (normed * gain + bias).astype(BF)


def norm_backward(at, left, got_left, right, got_right, stream, upstream, wide, grad_out, low_out, sums):
    grad = pair_sum(left, got_left, right, got_right)
    norm_backward_of(grad, at, stream, upstream, wide, grad_out, low_out, sums)


def norm_backward_single(at, part, got, stream, upstream, wide, grad_out, low_out, sums):
    grad = part[...].astype(F32) + got[...].astype(F32)
    norm_backward_of(grad, at, stream, upstream, wide, grad_out, low_out, sums)


def norm_backward_of(grad, at, stream, upstream, wide, grad_out, low_out, sums):
    normed, factor = norm_parts(stream[...])
    scaled = grad * wide[at[0], at[1] : at[1] + 1]
    first = jnp.mean(scaled, axis=-1, keepdims=True)
    second = jnp.mean(scaled * normed, axis=-1, keepdims=True)
    new = upstream[...].astype(F32) + factor * (scaled - first - normed * second)
    grad_out[...] = new
    low = new.astype(BF)
    low_out[...] = low.astype(low_out.dtype)
    sums[0:1] = jnp.sum(grad * normed, axis=0, keepdims=True)
    sums[1:2] = jnp.sum(grad, axis=0, keepdims=True)
    sums[2:3] = jnp.sum(low.astype(F32), axis=0, keepdims=True)
    sums[3:8] = jnp.zeros((5, WIDTH), F32)


def norm_backward_last(
    place, left, got_left, right, got_right, stream, upstream, wide, s20, s11, s21, low_sum,
    keep, give, keep_v, give_v, new, sums, table,
):
    norm_backward((0, 0), left, got_left, right, got_right, stream, upstream, wide, new, new, sums)
    owner_lanes(new, place[0], place[1] == 0, keep, give)
    pieces = [sums[0:2], s20[2:3], s20[0:2], s11[2:3], s11[0:2], s21[2:3], s21[0:2], low_sum[...]]
    table[...] = jnp.concatenate(pieces + [jnp.zeros((4, WIDTH), F32)], axis=0)
    owner_lanes(table, place[0], place[1] == 0, keep_v, give_v)


def final_rows(place, rows_in, keep, got, keep_v, got_v, p0, p1, u0, u1, out, held, sem):
    wide = keep_v[...] + got_v[...]
    high = wide.astype(BF).astype(F32)
    low = wide - high
    tokens = owner_rows(place[1] == 0, keep, got)
    for i in range(2):
        part = slice(64 * i, 64 * i + 64)
        narrow = [
            jnp.concatenate(
                [p[:, 128 * i : 128 * i + 64], p[:, 256 + 64 * i : 320 + 64 * i]], axis=1
            )
            for p in (p0, p1)
        ]
        for u in (u0, u1):
            narrow += [u[:, 256 * i : 256 * i + 128], u[:, 256 * i + 128 : 256 * i + 256]]
        narrow = jnp.concatenate(narrow + [jnp.zeros((2, 128), F32)], axis=0)
        narrow_high = narrow.astype(BF).astype(F32)
        rows = jnp.concatenate(
            [jnp.concatenate([high[:, part], low[:, part]], axis=1), narrow_high, narrow - narrow_high],
            axis=0,
        ).astype(BF)
        for g in range(8):
            held[2 * g + i, :HALF] = tokens[i]
            held[2 * g + i, HALF:] = rows
    copy = pltpu.make_async_copy(held, out.at[:, 256:400], sem)
    copy.start()
    copy.wait()


def collect(meta, received, out, held, sems):
    copies = []
    for s in range(3):
        at = jnp.minimum(meta[2] + s, 15)
        copies.append(
            pltpu.make_async_copy(received.at[at, 256:368], held.at[s], sems.at[s])
        )
        copies[-1].start()
    for s in range(3):
        copies[s].wait()
        out[s] = owner_tokens(held[s], s < meta[3])


def finish(meta, received, sum_1, out, qkv, w_out, g1, b1, bo, g2, b2, bd, qv, up, weights, vectors, held, sems):
    copies = [
        pltpu.make_async_copy(received.at[:, 0:256], weights, sems.at[3]),
        pltpu.make_async_copy(received.at[:, 368:400], vectors, sems.at[4]),
    ]
    for s in range(3):
        at = jnp.minimum(meta[2] + s, 15)
        copies.append(
            pltpu.make_async_copy(received.at[at, 256:368], held.at[s], sems.at[s])
        )
    for copy in copies:
        copy.start()
    for copy in copies:
        copy.wait()
    for s in range(3):
        out[s] = owner_tokens(held[s], s < meta[3])
    total_v = jnp.sum(vectors[...].astype(F32), axis=0)
    wide = total_v[:16, :64] + total_v[:16, 64:]
    for v, ref in enumerate((g1, b1, bo, g2, b2, bd)):
        ref[...] = jnp.concatenate([wide[v : v + 1], wide[v + 6 : v + 7]], axis=0)
    narrow = total_v[16:24] + total_v[24:32]
    qv[...] = narrow[0:2]
    for d in range(2):
        up[d : d + 1] = jnp.concatenate([narrow[2 + 2 * d : 3 + 2 * d], narrow[3 + 2 * d : 4 + 2 * d]], axis=1)
    for d in range(2):
        block = jnp.sum(weights[...].astype(F32), axis=0) if d == 0 else sum_1[...]
        qkv[d] = block[:192]
        w_out[d] = block[192:256]


ATTENTION_SCRATCH = (pltpu.VMEM((384, WIDTH), BF), pltpu.VMEM((128, WIDTH), BF))
MLP_SCRATCH = (pltpu.VMEM((WIDTH, 512), BF), pltpu.VMEM((512, WIDTH), BF))
SUM_SHAPES = (shape(F32, HALF, WIDTH), shape(BF, HALF, WIDTH))
NORM_SHAPES = (shape(F32, HALF, WIDTH), shape(BF, HALF, WIDTH))
ATTENTION_FLOPS = 2 * ROWS * WIDTH * 512
MLP_FLOPS = 2 * ROWS * WIDTH * 1024


def exchange(chunks):
    return lax.all_to_all(chunks, DP, 0, 0)


def shards(
    inputs,
    cotangent,
    group_images,
    ln1_gain,
    ln1_bias,
    w_qkv,
    b_qv,
    w_out,
    b_out,
    ln2_gain,
    ln2_bias,
    w_up,
    b_up,
    w_down,
    b_down,
):
    seq = inputs.shape[1]
    half, rows = HALF, ROWS
    core = lax.axis_index("c")
    ring = lax.axis_index("z")
    group = lax.axis_index(("y", "xl"))
    worker = lax.axis_index(DP)
    first_core = core == 0

    earlier = jnp.arange(8)[:, None] > jnp.arange(8)[None, :]
    offsets = jnp.sum(jnp.where(earlier, group_images[None, :], 0), axis=1)
    my_offset = jnp.sum(jnp.where(jnp.arange(8) < group, group_images, 0))
    my_live = jnp.sum(jnp.where(jnp.arange(8) == group, group_images, 0))
    source = jnp.sum((offsets <= worker).astype(jnp.int32)) - 1
    mine_valid = jnp.where(first_core, half, seq - half)
    place = jnp.stack([ring, core, my_offset, my_live, mine_valid, seq - mine_valid])
    place = place.astype(jnp.int32)

    w_qkv = w_qkv.transpose(0, 2, 3, 1).reshape(2, 192, 128)
    (chunks,) = run(
        prepare,
        (shape(BF, 16, 512, 128),),
        (group_images, inputs.transpose(0, 2, 1), cotangent.transpose(0, 2, 1))
        + (ln1_gain, ln1_bias, b_out, ln2_gain, ln2_bias, b_down, b_qv, b_up, w_qkv, w_out),
        0,
        (
            pltpu.VMEM((128, 256), F32),
            pltpu.VMEM((3, rows, 128), BF),
            pltpu.VMEM((288, 128), BF),
            pltpu.SemaphoreType.DMA((32,)),
        ),
        1,
        range(1, 13),
        56,
        (),
        True,
    )
    arrived = exchange(chunks)
    (next_rows,) = run(
        prepare_next, (shape(BF, 16, 768, 128),), (w_qkv, w_out, w_up, w_down), 0
    )
    (mlp_rows_1,) = run(prepare_mlp, (shape(BF, 16, 512, 128),), (w_up, w_down), 0)
    next_rows, mlp_rows_1, arrived, place = lax.optimization_barrier(
        (next_rows, mlp_rows_1, arrived, place)
    )

    picked = lax.dynamic_slice(arrived, (2 * source, 0, 0), (2, rows, 128))
    vectors_here = arrived[:2, rows:256]
    low_part, high_part = picked[:, :half], picked[:, half:rows]
    tail = vectors_here[:, :16]
    keep = jnp.concatenate([jnp.where(first_core, low_part, high_part), tail], axis=1)
    give = jnp.concatenate([jnp.where(first_core, high_part, low_part), tail], axis=1)
    got = core_swap(give)
    part_0 = jnp.where(first_core, keep, got)
    part_1 = jnp.where(first_core, got, keep)
    left = jnp.concatenate([part_0[..., :64], part_1[..., :64]], axis=-1)
    right = jnp.concatenate([part_0[..., 64:], part_1[..., 64:]], axis=-1)
    blocks = ring_blocks(jnp.concatenate([left, right[:, half:], right[:, :half]], axis=1))
    following = exchange(next_rows)
    mlp_w = [following, None]
    attention_w = [arrived, following]
    attention_at = [256, 512]
    stream, h1, wide, cotangent_low, low_sum, bias = run(
        norm_first,
        NORM_SHAPES
        + (shape(F32, 2, 8, WIDTH), shape(BF, half, WIDTH), shape(F32, 1, WIDTH))
        + (shape(F32, 2, 2, 512),),
        [place] + blocks + [vectors_here[:, 16:]],
        0,
        (),
        1,
    )
    kept = []
    for d in range(2):
        h1_other = core_swap(h1)
        packed, heads, mine, theirs = run(
            functools.partial(attention_forward, d),
            (shape(BF, ROWS, 384), shape(BF, ROWS, 128)) + SUM_SHAPES,
            (place, h1, h1_other, attention_w[d], bias),
            ATTENTION_FLOPS,
            ATTENTION_SCRATCH,
            1,
            ((3, attention_at[d], 256),),
        )
        pairs, _, _ = total(mine, theirs)
        middle, h2 = run(
            functools.partial(norm_forward, ((d, 2), (d, 3), (d, 4))),
            NORM_SHAPES,
            pairs + (stream, wide),
            0,
        )
        if d == 0:
            mlp_rows_1, _, h2 = lax.optimization_barrier((mlp_rows_1, following, h2))
            mlp_w[1] = exchange(mlp_rows_1)
        h2_other = core_swap(h2)
        act, slope, mine, theirs = run(
            functools.partial(mlp_forward, d),
            (shape(BF, ROWS, 512), shape(F32, ROWS, 512)) + SUM_SHAPES,
            (h2, h2_other, mlp_w[d], bias),
            MLP_FLOPS,
            MLP_SCRATCH,
            0,
            ((2, 0, 512),),
        )
        kept.append((stream, h1, h1_other, packed, heads, middle, h2, h2_other, act, slope))
        if d == 0:
            pairs, _, _ = total(mine, theirs)
            stream, h1 = run(
                functools.partial(norm_forward, ((0, 5), (1, 0), (1, 1))),
                NORM_SHAPES,
                pairs + (middle, wide),
                0,
            )
    grad_low = cotangent_low
    low_other = core_swap(grad_low)
    grad_stream = cotangent_low
    previous = mlp_got = None
    sums, narrow_sums = {}, {}
    for d in (1, 0):
        start, h1, h1_other, packed, heads, middle, h2, h2_other, act, slope = kept[d]
        if d == 0:
            low_other = core_swap(grad_low)
            attention_grad, _ = lax.optimization_barrier((attention_grad, mlp_got))
            mixed = exchange(attention_grad)
        extra = (mine, theirs) if d == 1 else ()
        both = WIDTH * 2 if d == 1 else WIDTH
        upper_grad, up_sum, mine, theirs = run(
            mlp_backward_and_out if d == 1 else mlp_backward,
            (shape(BF, ROWS, 512), shape(F32, 1, 512))
            + (shape(F32, HALF, both), shape(BF, HALF, both)),
            (grad_low, low_other, mlp_w[d], slope) + extra,
            MLP_FLOPS,
            MLP_SCRATCH,
            0,
            ((2, 0, 512),),
        )

        def mlp_work(upper_grad):
            args = (h2, h2_other, upper_grad, act, grad_low, low_other)
            return run(
                mlp_weights,
                (shape(BF, 16, 512, 128),),
                args,
                MLP_FLOPS,
                mirrors=(0,),
            )[1]

        pairs, mlp_grad, _ = total(mine, theirs, (mlp_work, upper_grad))
        if d == 0:
            mlp_grad, mixed = lax.optimization_barrier((mlp_grad, mixed))
        previous = exchange(mlp_grad)
        step = norm_backward
        if d == 1:
            pairs = lax.optimization_barrier(pairs)
            keep, give = run(
                norm_last,
                (shape(BF, half, 128), shape(BF, half, 128)),
                (place,) + pairs[2:] + (middle, wide),
                0,
                (pltpu.VMEM((half, WIDTH), F32),),
                1,
            )
            keep, give, pairs = lax.optimization_barrier((keep, give, pairs))
            out_keep, out_got = keep, core_swap(give)
            step, pairs = norm_backward_single, pairs[:2]
        grad_stream, grad_low, sums[2, d] = run(
            functools.partial(step, (d, 3)),
            NORM_SHAPES + (shape(F32, 8, WIDTH),),
            pairs + (middle, grad_stream, wide),
            0,
        )
        low_other = core_swap(grad_low)
        packed_grad, packed_sum, mine, theirs = run(
            attention_backward,
            (shape(BF, ROWS, 384), shape(F32, 1, 384)) + SUM_SHAPES,
            (place, grad_low, low_other, packed, attention_w[d]),
            ATTENTION_FLOPS,
            ATTENTION_SCRATCH,
            1,
            ((4, attention_at[d], 256),),
        )
        narrow_sums[d] = (packed_sum, up_sum)

        def attention_work(packed_grad):
            args = (h1, h1_other, packed_grad, heads, grad_low, low_other)
            if d == 1:
                return run(
                    attention_weights_and_out,
                    (shape(BF, 16, 368, 128),),
                    (place,) + args + (out_keep, out_got),
                    ATTENTION_FLOPS,
                    smem=1,
                    mirrors=(0,),
                )[1]
            return run(
                attention_weights,
                (shape(BF, 16, 400, 128),),
                args,
                ATTENTION_FLOPS,
                mirrors=(0,),
            )[1]

        pairs, attention_grad, mlp_done = total(
            mine, theirs, (attention_work, packed_grad), previous if d == 1 else None
        )
        if d == 1:
            mlp_got = mlp_done
        if d == 1:
            grad_stream, grad_low, sums[1, d] = run(
                functools.partial(norm_backward, (d, 0)),
                NORM_SHAPES + (shape(F32, 8, WIDTH),),
                pairs + (start, grad_stream, wide),
                0,
            )
    keep, give, keep_v, give_v = run(
        norm_backward_last,
        (shape(BF, half, 128), shape(BF, half, 128), shape(F32, 16, 128), shape(F32, 16, 128)),
        (place,) + pairs + (start, grad_stream, wide, sums[2, 0], sums[1, 1], sums[2, 1], low_sum),
        0,
        (pltpu.VMEM((half, WIDTH), F32), pltpu.VMEM((8, WIDTH), F32), pltpu.VMEM((16, WIDTH), F32)),
        1,
    )
    (last_rows,) = pl.pallas_call(
        final_rows,
        out_shape=[shape(BF, 16, 400, 128)],
        in_specs=[pl.BlockSpec(memory_space=pltpu.SMEM), pl.BlockSpec(memory_space=pltpu.HBM)]
        + [pl.BlockSpec(memory_space=pltpu.VMEM)] * 8,
        out_specs=[pl.BlockSpec(memory_space=pltpu.HBM)],
        scratch_shapes=[pltpu.VMEM((16, 144, 128), BF), pltpu.SemaphoreType.DMA(())],
        input_output_aliases={1: 0},
        compiler_params=pltpu.CompilerParams(vmem_limit_bytes=56 * 2**20),
    )(
        place,
        attention_grad,
        keep,
        core_swap(give),
        keep_v,
        core_swap(give_v),
        narrow_sums[0][0],
        narrow_sums[1][0],
        narrow_sums[0][1],
        narrow_sums[1][1],
    )
    last_rows, previous = lax.optimization_barrier((last_rows, previous))
    last = exchange(last_rows)
    mixed, previous, mlp_got, _ = lax.optimization_barrier((mixed, previous, mlp_got, last_rows))

    def summed(block):
        return jnp.sum(block.astype(F32), axis=0)

    mlp = [summed(previous), summed(mlp_got)]
    grad_up = jnp.stack([jnp.concatenate([m[:128], m[128:256]], axis=-1) for m in mlp])
    grad_down = jnp.stack([m[256:] for m in mlp])
    hbm, vmem = pl.BlockSpec(memory_space=pltpu.HBM), pl.BlockSpec(memory_space=pltpu.VMEM)
    smem = pl.BlockSpec(memory_space=pltpu.SMEM)
    (result,) = pl.pallas_call(
        collect,
        out_shape=[shape(F32, 3, 64, seq)],
        in_specs=[smem, hbm],
        out_specs=[vmem],
        scratch_shapes=[pltpu.VMEM((3, half, 128), BF), pltpu.SemaphoreType.DMA((3,))],
    )(place, mixed)
    grad_inputs, grad_qkv, grad_out, g1, b1, bo, g2, b2, bd, grad_qv, grad_b_up = pl.pallas_call(
        finish,
        out_shape=[shape(F32, 3, 64, seq), shape(F32, 2, 192, 128), shape(F32, 2, 64, 128)]
        + [shape(F32, 2, 64)] * 6
        + [shape(F32, 2, 128), shape(F32, 2, 256)],
        in_specs=[smem, hbm, vmem],
        out_specs=[vmem] * 11,
        scratch_shapes=[
            pltpu.VMEM((16, 256, 128), BF),
            pltpu.VMEM((16, 32, 128), BF),
            pltpu.VMEM((3, half, 128), BF),
            pltpu.SemaphoreType.DMA((5,)),
        ],
        compiler_params=pltpu.CompilerParams(vmem_limit_bytes=16 * 2**20),
    )(place, last, summed(mixed[:, :256]))
    return (
        result.transpose(0, 2, 1),
        grad_inputs.transpose(0, 2, 1),
        g1,
        b1,
        grad_qkv[:, None].transpose(0, 3, 1, 2),
        grad_qv[:, None, :],
        grad_out,
        bo,
        g2,
        b2,
        grad_up,
        grad_b_up,
        grad_down,
        bd,
    )


def solution(mesh):
    split = Mesh(mesh.devices.reshape(4, 2, 2, 4, 2), ("y", "xl", "xh", "z", "c"))
    gx = ("y", "xl")
    gy = ("xh", "z", "c")
    token = P(gx, None, gy)
    vector = P(None, gy)
    return jax.shard_map(
        shards,
        mesh=split,
        in_specs=(
            token,
            token,
            P(),
            vector,
            vector,
            P(None, gx, gy, None),
            P(None, gy, None),
            P(None, gy, gx),
            vector,
            vector,
            vector,
            P(None, gx, gy),
            vector,
            P(None, gy, gx),
            vector,
        ),
        out_specs=(
            token,
            token,
            vector,
            vector,
            P(None, gx, gy, None),
            P(None, gy, None),
            P(None, gy, gx),
            vector,
            vector,
            vector,
            P(None, gx, gy),
            vector,
            P(None, gy, gx),
            vector,
        ),
        check_vma=False,
    )
```

```python
import functools

import jax
import jax.numpy as jnp
from jax import lax
from jax.experimental import pallas as pl
from jax.experimental.pallas import tpu as pltpu
from jax.sharding import Mesh, PartitionSpec as P

EPS = 1e-06
BF = jnp.bfloat16
F32 = jnp.float32
DP = ("y", "xl", "xh")
SWAP = [(0, 1), (1, 0)]
PAIR_A = [(0, 1), (1, 0), (2, 3), (3, 2)]
PAIR_B = [(0, 3), (3, 0), (1, 2), (2, 1)]


def dot(a, b, ca, cb):
    return lax.dot_general(a, b, (((ca,), (cb,)), ((), ())), preferred_element_type=F32)


def core_swap(block):
    return lax.ppermute(block, "c", SWAP)


def ring_blocks(block):
    return [block] + [
        lax.ppermute(block, "z", [(i, (i + step) % 4) for i in range(4)]) for step in (1, 3, 2)
    ]


def total(mine, theirs, work=None, late=None):
    parts = (shape(BF, HALF, mine.shape[1] // 2),) * 2
    left, right = run(add_cores, parts, (mine, core_swap(theirs)), 0)
    if work is not None:
        left, right, given = lax.optimization_barrier((left, right, work[1]))
    got_left = lax.ppermute(left, "z", PAIR_A)
    got_right = lax.ppermute(right, "z", PAIR_B)
    done = work[0](given) if work is not None else None
    left, right = run(add_pairs, parts, (left, got_left, right, got_right), 0)
    left, right, late, done = lax.optimization_barrier((left, right, late, done))
    got_left = lax.ppermute(left, "z", PAIR_B)
    got_right = lax.ppermute(right, "z", PAIR_A)
    return (left, got_left, right, got_right), done, late


def add_cores(mine, got, left, right):
    both = (mine[...] + got[...].astype(F32)).astype(BF)
    cut = mine.shape[1] // 2
    left[...] = both[:, :cut]
    right[...] = both[:, cut:]


def add_pairs(left, got_left, right, got_right, left_out, right_out):
    left_out[...] = (left[...].astype(F32) + got_left[...].astype(F32)).astype(BF)
    right_out[...] = (right[...].astype(F32) + got_right[...].astype(F32)).astype(BF)


HALF = 112
ROWS = 2 * HALF
WIDTH = 1024


def run(
    kernel, outs, args, flops, scratch=(), smem=0, far=(), grant=16, mirrors=(), direct=False
):
    far = [f if isinstance(f, tuple) else (f, None, None) for f in far]
    size = sum(a.size * a.dtype.itemsize for a in args)
    size += sum(o.size * o.dtype.itemsize for o in outs)
    fetched = [f[0] for f in far]
    specs = [
        pl.BlockSpec(
            memory_space=pltpu.SMEM if i < smem else pltpu.HBM if i in fetched else pltpu.VMEM
        )
        for i in range(len(args))
    ]
    held = []
    for i, _, count in far:
        sizes = args[i].shape
        sizes = sizes if count is None else (sizes[0], count) + sizes[2:]
        held.append(pltpu.VMEM(sizes, args[i].dtype))
    more = [
        shape(args[m[0]].dtype, ROWS, WIDTH) if isinstance(m, tuple) else outs[m] for m in mirrors
    ]
    semaphores = [pltpu.SemaphoreType.DMA((max(len(far), 1),))]
    semaphores += [pltpu.SemaphoreType.DMA((max(2 * len(mirrors), 1),))]

    def body(*refs):
        refs = list(refs)
        n, m = len(args), len(outs)
        results, copied = refs[n : n + m], refs[n + m : n + m + len(mirrors)]
        rest = refs[n + m + len(mirrors) : -2]
        sems, out_sems = refs[-2:]
        spaces, rest = rest[len(rest) - len(far) :], rest[: len(rest) - len(far)]
        copies = []
        for k, (i, start, count) in enumerate(far):
            source = refs[i] if count is None else refs[i].at[:, start : start + count]
            copies.append(pltpu.make_async_copy(source, spaces[k], sems.at[k]))
            copies[-1].start()
        sent = {}

        def send(k):
            if isinstance(mirrors[k], tuple):
                sent[k] = [
                    pltpu.make_async_copy(
                        refs[i], copied[k].at[HALF * j : HALF * j + HALF], out_sems.at[2 * k + j]
                    )
                    for j, i in enumerate(mirrors[k])
                ]
            else:
                sent[k] = [
                    pltpu.make_async_copy(results[mirrors[k]], copied[k], out_sems.at[2 * k])
                ]
            for copy in sent[k]:
                copy.start()

        for k, mirror in enumerate(mirrors):
            if isinstance(mirror, tuple):
                send(k)
        for k, copy in enumerate(copies):
            copy.wait()
            refs[fetched[k]] = spaces[k]
        if mirrors:
            kernel(*refs[:n], *results, *rest, send=send)
        else:
            kernel(*refs[:n], *results, *rest)
        for k in range(len(mirrors)):
            if k not in sent:
                send(k)
        for group in sent.values():
            for copy in group:
                copy.wait()

    space = pltpu.HBM if direct else pltpu.VMEM
    return pl.pallas_call(
        body,
        out_shape=list(outs) + more,
        in_specs=specs,
        out_specs=[pl.BlockSpec(memory_space=space)] * len(outs)
        + [pl.BlockSpec(memory_space=pltpu.HBM)] * len(more),
        scratch_shapes=list(scratch) + held + semaphores,
        compiler_params=pltpu.CompilerParams(vmem_limit_bytes=grant * 2**20),
        cost_estimate=pl.CostEstimate(
            flops=int(flops), bytes_accessed=int(size), transcendentals=0
        ),
    )(*args)


def shape(dtype, *sizes):
    return jax.ShapeDtypeStruct(sizes, dtype)


def norm_parts(stream):
    center = stream - jnp.mean(stream, axis=-1, keepdims=True)
    factor = lax.rsqrt(jnp.mean(center * center, axis=-1, keepdims=True) + EPS)
    return center * factor, factor


def place_attention(w, w_qkv, w_out):
    for g in range(8):
        cols = slice(128 * g, 128 * g + 128)
        for i in range(2):
            w_qkv[128 * i : 128 * i + 128, cols] = w[2 * g + i, :128]
            w_qkv[256 + 64 * i : 320 + 64 * i, cols] = w[2 * g + i, 128:192]
            w_out[64 * i : 64 * i + 64, cols] = w[2 * g + i, 192:256]


def place_mlp(w, w_up, w_down):
    for g in range(8):
        rows = slice(128 * g, 128 * g + 128)
        for i in range(2):
            for j in range(2):
                at = 256 * i + 128 * j
                w_up[rows, at : at + 128] = w[2 * g + i, 128 * j : 128 * j + 128]
            w_down[256 * i : 256 * i + 256, rows] = w[2 * g + i, 256:512]


def both_rows(mine, other):
    return jnp.concatenate([mine[...], other[...]], axis=0)


def softmax(valid, query, key):
    scores = dot(query, key, 1, 1) * 64**-0.5
    at = lax.broadcasted_iota(jnp.int32, (1, ROWS), 1)
    limit = jnp.where(at < HALF, valid[4], valid[5] + HALF)
    scores = jnp.where(at < limit, scores, -1e30)
    exponent = jnp.exp(scores - jnp.max(scores, axis=-1, keepdims=True))
    return exponent / jnp.sum(exponent, axis=-1, keepdims=True)


def part_of(packed, name, i):
    start = {"q": 128 * i, "k": 128 * i + 64, "v": 256 + 64 * i}[name]
    return packed[:, start : start + 64]


def attention_forward(at, valid, mine, other, w, bias, packed_out, heads_out, out, away, w_qkv, w_out):
    place_attention(w, w_qkv, w_out)
    packed = dot(both_rows(mine, other), w_qkv[...], 1, 1) + bias[at, 0:1, :384]
    packed_out[...] = packed.astype(BF)
    heads = []
    for i in range(2):
        query, key, value = [part_of(packed, n, i).astype(BF) for n in "qkv"]
        probs = softmax(valid, query, key).astype(BF)
        heads.append(dot(probs, value, 1, 0))
    heads = jnp.concatenate(heads, axis=1).astype(BF)
    heads_out[...] = heads
    result = dot(heads, w_out[...], 1, 0)
    out[...] = result[:HALF]
    away[...] = result[HALF:].astype(BF)


def attention_backward(valid, mine, other, packed_in, w, grad_out, sums, out, away, w_qkv, w_out):
    place_attention(w, w_qkv, w_out)
    heads_grad = dot(both_rows(mine, other), w_out[...], 1, 1)
    packed = packed_in[...].astype(F32)
    parts = []
    values = []
    for i in range(2):
        query, key, value = [part_of(packed, n, i).astype(BF) for n in "qkv"]
        p = softmax(valid, query, key)
        upstream = heads_grad[:, 64 * i : 64 * i + 64].astype(BF)
        prob_grad = dot(upstream, value, 1, 1)
        values.append(dot(p.astype(BF), upstream, 0, 0))
        score_grad = (
            p * (prob_grad - jnp.sum(prob_grad * p, axis=-1, keepdims=True))
        ).astype(BF)
        parts.append(dot(score_grad, key, 1, 0) * 64**-0.5)
        parts.append(dot(score_grad, query, 0, 0) * 64**-0.5)
    grad = jnp.concatenate(parts + values, axis=1).astype(BF)
    grad_out[...] = grad
    sums[...] = jnp.sum(grad.astype(F32), axis=0, keepdims=True)
    result = dot(grad, w_qkv[...], 1, 0)
    out[...] = result[:HALF]
    away[...] = result[HALF:].astype(BF)


def attention_weights(h_mine, h_other, grad, heads, mine, other, rows_out, send):
    qkv = dot(grad[...], both_rows(h_mine, h_other), 0, 0).astype(BF)
    back = dot(heads[...], both_rows(mine, other), 0, 0).astype(BF)
    for g in range(8):
        cols = slice(128 * g, 128 * g + 128)
        for i in range(2):
            at = 2 * g + i
            rows_out[at, :128] = qkv[128 * i : 128 * i + 128, cols]
            rows_out[at, 128:192] = qkv[256 + 64 * i : 320 + 64 * i, cols]
            rows_out[at, 192:256] = back[64 * i : 64 * i + 64, cols]


def mlp_forward(at, mine, other, w, bias, act_out, slope_out, out, away, w_up, w_down):
    place_mlp(w, w_up, w_down)
    upper = dot(both_rows(mine, other), w_up[...], 1, 0) + bias[at, 1:2]
    phi = 0.5 * (1.0 + lax.erf(upper * 0.5**0.5))
    act = (upper * phi).astype(BF)
    act_out[...] = act
    slope_out[...] = phi + upper * (jnp.exp(-0.5 * upper * upper) * 0.3989422804014327)
    result = dot(act, w_down[...], 1, 0)
    out[...] = result[:HALF]
    away[...] = result[HALF:].astype(BF)


def mlp_backward(mine, other, w, slope, grad_out, sums, out, away, w_up, w_down):
    place_mlp(w, w_up, w_down)
    grad = (dot(both_rows(mine, other), w_down[...], 1, 1) * slope[...]).astype(BF)
    grad_out[...] = grad
    sums[...] = jnp.sum(grad.astype(F32), axis=0, keepdims=True)
    result = dot(grad, w_up[...], 1, 1)
    out[...] = result[:HALF]
    away[...] = result[HALF:].astype(BF)


def mlp_backward_and_out(
    mine, other, w, slope, f_mine, f_theirs, grad_out, sums, out, away, w_up, w_down
):
    mlp_backward(
        mine, other, w, slope, grad_out, sums, out.at[:, :WIDTH], away.at[:, :WIDTH], w_up, w_down
    )
    out[:, WIDTH:] = f_mine[...]
    away[:, WIDTH:] = f_theirs[...]


def attention_weights_and_out(place, h_mine, h_other, grad, heads, mine, other, keep, got, rows_out, send):
    attention_weights(h_mine, h_other, grad, heads, mine, other, rows_out, send)
    tokens = owner_rows(place[1] == 0, keep, got)
    for g in range(8):
        for i in range(2):
            rows_out[2 * g + i, 256:] = tokens[i]


def mlp_weights(h_mine, h_other, grad, act, mine, other, rows_out, send):
    up = dot(both_rows(h_mine, h_other), grad[...], 0, 0).astype(BF)
    down = dot(act[...], both_rows(mine, other), 0, 0).astype(BF)
    for g in range(8):
        cols = slice(128 * g, 128 * g + 128)
        for i in range(2):
            for j in range(2):
                at = 256 * i + 128 * j
                rows_out[2 * g + i, 128 * j : 128 * j + 128] = up[cols, at : at + 128]
            rows_out[2 * g + i, 256:512] = down[256 * i : 256 * i + 256, cols]


def pair_sum(left, got_left, right, got_right):
    return jnp.concatenate(
        [
            left[...].astype(F32) + got_left[...].astype(F32),
            right[...].astype(F32) + got_right[...].astype(F32),
        ],
        axis=1,
    )


def ring_place(ring, blocks, store):
    for step, block in zip((0, 1, 3, 2), blocks):
        place = lax.rem(ring + 4 - step, 4) * 128
        for i in range(2):
            store(pl.ds(pl.multiple_of(512 * i + place, 128), 128), block, i)


def norm_first(ring, a, b, c, d, narrow, stream_out, out, wide_out, cotangent, sums, bias_out):
    def store(columns, block, i):
        stream_out[:, columns] = block[i, :HALF].astype(F32)
        for depth in range(2):
            rows = block[i, HALF + 16 * depth : HALF + 16 * depth + 16].astype(F32)
            wide_out[depth, :, columns] = rows[:8] + rows[8:]
        upstream = block[i, HALF + 32 :]
        cotangent[:, columns] = upstream
        sums[:, columns] = jnp.sum(upstream.astype(F32), axis=0, keepdims=True)

    ring_place(ring[0], (a, b, c, d), store)
    normed, _ = norm_parts(stream_out[...])
    out[...] = (normed * wide_out[0, 0:1] + wide_out[0, 1:2]).astype(BF)
    pieces = []
    for i in range(2):
        piece = narrow[i].astype(F32)
        pieces.append(piece[:8] + piece[8:])
    blank = jnp.zeros((1, 64), F32)
    for depth in range(2):
        qv = [piece[depth : depth + 1] for piece in pieces]
        bias_out[depth, 0:1] = jnp.concatenate(
            [qv[0][:, :64], blank, qv[1][:, :64], blank, qv[0][:, 64:], qv[1][:, 64:]]
            + [jnp.zeros((1, 128), F32)],
            axis=1,
        )
        bias_out[depth, 1:2] = jnp.concatenate(
            [piece[at : at + 1] for piece in pieces for at in (2 + 2 * depth, 3 + 2 * depth)],
            axis=1,
        )


def owner_lanes(source, ring, first_core, keep, give):
    parts = []
    for i in range(2):
        at = pl.multiple_of(512 * i + 128 * ring, 128)
        parts.append(source[:, pl.ds(at, 128)].astype(F32))
    lanes = [
        jnp.concatenate([parts[0][:, s], parts[1][:, s]], axis=1)
        for s in (slice(0, 64), slice(64, 128))
    ]
    keep[...] = jnp.where(first_core, lanes[0], lanes[1]).astype(keep.dtype)
    give[...] = jnp.where(first_core, lanes[1], lanes[0]).astype(give.dtype)


def owner_rows(first_core, keep, got):
    keep, got = keep[...].astype(F32), got[...].astype(F32)
    early, late = jnp.where(first_core, keep, got), jnp.where(first_core, got, keep)
    return [
        jnp.concatenate([early[:, s], late[:, s]], axis=1).astype(BF)
        for s in (slice(0, 64), slice(64, 128))
    ]


def owner_tokens(block, live):
    block = block.astype(F32)
    tokens = jnp.concatenate([block[:, :64], block[:, 64:]], axis=0)
    return jnp.where(live, tokens.T[:, :197], 0.0)


def norm_last(place, part, got, stream, wide, keep, give, new):
    new[...] = stream[...] + (part[...].astype(F32) + got[...].astype(F32) + wide[1, 5:6])
    owner_lanes(new, place[0], place[1] == 0, keep, give)


def prepare(
    counts, inputs, cotangent, g1, b1, bo, g2, b2, bd, qv, up, w_qkv, w_out, out, turned, held, block, sems
):
    group = lax.axis_index(("y", "xl"))
    first = jnp.int32(0)
    for g in range(8):
        first = first + jnp.where(g < group, counts[g], 0)
    wide = [jnp.concatenate([v[0:1], v[1:2]], axis=1) for v in (g1, b1, bo, g2, b2, bd)]
    wide = jnp.concatenate(wide + [jnp.zeros((2, 128), F32)], axis=0)
    narrow = [qv[0], qv[1], up[0:1, :128], up[0:1, 128:], up[1:2, :128], up[1:2, 128:]]
    narrow = jnp.concatenate(narrow + [jnp.zeros((2, 128), F32)], axis=0)
    rows = []
    for v in (wide, narrow):
        high = v.astype(BF).astype(F32)
        rows += [high, v - high]
    block[:32] = jnp.concatenate(rows, axis=0).astype(BF)
    block[32:224] = w_qkv[0]
    block[224:288] = w_out[0]
    copies = [pltpu.make_async_copy(block, out.at[w, ROWS:512], sems.at[16 + w]) for w in range(16)]
    for copy in copies:
        copy.start()
    seq = inputs.shape[2]
    turned[...] = jnp.zeros(turned.shape, F32)
    for s in range(3):
        turned[:64, :seq] = inputs[s].astype(F32)
        turned[64:, :seq] = cotangent[s].astype(F32)
        held[s] = turned[...].T[:ROWS].astype(BF)
    for w in range(16):
        slot = jnp.clip(w - first, 0, 2)
        copies.append(pltpu.make_async_copy(held.at[slot], out.at[w, 0:ROWS], sems.at[w]))
        copies[-1].start()
    for copy in copies:
        copy.wait()


def prepare_next(w_qkv, w_out, w_up, w_down, out):
    for w in range(16):
        out[w, :128] = w_up[0, :, :128]
        out[w, 128:256] = w_up[0, :, 128:]
        out[w, 256:512] = w_down[0]
        out[w, 512:704] = w_qkv[1]
        out[w, 704:768] = w_out[1]


def prepare_mlp(w_up, w_down, out):
    for w in range(out.shape[0]):
        out[w, :128] = w_up[1, :, :128]
        out[w, 128:256] = w_up[1, :, 128:]
        out[w, 256:] = w_down[1]


def norm_forward(at, left, got_left, right, got_right, stream, wide, stream_out, out):
    shift, gain, bias = [wide[d, i : i + 1] for d, i in at]
    new = stream[...] + (pair_sum(left, got_left, right, got_right) + shift)
    stream_out[...] = new
    normed, _ = norm_parts(new)
    out[...] = (normed * gain + bias).astype(BF)


def norm_backward(at, left, got_left, right, got_right, stream, upstream, wide, grad_out, low_out, sums):
    grad = pair_sum(left, got_left, right, got_right)
    norm_backward_of(grad, at, stream, upstream, wide, grad_out, low_out, sums)


def norm_backward_single(at, part, got, stream, upstream, wide, grad_out, low_out, sums):
    grad = part[...].astype(F32) + got[...].astype(F32)
    norm_backward_of(grad, at, stream, upstream, wide, grad_out, low_out, sums)


def norm_backward_of(grad, at, stream, upstream, wide, grad_out, low_out, sums):
    normed, factor = norm_parts(stream[...])
    scaled = grad * wide[at[0], at[1] : at[1] + 1]
    first = jnp.mean(scaled, axis=-1, keepdims=True)
    second = jnp.mean(scaled * normed, axis=-1, keepdims=True)
    new = upstream[...].astype(F32) + factor * (scaled - first - normed * second)
    grad_out[...] = new
    low = new.astype(BF)
    low_out[...] = low.astype(low_out.dtype)
    sums[0:1] = jnp.sum(grad * normed, axis=0, keepdims=True)
    sums[1:2] = jnp.sum(grad, axis=0, keepdims=True)
    sums[2:3] = jnp.sum(low.astype(F32), axis=0, keepdims=True)
    sums[3:8] = jnp.zeros((5, WIDTH), F32)


def norm_backward_last(
    place, left, got_left, right, got_right, stream, upstream, wide, s20, s11, s21, low_sum,
    keep, give, keep_v, give_v, new, sums, table,
):
    norm_backward((0, 0), left, got_left, right, got_right, stream, upstream, wide, new, new, sums)
    owner_lanes(new, place[0], place[1] == 0, keep, give)
    pieces = [sums[0:2], s20[2:3], s20[0:2], s11[2:3], s11[0:2], s21[2:3], s21[0:2], low_sum[...]]
    table[...] = jnp.concatenate(pieces + [jnp.zeros((4, WIDTH), F32)], axis=0)
    owner_lanes(table, place[0], place[1] == 0, keep_v, give_v)


def final_rows(place, rows_in, keep, got, keep_v, got_v, p0, p1, u0, u1, out, held, sem):
    wide = keep_v[...] + got_v[...]
    high = wide.astype(BF).astype(F32)
    low = wide - high
    tokens = owner_rows(place[1] == 0, keep, got)
    for i in range(2):
        part = slice(64 * i, 64 * i + 64)
        narrow = [
            jnp.concatenate(
                [p[:, 128 * i : 128 * i + 64], p[:, 256 + 64 * i : 320 + 64 * i]], axis=1
            )
            for p in (p0, p1)
        ]
        for u in (u0, u1):
            narrow += [u[:, 256 * i : 256 * i + 128], u[:, 256 * i + 128 : 256 * i + 256]]
        narrow = jnp.concatenate(narrow + [jnp.zeros((2, 128), F32)], axis=0)
        narrow_high = narrow.astype(BF).astype(F32)
        rows = jnp.concatenate(
            [jnp.concatenate([high[:, part], low[:, part]], axis=1), narrow_high, narrow - narrow_high],
            axis=0,
        ).astype(BF)
        for g in range(8):
            held[2 * g + i, :HALF] = tokens[i]
            held[2 * g + i, HALF:] = rows
    copy = pltpu.make_async_copy(held, out.at[:, 256:400], sem)
    copy.start()
    copy.wait()


def collect(meta, received, out, held, sems):
    copies = []
    for s in range(3):
        at = jnp.minimum(meta[2] + s, 15)
        copies.append(
            pltpu.make_async_copy(received.at[at, 256:368], held.at[s], sems.at[s])
        )
        copies[-1].start()
    for s in range(3):
        copies[s].wait()
        out[s] = owner_tokens(held[s], s < meta[3])


def finish(meta, received, sum_1, out, qkv, w_out, g1, b1, bo, g2, b2, bd, qv, up, weights, vectors, held, sems):
    copies = [
        pltpu.make_async_copy(received.at[:, 0:256], weights, sems.at[3]),
        pltpu.make_async_copy(received.at[:, 368:400], vectors, sems.at[4]),
    ]
    for s in range(3):
        at = jnp.minimum(meta[2] + s, 15)
        copies.append(
            pltpu.make_async_copy(received.at[at, 256:368], held.at[s], sems.at[s])
        )
    for copy in copies:
        copy.start()
    for copy in copies:
        copy.wait()
    for s in range(3):
        out[s] = owner_tokens(held[s], s < meta[3])
    total_v = jnp.sum(vectors[...].astype(F32), axis=0)
    wide = total_v[:16, :64] + total_v[:16, 64:]
    for v, ref in enumerate((g1, b1, bo, g2, b2, bd)):
        ref[...] = jnp.concatenate([wide[v : v + 1], wide[v + 6 : v + 7]], axis=0)
    narrow = total_v[16:24] + total_v[24:32]
    qv[...] = narrow[0:2]
    for d in range(2):
        up[d : d + 1] = jnp.concatenate([narrow[2 + 2 * d : 3 + 2 * d], narrow[3 + 2 * d : 4 + 2 * d]], axis=1)
    for d in range(2):
        block = jnp.sum(weights[...].astype(F32), axis=0) if d == 0 else sum_1[...]
        qkv[d] = block[:192]
        w_out[d] = block[192:256]


ATTENTION_SCRATCH = (pltpu.VMEM((384, WIDTH), BF), pltpu.VMEM((128, WIDTH), BF))
MLP_SCRATCH = (pltpu.VMEM((WIDTH, 512), BF), pltpu.VMEM((512, WIDTH), BF))
SUM_SHAPES = (shape(F32, HALF, WIDTH), shape(BF, HALF, WIDTH))
NORM_SHAPES = (shape(F32, HALF, WIDTH), shape(BF, HALF, WIDTH))
ATTENTION_FLOPS = 2 * ROWS * WIDTH * 512
MLP_FLOPS = 2 * ROWS * WIDTH * 1024


def exchange(chunks):
    return lax.all_to_all(chunks, DP, 0, 0)


def shards(
    inputs,
    cotangent,
    group_images,
    ln1_gain,
    ln1_bias,
    w_qkv,
    b_qv,
    w_out,
    b_out,
    ln2_gain,
    ln2_bias,
    w_up,
    b_up,
    w_down,
    b_down,
):
    seq = inputs.shape[1]
    half, rows = HALF, ROWS
    core = lax.axis_index("c")
    ring = lax.axis_index("z")
    group = lax.axis_index(("y", "xl"))
    worker = lax.axis_index(DP)
    first_core = core == 0

    earlier = jnp.arange(8)[:, None] > jnp.arange(8)[None, :]
    offsets = jnp.sum(jnp.where(earlier, group_images[None, :], 0), axis=1)
    my_offset = jnp.sum(jnp.where(jnp.arange(8) < group, group_images, 0))
    my_live = jnp.sum(jnp.where(jnp.arange(8) == group, group_images, 0))
    source = jnp.sum((offsets <= worker).astype(jnp.int32)) - 1
    mine_valid = jnp.where(first_core, half, seq - half)
    place = jnp.stack([ring, core, my_offset, my_live, mine_valid, seq - mine_valid])
    place = place.astype(jnp.int32)

    w_qkv = w_qkv.transpose(0, 2, 3, 1).reshape(2, 192, 128)
    (chunks,) = run(
        prepare,
        (shape(BF, 16, 512, 128),),
        (group_images, inputs.transpose(0, 2, 1), cotangent.transpose(0, 2, 1))
        + (ln1_gain, ln1_bias, b_out, ln2_gain, ln2_bias, b_down, b_qv, b_up, w_qkv, w_out),
        0,
        (
            pltpu.VMEM((128, 256), F32),
            pltpu.VMEM((3, rows, 128), BF),
            pltpu.VMEM((288, 128), BF),
            pltpu.SemaphoreType.DMA((32,)),
        ),
        1,
        range(1, 13),
        56,
        (),
        True,
    )
    arrived = exchange(chunks)
    (next_rows,) = run(
        prepare_next, (shape(BF, 16, 768, 128),), (w_qkv, w_out, w_up, w_down), 0
    )
    (mlp_rows_1,) = run(prepare_mlp, (shape(BF, 16, 512, 128),), (w_up, w_down), 0)
    next_rows, mlp_rows_1, arrived, place = lax.optimization_barrier(
        (next_rows, mlp_rows_1, arrived, place)
    )

    picked = lax.dynamic_slice(arrived, (2 * source, 0, 0), (2, rows, 128))
    vectors_here = arrived[:2, rows:256]
    low_part, high_part = picked[:, :half], picked[:, half:rows]
    tail = vectors_here[:, :16]
    keep = jnp.concatenate([jnp.where(first_core, low_part, high_part), tail], axis=1)
    give = jnp.concatenate([jnp.where(first_core, high_part, low_part), tail], axis=1)
    got = core_swap(give)
    part_0 = jnp.where(first_core, keep, got)
    part_1 = jnp.where(first_core, got, keep)
    left = jnp.concatenate([part_0[..., :64], part_1[..., :64]], axis=-1)
    right = jnp.concatenate([part_0[..., 64:], part_1[..., 64:]], axis=-1)
    blocks = ring_blocks(jnp.concatenate([left, right[:, half:], right[:, :half]], axis=1))
    following = exchange(next_rows)
    mlp_w = [following, None]
    attention_w = [arrived, following]
    attention_at = [256, 512]
    stream, h1, wide, cotangent_low, low_sum, bias = run(
        norm_first,
        NORM_SHAPES
        + (shape(F32, 2, 8, WIDTH), shape(BF, half, WIDTH), shape(F32, 1, WIDTH))
        + (shape(F32, 2, 2, 512),),
        [place] + blocks + [vectors_here[:, 16:]],
        0,
        (),
        1,
    )
    kept = []
    for d in range(2):
        h1_other = core_swap(h1)
        packed, heads, mine, theirs = run(
            functools.partial(attention_forward, d),
            (shape(BF, ROWS, 384), shape(BF, ROWS, 128)) + SUM_SHAPES,
            (place, h1, h1_other, attention_w[d], bias),
            ATTENTION_FLOPS,
            ATTENTION_SCRATCH,
            1,
            ((3, attention_at[d], 256),),
        )
        pairs, _, _ = total(mine, theirs)
        middle, h2 = run(
            functools.partial(norm_forward, ((d, 2), (d, 3), (d, 4))),
            NORM_SHAPES,
            pairs + (stream, wide),
            0,
        )
        if d == 0:
            mlp_rows_1, _, h2 = lax.optimization_barrier((mlp_rows_1, following, h2))
            mlp_w[1] = exchange(mlp_rows_1)
        h2_other = core_swap(h2)
        act, slope, mine, theirs = run(
            functools.partial(mlp_forward, d),
            (shape(BF, ROWS, 512), shape(F32, ROWS, 512)) + SUM_SHAPES,
            (h2, h2_other, mlp_w[d], bias),
            MLP_FLOPS,
            MLP_SCRATCH,
            0,
            ((2, 0, 512),),
        )
        kept.append((stream, h1, h1_other, packed, heads, middle, h2, h2_other, act, slope))
        if d == 0:
            pairs, _, _ = total(mine, theirs)
            stream, h1 = run(
                functools.partial(norm_forward, ((0, 5), (1, 0), (1, 1))),
                NORM_SHAPES,
                pairs + (middle, wide),
                0,
            )
    grad_low = cotangent_low
    low_other = core_swap(grad_low)
    grad_stream = cotangent_low
    previous = mlp_got = None
    sums, narrow_sums = {}, {}
    for d in (1, 0):
        start, h1, h1_other, packed, heads, middle, h2, h2_other, act, slope = kept[d]
        if d == 0:
            low_other = core_swap(grad_low)
            attention_grad, _ = lax.optimization_barrier((attention_grad, mlp_got))
            mixed = exchange(attention_grad)
        extra = (mine, theirs) if d == 1 else ()
        both = WIDTH * 2 if d == 1 else WIDTH
        upper_grad, up_sum, mine, theirs = run(
            mlp_backward_and_out if d == 1 else mlp_backward,
            (shape(BF, ROWS, 512), shape(F32, 1, 512))
            + (shape(F32, HALF, both), shape(BF, HALF, both)),
            (grad_low, low_other, mlp_w[d], slope) + extra,
            MLP_FLOPS,
            MLP_SCRATCH,
            0,
            ((2, 0, 512),),
        )

        def mlp_work(upper_grad):
            args = (h2, h2_other, upper_grad, act, grad_low, low_other)
            return run(
                mlp_weights,
                (shape(BF, 16, 512, 128),),
                args,
                MLP_FLOPS,
                mirrors=(0,),
            )[1]

        pairs, mlp_grad, _ = total(mine, theirs, (mlp_work, upper_grad))
        if d == 0:
            mlp_grad, mixed = lax.optimization_barrier((mlp_grad, mixed))
        previous = exchange(mlp_grad)
        step = norm_backward
        if d == 1:
            pairs = lax.optimization_barrier(pairs)
            keep, give = run(
                norm_last,
                (shape(BF, half, 128), shape(BF, half, 128)),
                (place,) + pairs[2:] + (middle, wide),
                0,
                (pltpu.VMEM((half, WIDTH), F32),),
                1,
            )
            keep, give, pairs = lax.optimization_barrier((keep, give, pairs))
            out_keep, out_got = keep, core_swap(give)
            step, pairs = norm_backward_single, pairs[:2]
        grad_stream, grad_low, sums[2, d] = run(
            functools.partial(step, (d, 3)),
            NORM_SHAPES + (shape(F32, 8, WIDTH),),
            pairs + (middle, grad_stream, wide),
            0,
        )
        low_other = core_swap(grad_low)
        packed_grad, packed_sum, mine, theirs = run(
            attention_backward,
            (shape(BF, ROWS, 384), shape(F32, 1, 384)) + SUM_SHAPES,
            (place, grad_low, low_other, packed, attention_w[d]),
            ATTENTION_FLOPS,
            ATTENTION_SCRATCH,
            1,
            ((4, attention_at[d], 256),),
        )
        narrow_sums[d] = (packed_sum, up_sum)

        def attention_work(packed_grad):
            args = (h1, h1_other, packed_grad, heads, grad_low, low_other)
            if d == 1:
                return run(
                    attention_weights_and_out,
                    (shape(BF, 16, 368, 128),),
                    (place,) + args + (out_keep, out_got),
                    ATTENTION_FLOPS,
                    smem=1,
                    mirrors=(0,),
                )[1]
            return run(
                attention_weights,
                (shape(BF, 16, 400, 128),),
                args,
                ATTENTION_FLOPS,
                mirrors=(0,),
            )[1]

        pairs, attention_grad, mlp_done = total(
            mine, theirs, (attention_work, packed_grad), previous if d == 1 else None
        )
        if d == 1:
            mlp_got = mlp_done
        if d == 1:
            grad_stream, grad_low, sums[1, d] = run(
                functools.partial(norm_backward, (d, 0)),
                NORM_SHAPES + (shape(F32, 8, WIDTH),),
                pairs + (start, grad_stream, wide),
                0,
            )
    keep, give, keep_v, give_v = run(
        norm_backward_last,
        (shape(BF, half, 128), shape(BF, half, 128), shape(F32, 16, 128), shape(F32, 16, 128)),
        (place,) + pairs + (start, grad_stream, wide, sums[2, 0], sums[1, 1], sums[2, 1], low_sum),
        0,
        (pltpu.VMEM((half, WIDTH), F32), pltpu.VMEM((8, WIDTH), F32), pltpu.VMEM((16, WIDTH), F32)),
        1,
    )
    (last_rows,) = pl.pallas_call(
        final_rows,
        out_shape=[shape(BF, 16, 400, 128)],
        in_specs=[pl.BlockSpec(memory_space=pltpu.SMEM), pl.BlockSpec(memory_space=pltpu.HBM)]
        + [pl.BlockSpec(memory_space=pltpu.VMEM)] * 8,
        out_specs=[pl.BlockSpec(memory_space=pltpu.HBM)],
        scratch_shapes=[pltpu.VMEM((16, 144, 128), BF), pltpu.SemaphoreType.DMA(())],
        input_output_aliases={1: 0},
        compiler_params=pltpu.CompilerParams(vmem_limit_bytes=16 * 2**20),
    )(
        place,
        attention_grad,
        keep,
        core_swap(give),
        keep_v,
        core_swap(give_v),
        narrow_sums[0][0],
        narrow_sums[1][0],
        narrow_sums[0][1],
        narrow_sums[1][1],
    )
    last_rows, previous = lax.optimization_barrier((last_rows, previous))
    last = exchange(last_rows)
    mixed, previous, mlp_got, _ = lax.optimization_barrier((mixed, previous, mlp_got, last_rows))

    def summed(block):
        return jnp.sum(block.astype(F32), axis=0)

    mlp = [summed(previous), summed(mlp_got)]
    grad_up = jnp.stack([jnp.concatenate([m[:128], m[128:256]], axis=-1) for m in mlp])
    grad_down = jnp.stack([m[256:] for m in mlp])
    hbm, vmem = pl.BlockSpec(memory_space=pltpu.HBM), pl.BlockSpec(memory_space=pltpu.VMEM)
    smem = pl.BlockSpec(memory_space=pltpu.SMEM)
    (result,) = pl.pallas_call(
        collect,
        out_shape=[shape(F32, 3, 64, seq)],
        in_specs=[smem, hbm],
        out_specs=[vmem],
        scratch_shapes=[pltpu.VMEM((3, half, 128), BF), pltpu.SemaphoreType.DMA((3,))],
    )(place, mixed)
    grad_inputs, grad_qkv, grad_out, g1, b1, bo, g2, b2, bd, grad_qv, grad_b_up = pl.pallas_call(
        finish,
        out_shape=[shape(F32, 3, 64, seq), shape(F32, 2, 192, 128), shape(F32, 2, 64, 128)]
        + [shape(F32, 2, 64)] * 6
        + [shape(F32, 2, 128), shape(F32, 2, 256)],
        in_specs=[smem, hbm, vmem],
        out_specs=[vmem] * 11,
        scratch_shapes=[
            pltpu.VMEM((16, 256, 128), BF),
            pltpu.VMEM((16, 32, 128), BF),
            pltpu.VMEM((3, half, 128), BF),
            pltpu.SemaphoreType.DMA((5,)),
        ],
        compiler_params=pltpu.CompilerParams(vmem_limit_bytes=16 * 2**20),
    )(place, last, summed(mixed[:, :256]))
    return (
        result.transpose(0, 2, 1),
        grad_inputs.transpose(0, 2, 1),
        g1,
        b1,
        grad_qkv[:, None].transpose(0, 3, 1, 2),
        grad_qv[:, None, :],
        grad_out,
        bo,
        g2,
        b2,
        grad_up,
        grad_b_up,
        grad_down,
        bd,
    )


def solution(mesh):
    split = Mesh(mesh.devices.reshape(4, 2, 2, 4, 2), ("y", "xl", "xh", "z", "c"))
    gx = ("y", "xl")
    gy = ("xh", "z", "c")
    token = P(gx, None, gy)
    vector = P(None, gy)
    return jax.shard_map(
        shards,
        mesh=split,
        in_specs=(
            token,
            token,
            P(),
            vector,
            vector,
            P(None, gx, gy, None),
            P(None, gy, None),
            P(None, gy, gx),
            vector,
            vector,
            vector,
            P(None, gx, gy),
            vector,
            P(None, gy, gx),
            vector,
        ),
        out_specs=(
            token,
            token,
            vector,
            vector,
            P(None, gx, gy, None),
            P(None, gy, None),
            P(None, gy, gx),
            vector,
            vector,
            vector,
            P(None, gx, gy),
            vector,
            P(None, gy, gx),
            vector,
        ),
        check_vma=False,
    )
```
